128 devices in a mesh: fsdp: 128 (over x, z, y, core).
Axes of the slice: x: 4, y: 4, z: 4, core: 2. Of those that a mesh axis runs over, the one named last changes fastest.
Arguments:
- tokens: bfloat16 [16384, 1536], P('fsdp'), may hold values from -6 to 6
- expert_ids: int32 [16384, 6], P('fsdp'), may hold values from 0 to 7, all different within a row; in each aligned block of 128 rows (0 to 127, 128 to 255, ...) at most 128 rows name the same one
- attn_gain: bfloat16 [1536], P('fsdp'), may hold values from 0.099609375 to 1.8984375
- w_qkv: bfloat16 [1536, 2560], P('fsdp'), may hold values from -0.15625 to 0.15625
- w_out: bfloat16 [1536, 1536], P('fsdp'), may hold values from -0.625 to 0.625
- moe_gain: bfloat16 [1536], P('fsdp'), may hold values from 0.099609375 to 1.8984375
- w_router: bfloat16 [1536, 8], P('fsdp'), may hold values from -0.078125 to 0.078125
- w_shared_in: bfloat16 [1536, 2048], P('fsdp'), may hold values from -0.15625 to 0.15625
- w_shared_out: bfloat16 [1536, 1024], P('fsdp'), may hold values from -0.1875 to 0.1875
- w_expert_in: bfloat16 [12288, 1024], P('fsdp'), may hold values from -0.15625 to 0.15625
- w_expert_out: bfloat16 [12288, 512], P('fsdp'), may hold values from -0.25 to 0.25
- out_grad: bfloat16 [16384, 1536], P('fsdp'), may hold values from -6 to 6
Outputs:
- block_out: bfloat16 [16384, 1536], P('fsdp')
- tokens_grad: float32 [16384, 1536], P('fsdp')
- attn_gain_grad: float32 [1536], P('fsdp')
- w_qkv_grad: float32 [1536, 2560], P('fsdp')
- w_out_grad: float32 [1536, 1536], P('fsdp')
- moe_gain_grad: float32 [1536], P('fsdp')
- w_router_grad: float32 [1536, 8], P('fsdp')
- w_shared_in_grad: float32 [1536, 2048], P('fsdp')
- w_shared_out_grad: float32 [1536, 1024], P('fsdp')
- w_expert_in_grad: float32 [12288, 1024], P('fsdp')
- w_expert_out_grad: float32 [12288, 512], P('fsdp')
The draws below stay inside these ranges and needn't reach their ends.
Inputs may be any that keep to these rules, and one draw needn't show every extreme that they name: `expert_ids`: each row names 6 different experts. Among the rows of one device no expert is named by more than 128 rows, and this bound is reached.
All inputs are finite; a program needn't handle non-finite values.
Results may differ from the reference program's by a relative error of at most 0.02.
Values may be sent and summed in bfloat16 or wider, within the bound.
A program may use at most 384 MiB of HBM per device.

```python
import math
import jax
import jax.numpy as jnp
import numpy as np
from jax import lax

D = 1536
HQ = 12
KV = 4
HD = 128
H = 512
SH = 1024
EXPERTS = 8
TOP = 6
SEQ = 128
TOKENS = 16384
QKV = 2560
AO = 1536
CAP = 128
N_FSDP = 128


def block_scale(own_key, extent, cuts, low, top_value):
    factor_of, own = 1.0, jax.random.fold_in(own_key, 6)
    for dim, shards_of in cuts:
        draws = jnp.exp(jax.random.uniform(jax.random.fold_in(own, dim), (shards_of,), jnp.float32, low / len(cuts), top_value / len(cuts)))
        factor_of = factor_of * jnp.repeat(draws, extent[dim] // shards_of).reshape([-1 if axis == dim else 1 for axis in range(len(extent))])
    return factor_of


def routed_block(stream_key, own, number, rows, number_of, top, limit, lean):
    order = jax.random.permutation(stream_key, number_of)
    heavy_load, usual = shares(number_of, rows * top, limit, lean, True), shares(number_of, rows * top, limit, lean, False)
    places = jnp.arange(number_of)

    def named(tallies, turn):
        used = int((tallies > 0).sum())
        fixed = max(1, used // 4)
        passed = fixed + (places - fixed + turn * (used - fixed)) % max(1, number_of - fixed)
        return jnp.zeros((number_of,), jnp.int32).at[order[jnp.where(places < fixed, places, passed)]].set(jnp.asarray(tallies, jnp.int32))

    tallies = jnp.where(number % 4 == 0, named(heavy_load, number // 4), named(usual, number - number // 4 - 1))
    mixed = jax.random.permutation(jax.random.fold_in(own, 3), number_of)
    source_of, receiver = mixed[0:number_of // 2 * 2:2], mixed[1:number_of // 2 * 2:2]
    slack = jnp.minimum(tallies[source_of] - 1, limit - tallies[receiver]) // 2
    slack = jnp.where((source_of == order[0]) | (receiver == order[0]) | (tallies[receiver] == 0), 0, jnp.maximum(slack, 0))
    passed = jax.random.randint(jax.random.fold_in(own, 4), (number_of // 2,), 0, 1 << 20) % (slack + 1)
    tallies = tallies.at[source_of].add(-passed).at[receiver].add(passed)
    items = jnp.searchsorted(jnp.cumsum(tallies), jnp.arange(rows * top), side="right").astype(jnp.int32)
    listing = items.reshape(top, rows).T
    listing = listing[jax.random.permutation(jax.random.fold_in(own, 1), rows)]
    turn = jax.random.randint(jax.random.fold_in(own, 2), (rows, 1), 0, top)
    return jnp.take_along_axis(listing, (jnp.arange(top)[None, :] + turn) % top, axis=1)


def shares(count, total, limit, lean, full):
    portions = [(1 << 20) // math.isqrt(standing ** lean) + 1 for standing in range(1, count + 1)]
    largest = limit if full else min(limit, max(-(-total // count), total * portions[0] // sum(portions)))
    least = 1 if total - largest >= count - 1 else 0
    given, rest = [largest] + [least] * (count - 1), total - largest - least * (count - 1)
    while rest > 0:
        free = [i for i in range(1, count) if given[i] < largest] or [i for i in range(1, count) if given[i] < limit]
        whole, remaining = sum([portions[i] for i in free]), rest
        for i in free:
            extra = min(limit - given[i], max(1, remaining * portions[i] // whole), rest)
            given[i] = given[i] + extra
            rest = rest - extra
    return np.array(given)


def bell_draw(own_key, dims, spread, most, shards=(), held_as=jnp.bfloat16):
    drawn = spread * jax.random.normal(own_key, dims, jnp.float32)
    if shards:
        drawn = drawn * block_scale(own_key, dims, shards, -0.22, 0.18)
    return jnp.clip(drawn, -most, most).astype(held_as)


def setup_inputs(seed: int = 0) -> dict:
    key_of = jax.random.split(jax.random.key(seed), 13)
    tokens = bell_draw(key_of[0], (TOKENS, D), 1.0, 6.0, ((0, 128),))
    expert_ids_keys = jax.random.split(jax.random.fold_in(key_of[1], 1), TOKENS // SEQ)
    expert_ids_turns = jax.random.permutation(jax.random.fold_in(key_of[1], 3), TOKENS // SEQ)
    expert_ids = jax.vmap(lambda own, number: routed_block(jax.random.fold_in(key_of[1], 2), own, number, SEQ, EXPERTS, TOP, CAP, 1))(expert_ids_keys, expert_ids_turns).reshape((TOKENS, TOP))
    attn_gain = jnp.clip(1.0 + 0.18 * jax.random.normal(key_of[2], (D,), jnp.float32), 0.099609375, 1.8984375).astype(jnp.bfloat16)
    w_qkv = bell_draw(key_of[3], (D, QKV), D ** -0.5, 0.15625, ((0, 128),))
    w_out = bell_draw(key_of[4], (D, AO), (AO // 16) ** -0.5, 0.625, ((0, 128),))
    moe_gain = jnp.clip(1.0 + 0.18 * jax.random.normal(key_of[5], (D,), jnp.float32), 0.099609375, 1.8984375).astype(jnp.bfloat16)
    w_router = bell_draw(key_of[6], (D, EXPERTS), (4 * D) ** -0.5, 0.078125, ((0, 128),))
    w_shared_in = bell_draw(key_of[7], (D, 2 * SH), D ** -0.5, 0.15625, ((0, 128),))
    w_shared_out = bell_draw(key_of[8], (D, SH), SH ** -0.5, 0.1875, ((0, 128),))
    w_expert_in = bell_draw(key_of[9], (EXPERTS * D, 2 * H), D ** -0.5, 0.15625, ((0, 128),))
    w_expert_out = bell_draw(key_of[10], (EXPERTS * D, H), H ** -0.5, 0.25, ((0, 128),))
    out_grad = bell_draw(key_of[11], (TOKENS, D), 1.0, 6.0, ((0, 128),))
    return {"tokens": tokens, "expert_ids": expert_ids, "attn_gain": attn_gain, "w_qkv": w_qkv, "w_out": w_out, "moe_gain": moe_gain, "w_router": w_router, "w_shared_in": w_shared_in, "w_shared_out": w_shared_out, "w_expert_in": w_expert_in, "w_expert_out": w_expert_out, "out_grad": out_grad}


@jax.custom_vjp
def low(v):
    return lax.optimization_barrier(v.astype(jnp.bfloat16)).astype(jnp.float32)

@jax.custom_vjp
def low_back(v):
    return v

def low_keep(v):
    return (low(v), None)

def low_pass(kept, grad):
    return (grad,)

def back_keep(v):
    return (v, None)

def back_low(kept, grad):
    return (low(grad),)
low.defvjp(low_keep, low_pass)
low_back.defvjp(back_keep, back_low)
highest = lax.Precision.HIGHEST
epsilon = 1e-05

def rms_scale(values, gain):
    factor = lax.rsqrt(lax.optimization_barrier(jnp.mean(values * values, axis=-1, keepdims=True)) + epsilon)
    return values * factor * gain

def swish_product(joined, width):
    return jax.nn.silu(joined[..., :width]) * joined[..., width:]

def attention(normed, w_qkv, w_out):
    length = normed.shape[0]
    group_size = HQ // KV
    qkv_rows = low(low_back(jnp.dot(low(normed), w_qkv, precision=highest)))
    query_rows = qkv_rows[:, :HQ * HD].reshape(length, KV, group_size, HD)
    key_rows = qkv_rows[:, HQ * HD:(HQ + KV) * HD].reshape(length, KV, HD)
    value_rows = qkv_rows[:, (HQ + KV) * HD:].reshape(length, KV, HD)
    scores = jnp.einsum('qkgd,skd->kgqs', query_rows, key_rows, precision=highest) * HD ** (-0.5)
    scores = low_back(scores)
    causal = jnp.arange(length)[:, None] >= jnp.arange(length)[None, :]
    scores = jnp.where(causal, scores, -1e+30)
    probs = low(jax.nn.softmax(scores, axis=-1))
    head_mix = jnp.einsum('kgqs,skd->qkgd', probs, value_rows, precision=highest).reshape(length, HQ * HD)
    head_mix = low(low_back(head_mix))
    return low_back(jnp.dot(head_mix, w_out.T, precision=highest))

def slot_numbers(expert_ids):
    flat_ids = expert_ids.reshape(-1).astype(jnp.int32)
    one_hot = (flat_ids[:, None] == jnp.arange(EXPERTS, dtype=jnp.int32)[None, :]).astype(jnp.int32)
    before = jnp.cumsum(one_hot, axis=0) - one_hot
    return (flat_ids, lax.optimization_barrier(jnp.sum(before * one_hot, axis=1)).astype(jnp.int32))

def mixture(moe_in, expert_ids, w_router, w_shared_in, w_shared_out, w_expert_in, w_expert_out):
    length = moe_in.shape[0]
    logits = low_back(jnp.dot(moe_in, w_router, precision=highest))
    router_probs = jax.nn.softmax(logits, axis=-1)
    gate_weights = jnp.take_along_axis(router_probs, expert_ids.astype(jnp.int32), axis=1)
    flat_ids, slot_index = slot_numbers(expert_ids)
    owner_row = jnp.arange(length * TOP, dtype=jnp.int32) // TOP
    dispatched = jnp.zeros((EXPERTS, CAP, D), jnp.float32).at[flat_ids, slot_index].set(moe_in[owner_row])
    gate_up = jnp.einsum('ecd,edh->ech', dispatched, w_expert_in.reshape(EXPERTS, D, 2 * H), precision=highest)
    gate_up = low(low_back(gate_up))
    expert_act = low(swish_product(gate_up, H))
    expert_out = jnp.einsum('ech,edh->ecd', expert_act, w_expert_out.reshape(EXPERTS, D, H), precision=highest)
    expert_out = low(low_back(expert_out))
    picked = expert_out[flat_ids, slot_index].reshape(length, TOP, D)
    routed = lax.optimization_barrier(jnp.sum(gate_weights[:, :, None] * picked, axis=1))
    shared_gate_up = low(low_back(jnp.dot(moe_in, w_shared_in, precision=highest)))
    shared_act = low(swish_product(shared_gate_up, SH))
    return routed + jnp.dot(shared_act, w_shared_out.T, precision=highest)

def one_sequence(weights, seq_tokens, seq_ids):
    attn_gain, w_qkv, w_out, moe_gain, w_router, w_shared_in, w_shared_out, w_expert_in, w_expert_out = weights
    hidden = seq_tokens + attention(rms_scale(seq_tokens, attn_gain), w_qkv, w_out)
    moe_in = low(rms_scale(hidden, moe_gain))
    return hidden + mixture(moe_in, seq_ids, w_router, w_shared_in, w_shared_out, w_expert_in, w_expert_out)

def block_layer(tokens, weights, expert_ids):
    group_count = math.gcd(N_FSDP, max(1, 4096 // SEQ))
    step_count = N_FSDP // group_count
    blocks = tokens.reshape(step_count, group_count, SEQ, D)
    id_blocks = expert_ids.reshape(step_count, group_count, SEQ, TOP)
    run_group = jax.checkpoint(jax.vmap(one_sequence, in_axes=(None, 0, 0)))

    def advance(carry_state, block_pair):
        return (carry_state, run_group(weights, block_pair[0], block_pair[1]))
    final_state, outputs = lax.scan(advance, jnp.zeros((), jnp.float32), (blocks, id_blocks))
    return outputs.reshape(N_FSDP * SEQ, D)

def reference(tokens, expert_ids, attn_gain, w_qkv, w_out, moe_gain, w_router, w_shared_in, w_shared_out, w_expert_in, w_expert_out, out_grad):
    weights = (attn_gain.astype(jnp.float32), w_qkv.astype(jnp.float32), w_out.astype(jnp.float32), moe_gain.astype(jnp.float32), w_router.astype(jnp.float32), w_shared_in.astype(jnp.float32), w_shared_out.astype(jnp.float32), w_expert_in.astype(jnp.float32), w_expert_out.astype(jnp.float32))

    def forward(tokens_in, weights_in):
        return block_layer(tokens_in, weights_in, expert_ids)
    result, pullback = jax.vjp(forward, tokens.astype(jnp.float32), weights)
    tokens_grad, weight_grads = pullback(out_grad.astype(jnp.float32))
    return (result.astype(jnp.bfloat16), tokens_grad, weight_grads[0], weight_grads[1], weight_grads[2], weight_grads[3], weight_grads[4], weight_grads[5], weight_grads[6], weight_grads[7], weight_grads[8])
```

```python
import functools

import jax
import jax.numpy as jnp
from jax import lax
from jax.experimental import pallas as pl
from jax.experimental.pallas import tpu as pltpu
from jax.sharding import PartitionSpec as P

D = 1536
HQ = 12
KV = 4
HD = 128
H = 512
SH = 1024
EXPERTS = 8
TOP = 6
ROWS = 12
W_ATT = 1152
W_SHARED = 768
W_ALL = W_ATT + W_SHARED
epsilon = 1e-05
MESH = pl.DeviceIdType.MESH
F32 = jnp.float32
BF16 = jnp.bfloat16
STRIDE = {"x": (32, 4), "z": (8, 4), "y": (2, 4), "c": (1, 2)}


def place(me, axis):
    stride, size = STRIDE[axis]
    return lax.rem(lax.div(me, stride), size)


def peer(me, axis, step):
    stride, size = STRIDE[axis]
    here = place(me, axis)
    return me + (lax.rem(here + step, size) - here) * stride


class Links:
    def __init__(self, send_sem, recv_sem, local_sem=None):
        self.me = lax.axis_index("fsdp")
        self.send_sem, self.recv_sem, self.local_sem = send_sem, recv_sem, local_sem
        self.count = 0
        self.local_count = 0
        self.x, self.y, self.z, self.c = (place(self.me, axis) for axis in "xyzc")

    def send(self, src, dst, axis, step):
        copy = pltpu.make_async_remote_copy(
            src_ref=src,
            dst_ref=dst,
            send_sem=self.send_sem.at[self.count],
            recv_sem=self.recv_sem.at[self.count],
            device_id=(peer(self.me, axis, step),),
            device_id_type=MESH,
        )
        copy.start()
        self.count += 1
        return copy

    def local(self, src, dst):
        copy = pltpu.make_async_copy(src, dst, self.local_sem.at[self.local_count])
        copy.start()
        self.local_count += 1
        return copy

    def greet(self, axes):
        barrier = pltpu.get_barrier_semaphore()
        total = 0
        for axis in axes:
            for step in range(1, STRIDE[axis][1]):
                pl.semaphore_signal(
                    barrier, inc=1, device_id=(peer(self.me, axis, step),), device_id_type=MESH
                )
                total += 1
        pl.semaphore_wait(barrier, total)


ORDER = (2, 1, 3)


def call(name, body, ins, outs, scratch, sends, locals_, collective_id):
    def kernel(*refs):
        n_in, n_out = len(ins), len(outs)
        send_sem, recv_sem, local_sem = refs[-3:]
        links = Links(send_sem, recv_sem, local_sem)
        body(links, refs[:n_in], refs[n_in : n_in + n_out], refs[n_in + n_out : -3])

    return pl.pallas_call(
        kernel,
        out_shape=[jax.ShapeDtypeStruct(shape, dtype) for shape, dtype in outs],
        in_specs=[pl.BlockSpec(memory_space=pltpu.VMEM)] * len(ins),
        out_specs=[pl.BlockSpec(memory_space=pltpu.VMEM)] * len(outs),
        scratch_shapes=[
            *[pltpu.VMEM(shape, dtype) for shape, dtype in scratch],
            pltpu.SemaphoreType.DMA((sends,)),
            pltpu.SemaphoreType.DMA((sends,)),
            pltpu.SemaphoreType.DMA((max(1, locals_),)),
        ],
        compiler_params=pltpu.CompilerParams(
            collective_id=collective_id, has_side_effects=True, vmem_limit_bytes=60 << 20
        ),
        name=name,
    )(*ins)


def pick_matrix(shape, source):
    row = lax.broadcasted_iota(jnp.int32, shape, 0)
    col = lax.broadcasted_iota(jnp.int32, shape, 1)
    return (col == source(row)).astype(BF16)


def moved(pick, rows):
    return jnp.dot(pick, rows, preferred_element_type=F32).astype(BF16)


def plane_gather_start(links, own, full, cut):
    here = links.z * 4 + links.y
    first = []
    for axis, half in (("y", cut[0]), ("z", cut[1])):
        for step in ORDER:
            first.append(links.send(own.at[half], full.at[(here, *half)], axis, step))
    return (first, own, full, cut)


def plane_gather_next(links, state):
    first, own, full, cut = state
    for copy in first[:3]:
        copy.wait_recv()
    second = []
    for step in ORDER:
        part = full.at[(pl.ds(links.z * 4, 4), *cut[0])]
        second.append(links.send(part, part, "z", step))
    for copy in first[3:]:
        copy.wait_recv()
    for step in ORDER:
        for z in range(4):
            part = full.at[(z * 4 + links.y, *cut[1])]
            second.append(links.send(part, part, "y", step))
    return (first, second)


def finish(copies):
    for copy in copies:
        copy.wait()


def weights_kernel(links, ins, outs, scratch):
    pack, expert_in, expert_out, normed, out_grad = ins
    dense, shared, all_in, all_out, all_normed, all_grad = outs
    arrived, own_dense, own_shared, got_dense, got_shared, got_in, got_out = scratch
    me, x, y, z, c = links.me, links.x, links.y, links.z, links.c
    here = z * 4 + y
    links.greet("xyzc")
    first = []
    for step in ORDER:
        first.append(links.send(pack.at[lax.rem(x + step, 4)], arrived.at[x], "x", step))
    late = [links.local(normed, all_normed.at[x]), links.local(out_grad, all_grad.at[c, x])]
    late.append(links.local(expert_in, got_in.at[here]))
    late.append(links.local(expert_out, got_out.at[here]))
    arrived[x] = pack[x]
    finish(first)
    pick = pick_matrix((48, 64), lambda row: row // ROWS * 16 + row % ROWS)
    for col in range(0, W_ALL, 384):
        block = moved(pick, arrived[:, :, col : col + 384].reshape(64, 384))
        if col < W_ATT:
            own_dense[:, col : col + 384] = block
        else:
            own_shared[:, col - W_ATT : col - W_ATT + 384] = block
    copies = [links.local(own_dense, got_dense.at[here]), links.local(own_shared, got_shared.at[here])]
    every = pl.ds(0, 48)
    lower, upper = pl.ds(0, 48), pl.ds(48, 48)
    states = [
        plane_gather_start(
            links, own_dense, got_dense, ((every, pl.ds(0, 640)), (every, pl.ds(640, 512)))
        ),
        plane_gather_start(
            links, own_shared, got_shared, ((every, pl.ds(0, 384)), (every, pl.ds(384, 384)))
        ),
        plane_gather_start(
            links, expert_in, got_in, ((lower, pl.ds(0, 1024)), (upper, pl.ds(0, 1024)))
        ),
        plane_gather_start(
            links, expert_out, got_out, ((lower, pl.ds(0, 512)), (upper, pl.ds(0, 512)))
        ),
    ]
    activations = []
    for step in ORDER:
        activations.append(links.send(normed, all_normed.at[x], "x", step))
        activations.append(links.send(out_grad, all_grad.at[c, x], "x", step))
    finish(copies)
    finish(late)
    done = [plane_gather_next(links, state) for state in states]
    finish(activations)
    for one, two in done:
        for copy in one:
            copy.wait_send()
        finish(two)
    last = [
        links.send(got_dense, dense.at[:, c], "c", 1),
        links.send(got_shared, shared.at[:, c], "c", 1),
        links.send(all_grad.at[c], all_grad.at[c], "c", 1),
        links.send(got_in.at[pl.ds(8 * (1 - c), 8)], all_in.at[:, c], "c", 1),
        links.send(got_out.at[pl.ds(8 * (1 - c), 8)], all_out.at[:, c], "c", 1),
    ]
    own = [
        links.local(got_dense, dense.at[:, c]),
        links.local(got_shared, shared.at[:, c]),
        links.local(got_in.at[pl.ds(8 * c, 8)], all_in.at[:, c]),
        links.local(got_out.at[pl.ds(8 * c, 8)], all_out.at[:, c]),
    ]
    finish(own)
    finish(last)


def gather_kernel(links, ins, outs, scratch):
    (own,) = ins
    (full,) = outs
    links.greet("x")
    copies = [links.send(own, full.at[links.x], "x", step) for step in ORDER]
    finish([links.local(own, full.at[links.x])])
    finish(copies)


def gather_pair_kernel(links, ins, outs, scratch):
    (own,) = ins
    (full,) = outs
    x, c = links.x, links.c
    links.greet("xc")
    copies = [links.send(own, full.at[c, x], "x", step) for step in ORDER]
    finish([links.local(own, full.at[c, x])])
    finish(copies)
    finish([links.send(full.at[c], full.at[c], "c", 1)])


def scatter_kernel(links, ins, outs, scratch):
    (parts,) = ins
    (total,) = outs
    (arrived,) = scratch
    x = links.x
    links.greet("x")
    copies = [
        links.send(parts.at[lax.rem(x + step, 4)], arrived.at[step - 1], "x", step) for step in ORDER
    ]
    finish(copies)
    total[...] = (
        parts[x].astype(F32) + arrived[0].astype(F32) + arrived[1].astype(F32) + arrived[2].astype(F32)
    )


def scatter_pair_kernel(links, ins, outs, scratch):
    (parts,) = ins
    (total,) = outs
    pair, arrived = scratch
    x, c = links.x, links.c
    links.greet("xc")
    finish([links.send(parts.at[1 - c], pair, "c", 1)])
    for block in range(4):
        pair[block] = (pair[block].astype(F32) + parts[c, block].astype(F32)).astype(BF16)
    copies = [
        links.send(pair.at[lax.rem(x + step, 4)], arrived.at[step - 1], "x", step) for step in ORDER
    ]
    finish(copies)
    total[...] = (
        pair[x].astype(F32) + arrived[0].astype(F32) + arrived[1].astype(F32) + arrived[2].astype(F32)
    )


def plane_scatter_start(links, full, first_got, cut):
    first = []
    for step in ORDER:
        to = lax.rem(links.z + step, 4) * 4
        first.append(
            links.send(full.at[(pl.ds(to, 4), *cut[0])], first_got[0].at[step - 1], "z", step)
        )
    for step in ORDER:
        to = lax.rem(links.y + step, 4)
        for z in range(4):
            first.append(
                links.send(full.at[(z * 4 + to, *cut[1])], first_got[1].at[step - 1, z], "y", step)
            )
    return (first, full, first_got, cut)


def plane_scatter_next(links, state, second_got):
    first, full, first_got, cut = state
    second = []
    for copy in first[:3]:
        copy.wait_recv()

    for half, axis in ((0, "y"), (1, "z")):
        if half:
            for copy in first[3:]:
                copy.wait_recv()
        for k in range(4):
            slot = links.z * 4 + k if half == 0 else k * 4 + links.y
            total = full[(slot, *cut[half])].astype(F32)
            for step in range(3):
                total = total + first_got[half][step, k].astype(F32)
            first_got[half][0, k] = total.astype(BF16)
        place_ = links.y if half == 0 else links.z
        for step in ORDER:
            second.append(
                links.send(
                    first_got[half].at[0, lax.rem(place_ + step, 4)],
                    second_got[half].at[step - 1],
                    axis,
                    step,
                )
            )
    return second


def plane_scatter_end(links, first_got, second_got, half):
    place_ = links.y if half == 0 else links.z
    total = first_got[half][0, place_].astype(F32)
    for step in range(3):
        total = total + second_got[half][step].astype(F32)
    return total


def grads_kernel(links, ins, outs, scratch):
    grad_in, grad_out, dense, shared = ins
    out_in, out_out, out_pack = outs
    (b_in, b_out, b_dense, b_shared, got_dense, back, pack_got) = scratch[:7]
    rest = scratch[7:]
    me, x, y, z, c = links.me, links.x, links.y, links.z, links.c
    links.greet("xyzc")
    pairs = [
        links.send(grad_in.at[:, 1 - c], b_in.at[pl.ds(8 * c, 8)], "c", 1),
        links.send(grad_out.at[:, 1 - c], b_out.at[pl.ds(8 * c, 8)], "c", 1),
        links.send(shared.at[:, 1 - c], b_shared.at[:, :, pl.ds(pl.multiple_of(c * 384, 128), 384)], "c", 1),
        links.send(dense.at[:, 1 - c], got_dense, "c", 1),
    ]
    own = [
        links.local(grad_in.at[:, c], b_in.at[pl.ds(8 * c, 8)]),
        links.local(grad_out.at[:, c], b_out.at[pl.ds(8 * c, 8)]),
        links.local(shared.at[:, c], b_shared.at[:, :, pl.ds(pl.multiple_of(c * 384, 128), 384)]),
    ]
    finish(pairs)
    finish(own)

    @pl.loop(0, 16)
    def _(block):
        b_dense[block] = (got_dense[block].astype(F32) + dense[block, c].astype(F32)).astype(BF16)

    every = pl.ds(0, 48)
    lower, upper = pl.ds(0, 48), pl.ds(48, 48)
    cuts = [
        ((lower, pl.ds(0, 1024)), (upper, pl.ds(0, 1024))),
        ((lower, pl.ds(0, 512)), (upper, pl.ds(0, 512))),
        ((every, pl.ds(0, 640)), (every, pl.ds(640, 512))),
        ((every, pl.ds(0, 384)), (every, pl.ds(384, 384))),
    ]
    states, seconds = [], []
    for index, (full, cut) in enumerate(zip((b_in, b_out, b_dense, b_shared), cuts)):
        first_got = rest[4 * index : 4 * index + 2]
        states.append(plane_scatter_start(links, full, first_got, cut))
    for index, state in enumerate(states):
        seconds.append(plane_scatter_next(links, state, rest[4 * index + 2 : 4 * index + 4]))
    targets = [
        (out_in, (slice(0, 48), slice(0, 1024)), (slice(48, 96), slice(0, 1024))),
        (out_out, (slice(0, 48), slice(0, 512)), (slice(48, 96), slice(0, 512))),
        (back, (slice(0, 48), slice(0, 640)), (slice(0, 48), slice(640, 1152))),
        (back, (slice(0, 48), slice(1152, 1536)), (slice(0, 48), slice(1536, 1920))),
    ]
    for index, second in enumerate(seconds):
        target, *where = targets[index]
        for copy in states[index][0]:
            copy.wait_send()
        finish(second)
        for half in range(2):
            total = plane_scatter_end(
                links, rest[4 * index : 4 * index + 2], rest[4 * index + 2 : 4 * index + 4], half
            )
            target[where[half]] = total.astype(target.dtype)
    pick = pick_matrix((64, 48), lambda row: jnp.where(row % 16 < ROWS, row // 16 * ROWS + row % 16, -1))
    for col in range(0, W_ALL, 384):
        pack_got[:, :, col : col + 384] = moved(pick, back[:, col : col + 384]).reshape(4, 16, 384)
    last = [
        links.send(pack_got.at[lax.rem(x + step, 4)], out_pack.at[x], "x", step) for step in ORDER
    ]
    out_pack[x] = pack_got[x]
    finish(last)


def swish_parts(joined, width):
    gate_part = joined[..., :width].astype(F32)
    up_part = joined[..., width:].astype(F32)
    return (gate_part, up_part, jax.nn.sigmoid(gate_part))


def swish_backward(joined, width, act_grad):
    gate_part, up_part, sig_gate = swish_parts(joined, width)
    gate_slope = sig_gate * (1.0 + gate_part * (1.0 - sig_gate))
    return jnp.concatenate(
        [act_grad * up_part * gate_slope, act_grad * gate_part * sig_gate], axis=-1
    ).astype(BF16)


def packed_weights(attn_gain, w_qkv, w_out, moe_gain, w_router, w_shared_in, w_shared_out):
    scaled = (w_qkv.astype(F32) * attn_gain.astype(F32)[:, None]).astype(BF16)
    parts = [
        scaled[:, :D].reshape(ROWS, 4, 384),
        scaled[:, D : D + 512].reshape(ROWS, 4, 128),
        scaled[:, D + 512 :].reshape(ROWS, 4, 128),
        w_out.reshape(ROWS, 4, 384),
    ]
    misc = jnp.concatenate(
        [w_router, moe_gain[:, None], jnp.zeros((ROWS, 119), BF16)], axis=1
    )
    parts.append(jnp.broadcast_to(misc[:, None], (ROWS, 4, 128)))
    gate = w_shared_in[:, :SH].reshape(ROWS, 4, 2, 128)
    up = w_shared_in[:, SH:].reshape(ROWS, 4, 2, 128)
    down = w_shared_out.reshape(ROWS, 4, 2, 128)
    parts.append(jnp.stack([gate, up, down], axis=3).reshape(ROWS, 4, 768))
    joined = jnp.concatenate(parts, axis=2).transpose(1, 0, 2)
    return jnp.pad(joined, ((0, 0), (0, 4), (0, 0)))


def natural(blocks):
    width = blocks.shape[-1]
    return blocks.reshape(32, 4, ROWS, width).transpose(1, 0, 2, 3).reshape(D, width)


def blocked(rows):
    width = rows.shape[-1]
    return rows.reshape(4, 32, ROWS, width).transpose(1, 0, 2, 3).reshape(16, 2, 48, width)


def mm(spec, a, b):
    return jnp.einsum(spec, a, b, preferred_element_type=F32)


def causal_scores(q, k):
    scores = mm("bqgd,bsd->bgqs", q, k) * HD**-0.5
    causal = jnp.arange(128)[:, None] >= jnp.arange(128)[None, :]
    return jnp.where(causal, scores, -1e30)


def local(
    tokens,
    expert_ids,
    attn_gain,
    w_qkv,
    w_out,
    moe_gain,
    w_router,
    w_shared_in,
    w_shared_out,
    w_expert_in,
    w_expert_out,
    out_grad,
):
    me = lax.axis_index("fsdp")
    x, c = me // 32, me % 2
    inputs = tokens.astype(F32)
    inverse_one = lax.rsqrt(jnp.mean(inputs * inputs, axis=-1, keepdims=True) + epsilon)
    normed = (inputs * inverse_one).astype(BF16)
    pack = packed_weights(attn_gain, w_qkv, w_out, moe_gain, w_router, w_shared_in, w_shared_out)
    dense, shared, all_in, all_out, all_normed, all_grad = call(
        "weights",
        weights_kernel,
        (pack, w_expert_in, w_expert_out, normed, out_grad),
        (
            ((16, 2, 48, W_ATT), BF16),
            ((16, 2, 48, W_SHARED), BF16),
            ((8, 2, 96, 1024), BF16),
            ((8, 2, 96, 512), BF16),
            ((4, 128, D), BF16),
            ((2, 4, 128, D), BF16),
        ),
        (
            ((4, 16, W_ALL), BF16),
            ((48, W_ATT), BF16),
            ((48, W_SHARED), BF16),
            ((16, 48, W_ATT), BF16),
            ((16, 48, W_SHARED), BF16),
            ((16, 96, 1024), BF16),
            ((16, 96, 512), BF16),
        ),
        100,
        20,
        1,
    )
    dense = natural(dense)
    shared = lax.dynamic_slice_in_dim(natural(shared), c * 384, 384, axis=1)
    att_in, att_out, misc = dense[:, :640], dense[:, 640:1024], dense[:, 1024:]
    in_weight = all_in.reshape(D, 1024)
    out_weight = all_out.reshape(D, 512)
    sh_in, sh_out = shared[:, :256], shared[:, 256:]
    gain_two = misc[:, 8].astype(F32)
    router = misc[:, :8]

    rows = all_normed.reshape(512, D)
    qkv = mm("sd,dc->sc", rows, att_in).astype(BF16)
    q = qkv[:, :384].reshape(4, 128, 3, HD)
    k = qkv[:, 384:512].reshape(4, 128, HD)
    v = qkv[:, 512:].reshape(4, 128, HD)
    scores = causal_scores(q, k)
    peak = jnp.max(scores, axis=-1, keepdims=True)
    exponent = jnp.exp(scores - peak)
    totals = jnp.sum(exponent, axis=-1, keepdims=True)
    probs = exponent / totals
    probs_low = probs.astype(BF16)
    head_mix = mm("bgqs,bsd->bqgd", probs_low, v).astype(BF16).reshape(512, 384)
    mixed = mm("sa,da->sd", head_mix, att_out).astype(BF16).reshape(4, 128, D)
    attended = call(
        "attended", scatter_kernel, (mixed,), (((128, D), F32),), (((3, 128, D), BF16),), 3, 1, 2
    )[0]
    hidden = inputs + attended
    inverse_two = lax.rsqrt(jnp.mean(hidden * hidden, axis=-1, keepdims=True) + epsilon)
    moe_in = (hidden * inverse_two * gain_two).astype(BF16)
    logits = jnp.dot(moe_in, router, preferred_element_type=F32)
    router_probs = jax.nn.softmax(logits, axis=-1)
    choose = (expert_ids[:, :, None] == jnp.arange(EXPERTS)[None, None, :]).astype(F32)
    chosen = jnp.sum(choose, axis=1)
    gates = chosen * router_probs
    high = gates.astype(BF16)
    low = (gates - high.astype(F32)).astype(BF16)
    sent = jnp.concatenate([moe_in, high, low, jnp.zeros((128, 112), BF16)], axis=1)
    everyone = call(
        "moe_rows", gather_pair_kernel, (sent,), (((2, 4, 128, 1664), BF16),), (), 4, 1, 3
    )[0].reshape(1024, 1664)
    everyone_in = everyone[:, :D]
    mine = 2 * x + c
    pick = (jnp.arange(16) % 8 == mine).astype(F32)
    gate = jnp.sum(everyone[:, D : D + 16].astype(F32) * pick, axis=1, keepdims=True)
    grads = all_grad.reshape(1024, D)

    gate_up = mm("sd,dh->sh", everyone_in, in_weight).astype(BF16)
    gp, up, sg = swish_parts(gate_up, H)
    act = (gp * sg * up).astype(BF16)
    gated = (act.astype(F32) * gate).astype(BF16)
    sh_gate_up = mm("sd,dh->sh", everyone_in, sh_in).astype(BF16)
    gp, up, sg = swish_parts(sh_gate_up, 128)
    sh_act = (gp * sg * up).astype(BF16)
    result = mm("sh,dh->sd", gated, out_weight) + mm("sh,dh->sd", sh_act, sh_out)
    moe_out = call(
        "moe_sum",
        scatter_pair_kernel,
        (result.astype(BF16).reshape(2, 4, 128, D),),
        (((128, D), F32),),
        (((4, 128, D), BF16), ((3, 128, D), BF16)),
        4,
        1,
        4,
    )[0]
    block_out = (hidden + moe_out).astype(BF16)

    act_raw = mm("sd,dh->sh", grads, out_weight)
    gate_grad = jnp.sum(act.astype(F32) * act_raw, axis=1, keepdims=True)
    gate_up_grad = swish_backward(gate_up, H, act_raw * gate)
    sh_grad = swish_backward(sh_gate_up, 128, mm("sd,dh->sh", grads, sh_out))
    in_grad = mm("sd,sh->dh", everyone_in, gate_up_grad).astype(BF16)
    out_w_grad = mm("sd,sh->dh", grads, gated).astype(BF16)
    sh_in_grad = mm("sd,sh->dh", everyone_in, sh_grad).astype(BF16)
    sh_out_grad = mm("sd,sh->dh", grads, sh_act).astype(BF16)
    back = mm("sh,dh->sd", gate_up_grad, in_weight) + mm("sh,dh->sd", sh_grad, sh_in)
    gg_high = gate_grad.astype(BF16)
    gg_low = (gate_grad - gg_high.astype(F32)).astype(BF16)
    spread = jnp.concatenate(
        [
            (gg_high.astype(F32) * pick[:8]),
            (gg_low.astype(F32) * pick[:8]),
            jnp.zeros((1024, 112), F32),
        ],
        axis=1,
    )
    back = jnp.concatenate([back, spread], axis=1).astype(BF16).reshape(2, 4, 128, 1664)
    moe_back = call(
        "moe_back",
        scatter_pair_kernel,
        (back,),
        (((128, 1664), F32),),
        (((4, 128, 1664), BF16), ((3, 128, 1664), BF16)),
        4,
        1,
        5,
    )[0]
    prob_grad = chosen * (moe_back[:, D : D + 8] + moe_back[:, D + 8 : D + 16])
    logit_grad = router_probs * (
        prob_grad - jnp.sum(router_probs * prob_grad, axis=-1, keepdims=True)
    )
    logit_grad = logit_grad.astype(BF16)
    moe_in_grad = moe_back[:, :D] + mm("se,de->sd", logit_grad, router)
    router_grad = mm("sd,se->de", moe_in, logit_grad)
    gain_two_grad = jnp.sum(moe_in_grad * hidden * inverse_two, axis=0)
    scaled = gain_two * moe_in_grad
    cotangent = out_grad.astype(F32)
    hidden_grad = (
        cotangent
        + inverse_two * scaled
        - hidden * inverse_two**3 * jnp.mean(scaled * hidden, axis=-1, keepdims=True)
    )
    all_hidden = call(
        "hidden_rows",
        gather_kernel,
        (hidden_grad.astype(BF16),),
        (((4, 128, D), BF16),),
        (),
        3,
        1,
        6,
    )[0].reshape(512, D)
    att_out_grad = mm("sd,sa->da", all_hidden, head_mix).astype(BF16)
    mix_grad = mm("sd,da->sa", all_hidden, att_out).astype(BF16).reshape(4, 128, 3, HD)
    dprob = mm("bqgd,bsd->bgqs", mix_grad, v)
    value_grad = mm("bgqs,bqgd->bsd", probs_low, mix_grad)
    delta = jnp.sum(probs * dprob, axis=-1, keepdims=True)
    score_grad = (probs * (dprob - delta)).astype(BF16)
    query_grad = mm("bgqs,bsd->bqgd", score_grad, k) * HD**-0.5
    key_grad = mm("bgqs,bqgd->bsd", score_grad, q) * HD**-0.5
    qkv_grad = jnp.concatenate(
        [query_grad.reshape(512, 384), key_grad.reshape(512, 128), value_grad.reshape(512, 128)],
        axis=1,
    ).astype(BF16)
    att_in_grad = mm("sd,sc->dc", rows, qkv_grad).astype(BF16)
    normed_back = mm("sc,dc->sd", qkv_grad, att_in).astype(BF16).reshape(4, 128, D)
    scaled = call(
        "normed_back",
        scatter_kernel,
        (normed_back,),
        (((128, D), F32),),
        (((3, 128, D), BF16),),
        3,
        1,
        7,
    )[0]
    tokens_grad = (
        hidden_grad
        + inverse_one * scaled
        - inputs * inverse_one**3 * jnp.mean(scaled * inputs, axis=-1, keepdims=True)
    )
    misc_grad = jnp.concatenate(
        [router_grad, gain_two_grad[:, None], jnp.zeros((D, 119), F32)], axis=1
    ).astype(BF16)
    dense_grad = blocked(jnp.concatenate([att_in_grad, att_out_grad, misc_grad], axis=1))
    shared_grad = blocked(jnp.concatenate([sh_in_grad, sh_out_grad], axis=1))
    halves = []
    for r, (w0, w1) in ((48, (1024, 1024)), (48, (512, 512)), (48, (640, 512)), (48, (384, 384))):
        halves += [((3, 4, r, w0), BF16), ((3, 4, r, w1), BF16), ((3, r, w0), BF16), ((3, r, w1), BF16)]
    grad_in, grad_out, grad_pack = call(
        "weight_sums",
        grads_kernel,
        (in_grad.reshape(8, 2, 96, 1024), out_w_grad.reshape(8, 2, 96, 512), dense_grad, shared_grad),
        (((96, 1024), F32), ((96, 512), F32), ((4, 16, W_ALL), BF16)),
        (
            ((16, 96, 1024), BF16),
            ((16, 96, 512), BF16),
            ((16, 48, W_ATT), BF16),
            ((16, 48, W_SHARED), BF16),
            ((16, 48, W_ATT), BF16),
            ((48, W_ALL), BF16),
            ((4, 16, W_ALL), BF16),
            *halves,
        ),
        120,
        8,
        8,
    )
    pieces = grad_pack[:, :ROWS].astype(F32)

    def spread_out(start, width):
        return pieces[:, :, start : start + width].transpose(1, 0, 2).reshape(ROWS, 4 * width)

    raw_qkv = jnp.concatenate(
        [spread_out(0, 384), spread_out(384, 128), spread_out(512, 128)], axis=1
    )
    attn_gain_grad = jnp.sum(raw_qkv * w_qkv.astype(F32), axis=1)
    qkv_weight_grad = raw_qkv * attn_gain.astype(F32)[:, None]
    misc_sum = jnp.sum(pieces[:, :, 1024:1152], axis=0)
    both = pieces[:, :, W_ATT:].reshape(4, ROWS, 2, 3, 128).transpose(1, 3, 0, 2, 4)
    both = both.reshape(ROWS, 3, SH)
    return (
        block_out,
        tokens_grad,
        attn_gain_grad,
        qkv_weight_grad,
        spread_out(640, 384),
        misc_sum[:, 8],
        misc_sum[:, :8],
        both[:, :2].reshape(ROWS, 2 * SH),
        both[:, 2],
        grad_in,
        grad_out,
    )


def solution(mesh):
    wide, flat = P("fsdp", None), P("fsdp")
    return jax.shard_map(
        local,
        mesh=mesh,
        in_specs=(wide, wide, flat, wide, wide, flat, wide, wide, wide, wide, wide, wide),
        out_specs=(wide, wide, flat, wide, wide, flat, wide, wide, wide, wide, wide),
        check_vma=False,
    )
```

```python
import jax
import jax.numpy as jnp
from jax import lax
from jax.experimental import pallas as pl
from jax.experimental.pallas import tpu as pltpu
from jax.sharding import PartitionSpec as P

D = 1536
HD = 128
SH = 1024
EXPERTS = 8
TOP = 6
ROWS = 12
SEQ = 128
W_ATT = 1152
W_SHARED = 768
W_ALL = W_ATT + W_SHARED
WIDE = D + 128
epsilon = 1e-05
MESH = pl.DeviceIdType.MESH
F32 = jnp.float32
BF16 = jnp.bfloat16
STRIDE = {"x": (32, 4), "z": (8, 4), "y": (2, 4), "c": (1, 2)}
FAR_FIRST = (2, 1, 3)
NEAR_FIRST = (1, 3, 2)


def place(me, axis):
    stride, size = STRIDE[axis]
    return lax.rem(lax.div(me, stride), size)


def peer(me, axis, step):
    stride, size = STRIDE[axis]
    here = place(me, axis)
    return me + (lax.rem(here + step, size) - here) * stride


class Links:
    def __init__(self, send_sem, recv_sem):
        self.me = lax.axis_index("fsdp")
        self.send_sem, self.recv_sem = send_sem, recv_sem
        self.count = 0
        self.x, self.y, self.z, self.c = (place(self.me, axis) for axis in "xyzc")

    def take(self, number):
        first = self.count
        self.count += number
        return first

    def copy(self, src, dst, axis, step, sem):
        return pltpu.make_async_remote_copy(
            src_ref=src,
            dst_ref=dst,
            send_sem=self.send_sem.at[sem],
            recv_sem=self.recv_sem.at[sem],
            device_id=(peer(self.me, axis, step),),
            device_id_type=MESH,
        )

    def send(self, src, dst, axis, step):
        copy = self.copy(src, dst, axis, step, self.take(1))
        copy.start()
        return copy

    def local(self, src, dst):
        copy = pltpu.make_async_copy(src, dst, self.send_sem.at[self.take(1)])
        copy.start()
        return copy

    def greet(self, axes):
        barrier = pltpu.get_barrier_semaphore()
        total = 0
        for axis in axes:
            for step in range(1, STRIDE[axis][1]):
                pl.semaphore_signal(
                    barrier, inc=1, device_id=(peer(self.me, axis, step),), device_id_type=MESH
                )
                total += 1
        return lambda: pl.semaphore_wait(barrier, total)


def finish(copies):
    for copy in copies:
        copy.wait()


def received(copies):
    for copy in copies:
        copy.wait_recv()


def sent(copies):
    for copy in copies:
        copy.wait_send()


def dot(a, b):
    return jnp.dot(a, b, preferred_element_type=F32)


def dot_nt(a, b):
    return lax.dot_general(a, b, (((1,), (1,)), ((), ())), preferred_element_type=F32)


def dot_tn(a, b):
    return lax.dot_general(a, b, (((0,), (0,)), ((), ())), preferred_element_type=F32)


def pick_matrix(shape, source):
    row = lax.broadcasted_iota(jnp.int32, shape, 0)
    col = lax.broadcasted_iota(jnp.int32, shape, 1)
    return (col == source(row)).astype(BF16)


def moved(pick, rows):
    return dot(pick, rows).astype(BF16)


def gather_first(links, own, part, here, cut):
    first = []
    for axis, half in (("y", cut[0]), ("z", cut[1])):
        for step in FAR_FIRST:
            first.append(links.send(own.at[half], part(here, half), axis, step))
    return first


def gather_second(links, first, part, cut):
    received(first[:3])
    second = []
    for step in FAR_FIRST:
        piece = part(pl.ds(links.z * 4, 4), cut[0])
        second.append(links.send(piece, piece, "z", step))
    received(first[3:])
    for step in FAR_FIRST:
        for z in range(4):
            piece = part(z * 4 + links.y, cut[1])
            second.append(links.send(piece, piece, "y", step))
    return second


def scatter_first(links, part, got, cut):
    first = []
    for step in FAR_FIRST:
        to = lax.rem(links.z + step, 4) * 4
        first.append(links.send(part(pl.ds(to, 4), cut[0]), got[0].at[step - 1], "z", step))
    for step in FAR_FIRST:
        to = lax.rem(links.y + step, 4)
        for z in range(4):
            first.append(
                links.send(part(z * 4 + to, cut[1]), got[1].at[step - 1, z], "y", step)
            )
    return first


def scatter_second(links, first, part, got, last, cut):
    second = []
    for half, axis in ((0, "y"), (1, "z")):
        received(first[3:] if half else first[:3])
        here = links.z if half else links.y

        @pl.loop(0, 4)
        def _(k):
            slot = k * 4 + links.y if half else links.z * 4 + k
            total = part(slot, cut[half])[...].astype(F32)
            for step in range(3):
                total = total + got[half][step, k].astype(F32)
            got[half][0, k] = total.astype(BF16)

        for step in FAR_FIRST:
            second.append(
                links.send(
                    got[half].at[0, lax.rem(here + step, 4)], last[half].at[step - 1], axis, step
                )
            )
    return second


def scatter_end(links, got, last, half):
    here = links.z if half else links.y
    total = got[half][0, here].astype(F32)
    for step in range(3):
        total = total + last[half][step].astype(F32)
    return total


INS = (
    "tokens",
    "ids",
    "gain_one",
    "w_qkv",
    "w_out",
    "w_router",
    "gain_two",
    "w_sin",
    "w_sout",
    "e_in",
    "e_out",
    "out_grad",
)
OUTS = {
    "block_out": ((SEQ, D), BF16),
    "tokens_grad": ((SEQ, D), F32),
    "g_gain": ((ROWS, 128), F32),
    "g_qkv": ((ROWS, 2560), F32),
    "g_out": ((ROWS, D), F32),
    "g_misc": ((ROWS, 128), F32),
    "g_sin": ((ROWS, 2 * SH), F32),
    "g_sout": ((ROWS, SH), F32),
    "g_ein": ((96, 1024), F32),
    "g_eout": ((96, 512), F32),
}
SCRATCH = {
    "pack": ((4, 16, W_ALL), BF16),
    "arrived": ((4, 16, W_ALL), BF16),
    "dense": ((16, 2, 48, W_ATT), BF16),
    "shared": ((16, 2, 48, W_SHARED), BF16),
    "got": ((16, 96, D), BF16),
    "full": ((8, 2, 96, D), BF16),
    "nat": ((D, D), BF16),
    "normed": ((4, SEQ, D), BF16),
    "qkv": ((4, SEQ, 640), BF16),
    "mix": ((4, SEQ, 384), BF16),
    "send_y": ((4, 2, SEQ, D), BF16),
    "send_x": ((4, 2, SEQ, WIDE), BF16),
    "pair_y": ((4, SEQ, D), BF16),
    "pair_x": ((4, SEQ, WIDE), BF16),
    "got_y": ((3, SEQ, D), BF16),
    "got_x": ((3, SEQ, WIDE), BF16),
    "hidden": ((SEQ, D), F32),
    "probs": ((SEQ, 128), F32),
    "rows": ((4, 2, SEQ, WIDE), BF16),
    "cot": ((4, 2, SEQ, D), BF16),
    "gated": ((4, 256, 640), BF16),
    "joint": ((4, 256, 1280), BF16),
    "low": ((4, SEQ, D), BF16),
    "dsh": ((16, 2, 48, 384), BF16),
    "dgot": ((16, 48, W_ATT), BF16),
    "back": ((48, W_ALL), BF16),
    "e_got0": ((3, 4, 48, D), BF16),
    "e_got1": ((3, 4, 48, D), BF16),
    "e_last0": ((3, 48, D), BF16),
    "e_last1": ((3, 48, D), BF16),
    "d_got0": ((3, 4, 48, 640), BF16),
    "d_got1": ((3, 4, 48, 512), BF16),
    "d_last0": ((3, 48, 640), BF16),
    "d_last1": ((3, 48, 512), BF16),
    "s_got0": ((3, 4, 48, 384), BF16),
    "s_got1": ((3, 4, 48, 384), BF16),
    "s_last0": ((3, 48, 384), BF16),
    "s_last1": ((3, 48, 384), BF16),
}
SEMS = 256


class Bag:
    pass


def near(i):
    return jnp.where(i == 2, 3, jnp.where(i == 3, 2, i))


def far(i):
    return jnp.where(i == 0, 2, jnp.where(i == 3, 0, jnp.where(i == 2, 3, 1)))


def causal_probs(q, k):
    scores = dot_nt(q, k) * HD**-0.5
    row = lax.broadcasted_iota(jnp.int32, (SEQ, SEQ), 0)
    col = lax.broadcasted_iota(jnp.int32, (SEQ, SEQ), 1)
    scores = jnp.where(col <= row, scores, -1e30)
    exponent = jnp.exp(scores - jnp.max(scores, axis=1, keepdims=True))
    return exponent / jnp.sum(exponent, axis=1, keepdims=True)


def kernel(*refs):
    b = Bag()
    names = [*INS, *OUTS, *SCRATCH]
    for name, ref in zip(names, refs):
        setattr(b, name, ref)
    links = Links(*refs[len(names) :])
    x, y, z, c = links.x, links.y, links.z, links.c
    other = 1 - c
    here = z * 4 + y
    mine = 2 * x + c
    every = pl.ds(0, 48)
    e_cut = ((pl.ds(0, 48),), (pl.ds(48, 48),))
    d_cut = ((every, pl.ds(0, 640)), (every, pl.ds(640, 512)))
    s_cut = ((every, pl.ds(0, 384)), (every, pl.ds(384, 384)))
    d_part = lambda slots, half: b.dense.at[(slots, c, *half)]
    s_part = lambda slots, half: b.shared.at[(slots, c, *half)]
    e_part = lambda slots, half: b.got.at[(slots, *half)]

    greeted = links.greet("xyzc")
    b.got[here, :, 0:1024] = b.e_in[...]
    b.got[here, :, 1024:1536] = b.e_out[...]
    b.pack[...] = jnp.zeros_like(b.pack)
    gain_one = b.gain_one[...].astype(F32)
    for k in range(4):
        for start, width, at in ((k * 384, 384, 0), (D + k * 128, 128, 384), (2048 + k * 128, 128, 512)):
            b.pack[k, 0:ROWS, at : at + width] = (
                b.w_qkv[:, start : start + width].astype(F32) * gain_one
            ).astype(BF16)
        b.pack[k, 0:ROWS, 640:1024] = b.w_out[:, k * 384 : k * 384 + 384]
        b.pack[k, 0:ROWS, 1024:1032] = b.w_router[...]
        b.pack[k, 0:ROWS, 1032:1033] = b.gain_two[...]
        for core in range(2):
            at, unit = W_ATT + 384 * core, (2 * k + core) * 128
            b.pack[k, 0:ROWS, at : at + 128] = b.w_sin[:, unit : unit + 128]
            b.pack[k, 0:ROWS, at + 128 : at + 256] = b.w_sin[:, SH + unit : SH + unit + 128]
            b.pack[k, 0:ROWS, at + 256 : at + 384] = b.w_sout[:, unit : unit + 128]
    greeted()
    exchange = [
        links.send(b.pack.at[lax.rem(x + step, 4)], b.arrived.at[x], "x", step)
        for step in FAR_FIRST
    ]
    e_first = gather_first(links, b.got.at[here], e_part, here, e_cut)
    inputs = b.tokens[...].astype(F32)
    inverse_one = lax.rsqrt(jnp.mean(inputs * inputs, axis=1, keepdims=True) + epsilon)
    b.normed[x] = (inputs * inverse_one).astype(BF16)
    b.cot[x, c] = b.out_grad[...]
    normed_sends = [
        links.send(b.normed.at[x], b.normed.at[x], "x", step) for step in FAR_FIRST
    ]
    cot_pair = links.send(b.cot.at[x, c], b.cot.at[x, c], "c", 1)
    b.arrived[x] = b.pack[x]
    finish(exchange)
    pick = pick_matrix((48, 64), lambda row: row // ROWS * 16 + row % ROWS)
    for col in range(0, W_ALL, 384):
        block = moved(pick, b.arrived[:, :, col : col + 384].reshape(64, 384))
        if col < W_ATT:
            b.dense[here, c, :, col : col + 384] = block
        else:
            b.shared[here, c, :, col - W_ATT : col - W_ATT + 384] = block

    d_first = gather_first(links, b.dense.at[here, c], d_part, here, d_cut)
    d_second = gather_second(links, d_first, d_part, d_cut)
    s_first = gather_first(links, b.shared.at[here, c], s_part, here, s_cut)
    received(d_second)
    sent(d_first + d_second)
    d_pair = links.send(b.dense.at[:, c], b.dense.at[:, c], "c", 1)
    e_second = gather_second(links, e_first, e_part, e_cut)
    s_second = gather_second(links, s_first, s_part, s_cut)
    received(normed_sends)
    cot_base = links.take(4)
    cot_copy = lambda step: links.copy(
        b.cot.at[x, c], b.cot.at[x, c], "x", step, cot_base + step
    )
    for step in NEAR_FIRST:
        cot_copy(step).start()
    d_pair.wait()

    order = pick_matrix(
        (192, 192), lambda row: row % 48 // ROWS * 48 + row // 48 * ROWS + row % ROWS
    )

    def to_rows(j, source, start, at):
        piece = source[pl.ds(2 * j, 2), :, :, start].reshape(192, 384)
        piece = moved(order, piece)
        for k in range(4):
            row = pl.multiple_of(k * 384 + j * 48, 16)
            b.nat[pl.ds(row, 48), at : at + 384] = piece[k * 48 : k * 48 + 48]

    def to_blocks(j, target, start, at):
        pieces = [
            b.nat[pl.ds(pl.multiple_of(k * 384 + j * 48, 16), 48), at : at + 384] for k in range(4)
        ]
        piece = moved(order, jnp.concatenate(pieces, axis=0))
        target[pl.ds(2 * j, 2), :, :, start] = piece.reshape(2, 2, 48, 384)

    @pl.loop(0, 8)
    def _(j):
        for part in range(3):
            to_rows(j, b.dense, pl.ds(part * 384, 384), part * 384)

    for at, width in ((0, 256), (256, 256), (512, 128)):
        result = dot(b.normed[...].reshape(512, D), b.nat[:, at : at + width])
        b.qkv[:, :, at : at + width] = result.astype(BF16).reshape(4, SEQ, width)
    mix_base = links.take(4)

    def mix_copy(step):
        return links.copy(
            b.send_y.at[lax.rem(x + step, 4), 0], b.got_y.at[step - 1], "x", step, mix_base + step
        )

    @pl.loop(0, 4)
    def _(i):
        step = far(i)
        s = lax.rem(x + step, 4)
        key, value = b.qkv[s, :, 384:512], b.qkv[s, :, 512:640]
        for h in range(3):
            head = slice(h * HD, (h + 1) * HD)
            probs = causal_probs(b.qkv[s, :, head], key)
            b.mix[s, :, head] = dot(probs.astype(BF16), value).astype(BF16)
        for n in range(2):
            rows = slice(n * 768, (n + 1) * 768)
            b.send_y[s, 0, :, rows] = dot_nt(b.mix[s], b.nat[rows, 640:1024]).astype(BF16)

        @pl.when(i < 3)
        def _():
            mix_copy(step).start()

    received(e_second)
    received(s_second)
    sent(e_first + e_second + s_first + s_second)
    half = pl.ds(pl.multiple_of(other * 384, 128), 384)
    s_pair = links.send(b.shared.at[:, c, :, half], b.shared.at[:, c, :, half], "c", 1)
    e_pair = links.send(b.got.at[pl.ds(8 * other, 8)], b.full.at[:, c], "c", 1)
    e_own = links.local(b.got.at[pl.ds(8 * c, 8)], b.full.at[:, c])

    for step in FAR_FIRST:
        mix_copy(step).wait()
    hidden = b.tokens[...].astype(F32) + b.send_y[x, 0].astype(F32)
    for step in range(3):
        hidden = hidden + b.got_y[step].astype(F32)
    b.hidden[...] = hidden
    inverse_two = lax.rsqrt(jnp.mean(hidden * hidden, axis=1, keepdims=True) + epsilon)
    lane8 = lax.broadcasted_iota(jnp.int32, (8, 128), 1)
    gain_two = dot_nt((lane8 == 8).astype(BF16), b.nat[:, 1024:1152])[0:1]
    moe_in = (hidden * inverse_two * gain_two).astype(BF16)
    b.rows[x, c, :, 0:D] = moe_in
    lane = lax.broadcasted_iota(jnp.int32, (SEQ, 128), 1)
    logits = jnp.where(lane < EXPERTS, dot(moe_in, b.nat[:, 1024:1152]), -1e30)
    exponent = jnp.exp(logits - jnp.max(logits, axis=1, keepdims=True))
    router_probs = exponent / jnp.sum(exponent, axis=1, keepdims=True)
    b.probs[...] = router_probs
    chosen = jnp.zeros((SEQ, 128), F32)
    for k in range(TOP):
        chosen = chosen + (b.ids[:, k : k + 1] == lane).astype(F32)
    gates = chosen * router_probs
    high = gates.astype(BF16).astype(F32)
    b.rows[x, c, :, D:WIDE] = (high + pltpu.roll(gates - high, 8, 1)).astype(BF16)
    rows_base = links.take(4)
    rows_copy = lambda step: links.copy(
        b.rows.at[x, c], b.rows.at[x, c], "x", step, rows_base + step
    )
    for step in NEAR_FIRST:
        rows_copy(step).start()
    pair_rows = links.take(4)
    pair_cot = links.take(4)
    forward_rows = lambda s, d: links.copy(
        b.rows.at[s, c], b.rows.at[s, c], "c", 1, pair_rows + d
    )
    forward_cot = lambda s, d: links.copy(b.cot.at[s, c], b.cot.at[s, c], "c", 1, pair_cot + d)
    forward_rows(x, 0).start()

    s_pair.wait()
    e_pair.wait()
    e_own.wait()

    @pl.loop(0, 8)
    def _(j):
        to_rows(j, b.shared, pl.ds(pl.multiple_of(c * 384, 128), 384), W_ATT)

    back_pair = links.take(4)
    back_base = links.take(4)
    sum_pair = links.take(4)
    sum_base = links.take(4)
    back_forward = lambda s, d: links.copy(
        b.send_x.at[s, other], b.pair_x.at[s], "c", 1, back_pair + d
    )
    sum_forward = lambda s, d: links.copy(
        b.send_y.at[s, other], b.pair_y.at[s], "c", 1, sum_pair + d
    )
    back_copy = lambda step: links.copy(
        b.send_x.at[lax.rem(x + step, 4), c], b.got_x.at[step - 1], "x", step, back_base + step
    )
    sum_copy = lambda step: links.copy(
        b.send_y.at[lax.rem(x + step, 4), c], b.got_y.at[step - 1], "x", step, sum_base + step
    )
    cot_pair.wait()

    @pl.loop(0, 4)
    def _(i):
        d = near(i)
        s = lax.rem(x + d, 4)

        @pl.when(i > 0)
        def _():
            rows_copy(4 - d).wait_recv()
            forward_rows(s, d).start()
            cot_copy(4 - d).wait_recv()
            forward_cot(s, d).start()
            forward_cot(s, d).wait_recv()

        forward_rows(s, d).wait_recv()
        tokens = b.rows[s, :, :, 0:D].reshape(256, D)
        grads = b.cot[s].reshape(256, D)
        lanes = lax.broadcasted_iota(jnp.int32, (256, 128), 1)
        gate = b.rows[s, :, :, D:WIDE].reshape(256, 128).astype(F32)
        gate = jnp.where((lanes == mine) | (lanes == mine + 8), gate, 0.0)
        gate = jnp.sum(gate, axis=1, keepdims=True)
        gate_grad = jnp.zeros((256, 1), F32)
        for part in range(3):
            if part < 2:
                at, width = part * 256, 256
                g = dot(tokens, b.full[:, :, :, at : at + 256].reshape(D, 256))
                u = dot(tokens, b.full[:, :, :, at + 512 : at + 768].reshape(D, 256))
                a = dot(grads, b.full[:, :, :, at + 1024 : at + 1280].reshape(D, 256))
                first, second, scale = at, at + 512, gate
            else:
                at, width = 512, 128
                gu = dot(tokens, b.nat[:, 1152:1408])
                g, u = gu[:, 0:128], gu[:, 128:256]
                a = dot(grads, b.nat[:, 1408:1536])
                first, second, scale = 1024, 1152, None
            g = g.astype(BF16).astype(F32)
            u = u.astype(BF16).astype(F32)
            sg = jax.nn.sigmoid(g)
            act = (g * sg * u).astype(BF16)
            if scale is not None:
                gate_grad = gate_grad + jnp.sum(act.astype(F32) * a, axis=1, keepdims=True)
                act = (act.astype(F32) * scale).astype(BF16)
                a = a * scale
            b.gated[s, :, at : at + width] = act
            b.joint[s, :, first : first + width] = (
                a * u * (sg * (1.0 + g * (1.0 - sg)))
            ).astype(BF16)
            b.joint[s, :, second : second + width] = (a * g * sg).astype(BF16)
        gate_high = gate_grad.astype(BF16).astype(F32)
        spread = jnp.where(lanes == mine, gate_high, 0.0)
        spread = spread + jnp.where(lanes == mine + 8, gate_grad - gate_high, 0.0)
        b.send_x[s, :, :, D:WIDE] = spread.astype(BF16).reshape(2, SEQ, 128)
        for n in range(2):
            rows = slice(n * 768, (n + 1) * 768)
            result = dot_nt(
                b.joint[s, :, 0:1024], b.full[4 * n : 4 * n + 4, :, :, 0:1024].reshape(768, 1024)
            ) + dot_nt(b.joint[s, :, 1024:1280], b.nat[rows, 1152:1408])
            b.send_x[s, :, :, rows] = result.astype(BF16).reshape(2, SEQ, 768)
        back_forward(s, d).start()

        for n in range(2):
            rows = slice(n * 768, (n + 1) * 768)
            result = dot_nt(
                b.gated[s, :, 0:512], b.full[4 * n : 4 * n + 4, :, :, 1024:1536].reshape(768, 512)
            ) + dot_nt(b.gated[s, :, 512:640], b.nat[rows, 1408:1536])
            b.send_y[s, :, :, rows] = result.astype(BF16).reshape(2, SEQ, 768)
        sum_forward(s, d).start()
        back_forward(s, d).wait_recv()
        b.send_x[s, c] = (b.send_x[s, c].astype(F32) + b.pair_x[s].astype(F32)).astype(BF16)

        @pl.when(i > 0)
        def _():
            back_copy(d).start()

    for n in range(4):
        cols = slice(n * 384, (n + 1) * 384)
        tokens = b.rows[:, :, :, cols].reshape(1024, 384)
        for at in (0, 512):
            result = dot_tn(tokens, b.joint[:, :, at : at + 512].reshape(1024, 512))
            b.full[2 * n : 2 * n + 2, :, :, at : at + 512] = result.astype(BF16).reshape(
                2, 2, 96, 512
            )
        result = dot_tn(tokens, b.joint[:, :, 1024:1280].reshape(1024, 256))
        b.nat[cols, 1152:1408] = result.astype(BF16)
        grads = b.cot[:, :, :, cols].reshape(1024, 384)
        result = dot_tn(grads, b.gated[:, :, 0:512].reshape(1024, 512))
        b.full[2 * n : 2 * n + 2, :, :, 1024:1536] = result.astype(BF16).reshape(2, 2, 96, 512)
        result = dot_tn(grads, b.gated[:, :, 512:640].reshape(1024, 128))
        b.nat[cols, 1408:1536] = result.astype(BF16)
    e_give = links.send(b.full.at[:, other], b.got.at[pl.ds(8 * c, 8)], "c", 1)
    e_keep = links.local(b.full.at[:, c], b.got.at[pl.ds(8 * c, 8)])

    @pl.loop(0, 8)
    def _(j):
        to_blocks(j, b.dsh, pl.ds(0, 384), W_ATT)

    half = pl.ds(pl.multiple_of(c * 384, 128), 384)
    s_give = links.send(b.dsh.at[:, other], b.shared.at[:, 0, :, half], "c", 1)
    s_keep = links.local(b.dsh.at[:, c], b.shared.at[:, 0, :, half])
    s_sum = lambda slots, half: b.shared.at[(slots, 0, *half)]
    e_give.wait()
    e_keep.wait()
    e_first = scatter_first(links, e_part, (b.e_got0, b.e_got1), e_cut)
    s_give.wait()
    s_keep.wait()
    s_first = scatter_first(links, s_sum, (b.s_got0, b.s_got1), s_cut)

    for step in NEAR_FIRST:
        back_copy(step).wait()
    moe_back = b.send_x[x, c].astype(F32)
    for step in range(3):
        moe_back = moe_back + b.got_x[step].astype(F32)
    raw = moe_back[:, D:WIDE]
    router_probs = b.probs[...]
    chosen = jnp.zeros((SEQ, 128), F32)
    for k in range(TOP):
        chosen = chosen + (b.ids[:, k : k + 1] == lane).astype(F32)
    prob_grad = chosen * (raw + pltpu.roll(raw, 120, 1))
    logit_grad = router_probs * (
        prob_grad - jnp.sum(router_probs * prob_grad, axis=1, keepdims=True)
    )
    logit_grad = logit_grad.astype(BF16)
    gain_two = dot_nt((lane8 == 8).astype(BF16), b.nat[:, 1024:1152])[0:1]
    moe_in_grad = moe_back[:, 0:D] + dot_nt(logit_grad, b.nat[:, 1024:1152])
    hidden = b.hidden[...]
    inverse_two = lax.rsqrt(jnp.mean(hidden * hidden, axis=1, keepdims=True) + epsilon)
    misc_grad = dot_tn(b.rows[x, c, :, 0:D], logit_grad) + dot_tn(
        (moe_in_grad * hidden * inverse_two).astype(BF16), (lane == 8).astype(BF16)
    )
    b.nat[:, 1024:1152] = misc_grad.astype(BF16)
    scaled = gain_two * moe_in_grad
    hidden_grad = (
        b.out_grad[...].astype(F32)
        + inverse_two * scaled
        - hidden
        * (inverse_two * inverse_two * inverse_two)
        * jnp.mean(scaled * hidden, axis=1, keepdims=True)
    )
    b.tokens_grad[...] = hidden_grad
    b.low[x] = hidden_grad.astype(BF16)
    low_base = links.take(4)
    low_copy = lambda step: links.copy(b.low.at[x], b.low.at[x], "x", step, low_base + step)
    for step in NEAR_FIRST:
        low_copy(step).start()

    norm_base = links.take(4)
    norm_copy = lambda step: links.copy(
        b.send_x.at[lax.rem(x + step, 4), 0, :, pl.ds(0, D)],
        b.got_x.at[step - 1, :, pl.ds(0, D)],
        "x",
        step,
        norm_base + step,
    )
    for d in range(4):
        back_forward(lax.rem(x + d, 4), d).wait_send()

    @pl.loop(0, 4)
    def _(i):
        d = near(i)
        s = lax.rem(x + d, 4)

        @pl.when(i > 0)
        def _():
            low_copy(4 - d).wait_recv()

        mix_grad = dot(b.low[s], b.nat[:, 640:1024]).astype(BF16)
        key, value = b.qkv[s, :, 384:512], b.qkv[s, :, 512:640]
        key_grad = jnp.zeros((SEQ, HD), F32)
        value_grad = jnp.zeros((SEQ, HD), F32)
        for h in range(3):
            head = slice(h * HD, (h + 1) * HD)
            query = b.qkv[s, :, head]
            mixed = mix_grad[:, head]
            probs = causal_probs(query, key)
            dprob = dot_nt(mixed, value)
            value_grad = value_grad + dot_tn(probs.astype(BF16), mixed)
            delta = jnp.sum(probs * dprob, axis=1, keepdims=True)
            score_grad = (probs * (dprob - delta)).astype(BF16)
            b.qkv[s, :, head] = (dot(score_grad, key) * HD**-0.5).astype(BF16)
            key_grad = key_grad + dot_tn(score_grad, query)
        b.qkv[s, :, 384:512] = (key_grad * HD**-0.5).astype(BF16)
        b.qkv[s, :, 512:640] = value_grad.astype(BF16)
        for n in range(2):
            rows = slice(n * 768, (n + 1) * 768)
            b.send_x[s, 0, :, rows] = dot_nt(b.qkv[s], b.nat[rows, 0:640]).astype(BF16)

        @pl.when(i > 0)
        def _():
            norm_copy(d).start()

    for d in range(4):
        s = lax.rem(x + d, 4)
        sum_forward(s, d).wait()
        b.send_y[s, c] = (b.send_y[s, c].astype(F32) + b.pair_y[s].astype(F32)).astype(BF16)
        if d:
            sum_copy(d).start()

    for n in range(4):
        cols = slice(n * 384, (n + 1) * 384)
        result = dot_tn(b.normed[:, :, cols].reshape(512, 384), b.qkv[...].reshape(512, 640))
        b.nat[cols, 0:640] = result.astype(BF16)
        result = dot_tn(b.low[:, :, cols].reshape(512, 384), b.mix[...].reshape(512, 384))
        b.nat[cols, 640:1024] = result.astype(BF16)

    @pl.loop(0, 8)
    def _(j):
        for part in range(3):
            to_blocks(j, b.dense, pl.ds(part * 384, 384), part * 384)

    d_give = links.send(b.dense.at[:, other], b.dgot, "c", 1)
    e_next = scatter_second(
        links, e_first, e_part, (b.e_got0, b.e_got1), (b.e_last0, b.e_last1), e_cut
    )
    d_give.wait()

    @pl.loop(0, 16)
    def _(block):
        b.dense[block, c] = (b.dense[block, c].astype(F32) + b.dgot[block].astype(F32)).astype(BF16)

    d_first = scatter_first(links, d_part, (b.d_got0, b.d_got1), d_cut)
    s_next = scatter_second(
        links, s_first, s_sum, (b.s_got0, b.s_got1), (b.s_last0, b.s_last1), s_cut
    )

    for step in NEAR_FIRST:
        norm_copy(step).wait()
    scaled = b.send_x[x, 0, :, 0:D].astype(F32)
    for step in range(3):
        scaled = scaled + b.got_x[step, :, 0:D].astype(F32)
    inputs = b.tokens[...].astype(F32)
    inverse_one = lax.rsqrt(jnp.mean(inputs * inputs, axis=1, keepdims=True) + epsilon)
    b.tokens_grad[...] = (
        b.tokens_grad[...]
        + inverse_one * scaled
        - inputs
        * (inverse_one * inverse_one * inverse_one)
        * jnp.mean(scaled * inputs, axis=1, keepdims=True)
    )
    for step in NEAR_FIRST:
        sum_copy(step).wait()
    result = b.hidden[...] + b.send_y[x, c].astype(F32)
    for step in range(3):
        result = result + b.got_y[step].astype(F32)
    b.block_out[...] = result.astype(BF16)

    received(e_next)
    for part in range(2):
        rows = slice(48 * part, 48 * part + 48)
        total = scatter_end(links, (b.e_got0, b.e_got1), (b.e_last0, b.e_last1), part)
        b.g_ein[rows] = total[:, 0:1024]
        b.g_eout[rows] = total[:, 1024:1536]
    received(s_next)
    for part in range(2):
        total = scatter_end(links, (b.s_got0, b.s_got1), (b.s_last0, b.s_last1), part)
        b.back[:, W_ATT + 384 * part : W_ATT + 384 * part + 384] = total.astype(BF16)
    d_next = scatter_second(
        links, d_first, d_part, (b.d_got0, b.d_got1), (b.d_last0, b.d_last1), d_cut
    )
    received(d_next)
    for part, cols in ((0, slice(0, 640)), (1, slice(640, 1152))):
        total = scatter_end(links, (b.d_got0, b.d_got1), (b.d_last0, b.d_last1), part)
        b.back[:, cols] = total.astype(BF16)
    pick = pick_matrix((64, 48), lambda row: jnp.where(row % 16 < ROWS, row // 16 * ROWS + row % 16, -1))
    for col in range(0, W_ALL, 384):
        b.pack[:, :, col : col + 384] = moved(pick, b.back[:, col : col + 384]).reshape(4, 16, 384)
    exchange = [
        links.send(b.pack.at[lax.rem(x + step, 4)], b.arrived.at[x], "x", step)
        for step in FAR_FIRST
    ]
    b.arrived[x] = b.pack[x]

    sent(normed_sends + e_first + s_first + d_first)
    for step in NEAR_FIRST:
        rows_copy(step).wait_send()
        cot_copy(step).wait_send()
        low_copy(step).wait_send()
    for d in range(4):
        forward_rows(lax.rem(x + d, 4), d).wait_send()
        if d:
            forward_cot(lax.rem(x + d, 4), d).wait_send()
    sent(e_next + s_next + d_next)
    received(exchange)
    gain_grad = jnp.zeros((ROWS, 1), F32)
    misc = jnp.zeros((ROWS, 128), F32)
    for k in range(4):
        piece = b.arrived[k].astype(F32)[0:ROWS]
        for start, width, at in ((k * 384, 384, 0), (D + k * 128, 128, 384), (2048 + k * 128, 128, 512)):
            raw = piece[:, at : at + width]
            gain_grad = gain_grad + jnp.sum(
                raw * b.w_qkv[:, start : start + width].astype(F32), axis=1, keepdims=True
            )
            b.g_qkv[:, start : start + width] = raw * gain_one
        b.g_out[:, k * 384 : k * 384 + 384] = piece[:, 640:1024]
        misc = misc + piece[:, 1024:1152]
        for core in range(2):
            at, unit = W_ATT + 384 * core, (2 * k + core) * 128
            b.g_sin[:, unit : unit + 128] = piece[:, at : at + 128]
            b.g_sin[:, SH + unit : SH + unit + 128] = piece[:, at + 128 : at + 256]
            b.g_sout[:, unit : unit + 128] = piece[:, at + 256 : at + 384]
    b.g_misc[...] = misc
    b.g_gain[...] = jnp.broadcast_to(gain_grad, (ROWS, 128))
    sent(exchange)


def local(
    tokens,
    expert_ids,
    attn_gain,
    w_qkv,
    w_out,
    moe_gain,
    w_router,
    w_shared_in,
    w_shared_out,
    w_expert_in,
    w_expert_out,
    out_grad,
):
    results = pl.pallas_call(
        kernel,
        out_shape=[jax.ShapeDtypeStruct(shape, dtype) for shape, dtype in OUTS.values()],
        in_specs=[pl.BlockSpec(memory_space=pltpu.VMEM)] * len(INS),
        out_specs=[pl.BlockSpec(memory_space=pltpu.VMEM)] * len(OUTS),
        scratch_shapes=[
            *[pltpu.VMEM(shape, dtype) for shape, dtype in SCRATCH.values()],
            pltpu.SemaphoreType.DMA((SEMS,)),
            pltpu.SemaphoreType.DMA((SEMS,)),
        ],
        compiler_params=pltpu.CompilerParams(
            collective_id=1, has_side_effects=True, vmem_limit_bytes=(64 << 20) - (1 << 16)
        ),
        cost_estimate=pl.CostEstimate(
            flops=23_000_000_000, bytes_accessed=10_000_000, transcendentals=2_000_000
        ),
        name="block",
    )(
        tokens,
        expert_ids,
        attn_gain[:, None],
        w_qkv,
        w_out,
        w_router,
        moe_gain[:, None],
        w_shared_in,
        w_shared_out,
        w_expert_in,
        w_expert_out,
        out_grad,
    )
    block_out, tokens_grad, gain, qkv, out, misc, sin, sout, ein, eout = results
    return (
        block_out,
        tokens_grad,
        gain[:, 0],
        qkv,
        out,
        misc[:, 8],
        misc[:, 0:EXPERTS],
        sin,
        sout,
        ein,
        eout,
    )


def solution(mesh):
    wide, flat = P("fsdp", None), P("fsdp")
    return jax.shard_map(
        local,
        mesh=mesh,
        in_specs=(wide, wide, flat, wide, wide, flat, wide, wide, wide, wide, wide, wide),
        out_specs=(wide, wide, flat, wide, wide, flat, wide, wide, wide, wide, wide),
        check_vma=False,
    )
```

```python
import jax
import jax.numpy as jnp
from jax import lax
from jax.experimental import pallas as pl
from jax.experimental.pallas import tpu as pltpu
from jax.sharding import PartitionSpec as P

D = 1536
HD = 128
SH = 1024
EXPERTS = 8
TOP = 6
ROWS = 12
SEQ = 128
W_ATT = 1152
W_SHARED = 768
W_ALL = W_ATT + W_SHARED
WIDE = D + 128
epsilon = 1e-05
MESH = pl.DeviceIdType.MESH
F32 = jnp.float32
BF16 = jnp.bfloat16
STRIDE = {"x": (32, 4), "z": (8, 4), "y": (2, 4), "c": (1, 2)}
FAR_FIRST = (2, 1, 3)
NEAR_FIRST = (1, 3, 2)


def place(me, axis):
    stride, size = STRIDE[axis]
    return lax.rem(lax.div(me, stride), size)


def peer(me, axis, step):
    stride, size = STRIDE[axis]
    here = place(me, axis)
    return me + (lax.rem(here + step, size) - here) * stride


class Links:
    def __init__(self, send_sem, recv_sem):
        self.me = lax.axis_index("fsdp")
        self.send_sem, self.recv_sem = send_sem, recv_sem
        self.count = 0
        self.x, self.y, self.z, self.c = (place(self.me, axis) for axis in "xyzc")

    def take(self, number):
        first = self.count
        self.count += number
        return first

    def copy(self, src, dst, axis, step, sem):
        return pltpu.make_async_remote_copy(
            src_ref=src,
            dst_ref=dst,
            send_sem=self.send_sem.at[sem],
            recv_sem=self.recv_sem.at[sem],
            device_id=(peer(self.me, axis, step),),
            device_id_type=MESH,
        )

    def send(self, src, dst, axis, step):
        copy = self.copy(src, dst, axis, step, self.take(1))
        copy.start()
        return copy

    def local(self, src, dst):
        copy = pltpu.make_async_copy(src, dst, self.send_sem.at[self.take(1)])
        copy.start()
        return copy

    def greet(self, axes):
        barrier = pltpu.get_barrier_semaphore()
        total = 0
        for axis in axes:
            for step in range(1, STRIDE[axis][1]):
                pl.semaphore_signal(
                    barrier, inc=1, device_id=(peer(self.me, axis, step),), device_id_type=MESH
                )
                total += 1
        return lambda: pl.semaphore_wait(barrier, total)


def finish(copies):
    for copy in copies:
        copy.wait()


def received(copies):
    for copy in copies:
        copy.wait_recv()


def sent(copies):
    for copy in copies:
        copy.wait_send()


def dot(a, b):
    return jnp.dot(a, b, preferred_element_type=F32)


def dot_nt(a, b):
    return lax.dot_general(a, b, (((1,), (1,)), ((), ())), preferred_element_type=F32)


def dot_tn(a, b):
    return lax.dot_general(a, b, (((0,), (0,)), ((), ())), preferred_element_type=F32)


def pick_matrix(shape, source):
    row = lax.broadcasted_iota(jnp.int32, shape, 0)
    col = lax.broadcasted_iota(jnp.int32, shape, 1)
    return (col == source(row)).astype(BF16)


def moved(pick, rows):
    return dot(pick, rows).astype(BF16)


def gather_first(links, own, part, here, cut):
    first = []
    for axis, half in (("y", cut[0]), ("z", cut[1])):
        for step in FAR_FIRST:
            first.append(links.send(own.at[half], part(here, half), axis, step))
    return first


def gather_second(links, first, part, cut):
    received(first[:3])
    second = []
    for step in FAR_FIRST:
        piece = part(pl.ds(links.z * 4, 4), cut[0])
        second.append(links.send(piece, piece, "z", step))
    received(first[3:])
    for step in FAR_FIRST:
        for z in range(4):
            piece = part(z * 4 + links.y, cut[1])
            second.append(links.send(piece, piece, "y", step))
    return second


class PlaneRing:
    def __init__(self, links, first, part, cut):
        self.links, self.part, self.cut = links, part, cut
        received(first)
        self.near, self.far = {}, []
        for step, order in ((1, (0, 1)), (3, (1, 0))):
            for h in order:
                piece = part(pl.ds(links.z * 4 + 2 * h, 2), cut[0])
                self.near["z", step, h] = links.send(piece, piece, "z", step)
        for step, order in ((1, (0, 1, 2, 3)), (3, (2, 3, 0, 1))):
            for z in order:
                piece = part(z * 4 + links.y, cut[1])
                self.near["y", step, z] = links.send(piece, piece, "y", step)

    def pass_on(self):
        links, part, cut = self.links, self.part, self.cut
        for step, h in ((1, 0), (3, 1)):
            self.near["z", step, h].wait_recv()
            piece = part(pl.ds(lax.rem(links.z + 4 - step, 4) * 4 + 2 * h, 2), cut[0])
            self.far.append(links.send(piece, piece, "z", step))
        for step, z in ((1, 0), (1, 1), (3, 2), (3, 3)):
            self.near["y", step, z].wait_recv()
            piece = part(z * 4 + lax.rem(links.y + 4 - step, 4), cut[1])
            self.far.append(links.send(piece, piece, "y", step))

    def arrive(self):
        passed = (("z", 1, 0), ("z", 3, 1), ("y", 1, 0), ("y", 1, 1), ("y", 3, 2), ("y", 3, 3))
        for key, copy in self.near.items():
            if key not in passed:
                copy.wait_recv()
        received(self.far)
        sent(self.near.values())
        sent(self.far)


class RowRing:
    def __init__(self, links, part):
        self.links, self.part = links, part
        self.first = links.take(4)

    def near(self, step):
        piece = self.part(self.links.x, pl.ds(0, SEQ))
        return self.links.copy(piece, piece, "x", step, self.first + step)

    def far(self, h):
        step = 3 if h else 1
        piece = self.part(lax.rem(self.links.x + 4 - step, 4), pl.ds(64 * h, 64))
        return self.links.copy(piece, piece, "x", step, self.first + 2 * h)


def scatter_first(links, part, got, cut):
    first = []
    for step in FAR_FIRST:
        to = lax.rem(links.z + step, 4) * 4
        first.append(links.send(part(pl.ds(to, 4), cut[0]), got[0].at[step - 1], "z", step))
    for step in FAR_FIRST:
        to = lax.rem(links.y + step, 4)
        for z in range(4):
            first.append(
                links.send(part(z * 4 + to, cut[1]), got[1].at[step - 1, z], "y", step)
            )
    return first


def scatter_second(links, first, part, got, last, cut):
    second = []
    for half, axis in ((0, "y"), (1, "z")):
        received(first[3:] if half else first[:3])
        here = links.z if half else links.y

        @pl.loop(0, 4)
        def _(k):
            slot = k * 4 + links.y if half else links.z * 4 + k
            total = part(slot, cut[half])[...].astype(F32)
            for step in range(3):
                total = total + got[half][step, k].astype(F32)
            got[half][0, k] = total.astype(BF16)

        for step in FAR_FIRST:
            second.append(
                links.send(
                    got[half].at[0, lax.rem(here + step, 4)], last[half].at[step - 1], axis, step
                )
            )
    return second


def scatter_end(links, got, last, half):
    here = links.z if half else links.y
    total = got[half][0, here].astype(F32)
    for step in range(3):
        total = total + last[half][step].astype(F32)
    return total


INS = (
    "tokens",
    "ids",
    "gain_one",
    "w_qkv",
    "w_out",
    "w_router",
    "gain_two",
    "w_sin",
    "w_sout",
    "e_in",
    "e_out",
    "out_grad",
)
OUTS = {
    "block_out": ((SEQ, D), BF16),
    "tokens_grad": ((SEQ, D), F32),
    "g_gain_one": ((1, ROWS), F32),
    "g_qkv": ((ROWS, 2560), F32),
    "g_out": ((ROWS, D), F32),
    "g_gain_two": ((1, ROWS), F32),
    "g_router": ((EXPERTS, ROWS), F32),
    "g_sin": ((ROWS, 2 * SH), F32),
    "g_sout": ((ROWS, SH), F32),
    "g_ein": ((96, 1024), F32),
    "g_eout": ((96, 512), F32),
}
SCRATCH = {
    "small": ((128, 128), F32),
    "pack": ((4, 16, W_ALL), BF16),
    "arrived": ((4, 16, W_ALL), BF16),
    "dense": ((16, 2, 48, W_ATT), BF16),
    "shared": ((16, 2, 48, W_SHARED), BF16),
    "got": ((16, 96, D), BF16),
    "full": ((8, 2, 96, D), BF16),
    "nat": ((D, D), BF16),
    "normed": ((4, SEQ, D), BF16),
    "qkv": ((4, SEQ, 640), BF16),
    "mix": ((4, SEQ, 384), BF16),
    "send_y": ((4, 2, SEQ, D), BF16),
    "send_x": ((4, 2, SEQ, WIDE), BF16),
    "pair_y": ((4, SEQ, D), BF16),
    "pair_x": ((4, SEQ, WIDE), BF16),
    "got_y": ((3, SEQ, D), BF16),
    "got_x": ((3, SEQ, WIDE), BF16),
    "hidden": ((SEQ, D), F32),
    "probs": ((SEQ, 128), F32),
    "chosen": ((SEQ, 128), F32),
    "rows": ((4, 2, SEQ, WIDE), BF16),
    "cot": ((4, 2, SEQ, D), BF16),
    "gated": ((4, 256, 640), BF16),
    "joint": ((4, 256, 1280), BF16),
    "low": ((4, SEQ, D), BF16),
    "dsh": ((16, 2, 48, 384), BF16),
    "back": ((48, W_ALL), BF16),
    "e_got0": ((3, 4, 48, D), BF16),
    "e_got1": ((3, 4, 48, D), BF16),
    "e_last0": ((3, 48, D), BF16),
    "e_last1": ((3, 48, D), BF16),
    "d_got0": ((3, 4, 48, 640), BF16),
    "d_got1": ((3, 4, 48, 512), BF16),
    "d_last0": ((3, 48, 640), BF16),
    "d_last1": ((3, 48, 512), BF16),
    "s_got0": ((3, 4, 48, 384), BF16),
    "s_got1": ((3, 4, 48, 384), BF16),
    "s_last0": ((3, 48, 384), BF16),
    "s_last1": ((3, 48, 384), BF16),
}
SEMS = 320


class Bag:
    pass


def near(i):
    return jnp.where(i == 2, 3, jnp.where(i == 3, 2, i))


def far(i):
    return jnp.where(i == 0, 2, jnp.where(i == 3, 0, jnp.where(i == 2, 3, 1)))


def causal_probs(q, k):
    scores = dot_nt(q, k) * HD**-0.5
    row = lax.broadcasted_iota(jnp.int32, (SEQ, SEQ), 0)
    col = lax.broadcasted_iota(jnp.int32, (SEQ, SEQ), 1)
    scores = jnp.where(col <= row, scores, -1e30)
    exponent = jnp.exp(scores - jnp.max(scores, axis=1, keepdims=True))
    return exponent / jnp.sum(exponent, axis=1, keepdims=True)


def kernel(*refs):
    b = Bag()
    names = [*INS, *OUTS, *SCRATCH]
    for name, ref in zip(names, refs):
        setattr(b, name, ref)
    links = Links(*refs[len(names) :])
    x, y, z, c = links.x, links.y, links.z, links.c
    other = 1 - c
    here = z * 4 + y
    mine = 2 * x + c
    every = pl.ds(0, 48)
    e_cut = ((pl.ds(0, 48),), (pl.ds(48, 48),))
    d_cut = ((every, pl.ds(0, 640)), (every, pl.ds(640, 512)))
    s_cut = ((every, pl.ds(0, 384)), (every, pl.ds(384, 384)))
    d_part = lambda slots, half: b.dense.at[(slots, c, *half)]
    s_part = lambda slots, half: b.shared.at[(slots, c, *half)]
    e_part = lambda slots, half: b.got.at[(slots, *half)]

    greeted = links.greet("xyzc")
    b.got[here, :, 0:1024] = b.e_in[...]
    b.got[here, :, 1024:1536] = b.e_out[...]
    b.pack[...] = jnp.zeros_like(b.pack)
    b.small[...] = jnp.zeros_like(b.small)
    b.small[0:EXPERTS, 0:ROWS] = b.w_router[...].astype(F32)
    b.small[8:9, 0:ROWS] = b.gain_two[...].astype(F32)
    b.small[9:10, 0:ROWS] = b.gain_one[...].astype(F32)
    small = b.small[...].T
    lane = lax.broadcasted_iota(jnp.int32, (SEQ, 128), 1)
    row = lax.broadcasted_iota(jnp.int32, (SEQ, 128), 0)
    named = jnp.zeros((SEQ, 128), F32)
    for k in range(TOP):
        named = named + (b.ids[k : k + 1, :] == row).astype(F32)
    b.chosen[...] = named.T
    gain_one = small[0:ROWS, 9:10]
    for k in range(4):
        for start, width, at in ((k * 384, 384, 0), (D + k * 128, 128, 384), (2048 + k * 128, 128, 512)):
            b.pack[k, 0:ROWS, at : at + width] = (
                b.w_qkv[:, start : start + width].astype(F32) * gain_one
            ).astype(BF16)
        b.pack[k, 0:ROWS, 640:1024] = b.w_out[:, k * 384 : k * 384 + 384]
        b.pack[k, 0:ROWS, 1024:1152] = small[0:ROWS].astype(BF16)
        for core in range(2):
            at, unit = W_ATT + 384 * core, (2 * k + core) * 128
            b.pack[k, 0:ROWS, at : at + 128] = b.w_sin[:, unit : unit + 128]
            b.pack[k, 0:ROWS, at + 128 : at + 256] = b.w_sin[:, SH + unit : SH + unit + 128]
            b.pack[k, 0:ROWS, at + 256 : at + 384] = b.w_sout[:, unit : unit + 128]
    greeted()
    exchange = [
        links.send(b.pack.at[lax.rem(x + step, 4)], b.arrived.at[x], "x", step)
        for step in FAR_FIRST
    ]
    e_first = gather_first(links, b.got.at[here], e_part, here, e_cut)
    inputs = b.tokens[...].astype(F32)
    inverse_one = lax.rsqrt(jnp.mean(inputs * inputs, axis=1, keepdims=True) + epsilon)
    b.normed[x] = (inputs * inverse_one).astype(BF16)
    b.cot[x, c] = b.out_grad[...]
    cot_pair = links.send(b.cot.at[x, c], b.cot.at[x, c], "c", 1)
    b.arrived[x] = b.pack[x]
    finish(exchange)
    normed_sends = [
        links.send(b.normed.at[x], b.normed.at[x], "x", step) for step in FAR_FIRST
    ]
    pick = pick_matrix((48, 64), lambda row: row // ROWS * 16 + row % ROWS)
    for col in range(0, W_ALL, 384):
        block = moved(pick, b.arrived[:, :, col : col + 384].reshape(64, 384))
        if col < W_ATT:
            b.dense[here, c, :, col : col + 384] = block
        else:
            b.shared[here, c, :, col - W_ATT : col - W_ATT + 384] = block

    d_first = gather_first(links, b.dense.at[here, c], d_part, here, d_cut)
    d_second = gather_second(links, d_first, d_part, d_cut)
    s_first = gather_first(links, b.shared.at[here, c], s_part, here, s_cut)
    received(d_second)
    sent(d_first + d_second)
    d_pair = links.send(b.dense.at[:, c], b.dense.at[:, c], "c", 1)
    d_pair.wait()
    e_ring = PlaneRing(links, e_first, e_part, e_cut)
    s_ring = PlaneRing(links, s_first, s_part, s_cut)
    received(normed_sends)
    cot_ring = RowRing(links, lambda s, rows: b.cot.at[s, c, rows])
    for step in (1, 3):
        cot_ring.near(step).start()

    order = pick_matrix(
        (192, 192), lambda row: row % 48 // ROWS * 48 + row // 48 * ROWS + row % ROWS
    )

    def to_rows(j, source, start, at):
        piece = source[pl.ds(2 * j, 2), :, :, start].reshape(192, 384)
        piece = moved(order, piece)
        for k in range(4):
            row = pl.multiple_of(k * 384 + j * 48, 16)
            b.nat[pl.ds(row, 48), at : at + 384] = piece[k * 48 : k * 48 + 48]

    def to_blocks(j, target, start, at):
        pieces = [
            b.nat[pl.ds(pl.multiple_of(k * 384 + j * 48, 16), 48), at : at + 384] for k in range(4)
        ]
        piece = moved(order, jnp.concatenate(pieces, axis=0))
        target[pl.ds(2 * j, 2), :, :, start] = piece.reshape(2, 2, 48, 384)

    @pl.loop(0, 8)
    def _(j):
        for part in range(3):
            to_rows(j, b.dense, pl.ds(part * 384, 384), part * 384)

    for at, width in ((0, 256), (256, 256), (512, 128)):
        result = dot(b.normed[...].reshape(512, D), b.nat[:, at : at + width])
        b.qkv[:, :, at : at + width] = result.astype(BF16).reshape(4, SEQ, width)
    mix_base = links.take(4)

    def mix_copy(step):
        return links.copy(
            b.send_y.at[lax.rem(x + step, 4), 0], b.got_y.at[step - 1], "x", step, mix_base + step
        )

    @pl.loop(0, 4)
    def _(i):
        step = far(i)
        s = lax.rem(x + step, 4)
        key, value = b.qkv[s, :, 384:512], b.qkv[s, :, 512:640]
        for h in range(3):
            head = slice(h * HD, (h + 1) * HD)
            probs = causal_probs(b.qkv[s, :, head], key)
            b.mix[s, :, head] = dot(probs.astype(BF16), value).astype(BF16)
        for n in range(2):
            rows = slice(n * 768, (n + 1) * 768)
            b.send_y[s, 0, :, rows] = dot_nt(b.mix[s], b.nat[rows, 640:1024]).astype(BF16)

        @pl.when(i < 3)
        def _():
            mix_copy(step).start()

    e_ring.pass_on()
    s_ring.pass_on()
    e_ring.arrive()
    sent(e_first + s_first)
    e_pair = links.send(b.got.at[pl.ds(8 * other, 8)], b.full.at[:, c], "c", 1)
    e_own = links.local(b.got.at[pl.ds(8 * c, 8)], b.full.at[:, c])

    for step in FAR_FIRST:
        mix_copy(step).wait()
    hidden = b.tokens[...].astype(F32) + b.send_y[x, 0].astype(F32)
    for step in range(3):
        hidden = hidden + b.got_y[step].astype(F32)
    b.hidden[...] = hidden
    inverse_two = lax.rsqrt(jnp.mean(hidden * hidden, axis=1, keepdims=True) + epsilon)
    lane8 = lax.broadcasted_iota(jnp.int32, (8, 128), 1)
    gain_two = dot_nt((lane8 == 8).astype(BF16), b.nat[:, 1024:1152])[0:1]
    moe_in = (hidden * inverse_two * gain_two).astype(BF16)
    b.rows[x, c, :, 0:D] = moe_in
    logits = jnp.where(lane < EXPERTS, dot(moe_in, b.nat[:, 1024:1152]), -1e30)
    exponent = jnp.exp(logits - jnp.max(logits, axis=1, keepdims=True))
    router_probs = exponent / jnp.sum(exponent, axis=1, keepdims=True)
    b.probs[...] = router_probs
    gates = b.chosen[...] * router_probs
    high = gates.astype(BF16).astype(F32)
    b.rows[x, c, :, D:WIDE] = (high + pltpu.roll(gates - high, 8, 1)).astype(BF16)
    rows_ring = RowRing(links, lambda s, rows: b.rows.at[s, c, rows])
    for step in (1, 3):
        rows_ring.near(step).start()
    pair_rows = links.take(4)
    pair_cot = links.take(4)
    forward_rows = lambda s, d: links.copy(
        b.rows.at[s, c], b.rows.at[s, c], "c", 1, pair_rows + d
    )
    forward_cot = lambda s, d: links.copy(b.cot.at[s, c], b.cot.at[s, c], "c", 1, pair_cot + d)
    forward_rows(x, 0).start()
    s_ring.arrive()
    half = pl.ds(pl.multiple_of(other * 384, 128), 384)
    s_pair = links.send(b.shared.at[:, c, :, half], b.shared.at[:, c, :, half], "c", 1)
    s_pair.wait()
    e_pair.wait()
    e_own.wait()

    @pl.loop(0, 8)
    def _(j):
        to_rows(j, b.shared, pl.ds(pl.multiple_of(c * 384, 128), 384), W_ATT)

    back_pair = links.take(8)
    back_base = links.take(8)
    sum_pair = links.take(4)
    sum_base = links.take(4)
    parts = (pl.ds(0, 768), pl.ds(768, WIDE - 768))
    back_forward = lambda s, d, n: links.copy(
        b.send_x.at[s, other, :, parts[n]], b.pair_x.at[s, :, parts[n]], "c", 1, back_pair + 2 * d + n
    )
    sum_forward = lambda s, d: links.copy(
        b.send_y.at[s, other], b.pair_y.at[s], "c", 1, sum_pair + d
    )
    back_copy = lambda step, n: links.copy(
        b.send_x.at[lax.rem(x + step, 4), c, :, parts[n]],
        b.got_x.at[step - 1, :, parts[n]],
        "x",
        step,
        back_base + 2 * step + n,
    )
    sum_copy = lambda step: links.copy(
        b.send_y.at[lax.rem(x + step, 4), c], b.got_y.at[step - 1], "x", step, sum_base + step
    )
    cot_pair.wait()

    def forward(d):
        s = lax.rem(x + d, 4)
        for ring in (rows_ring, cot_ring):
            if d == 2:
                ring.far(0).wait_recv()
                ring.far(1).wait_recv()
            else:
                ring.near(4 - d).wait_recv()
                ring.far(0 if d == 3 else 1).start()
        forward_rows(s, d).start()
        forward_cot(s, d).start()

    @pl.loop(0, 4)
    def _(i):
        d = near(i)
        s = lax.rem(x + d, 4)

        @pl.when(i == 1)
        def _():
            forward(1)
            forward(3)

        @pl.when(i == 3)
        def _():
            forward(2)

        @pl.when(i > 0)
        def _():
            forward_cot(s, d).wait_recv()

        forward_rows(s, d).wait_recv()
        tokens = b.rows[s, :, :, 0:D].reshape(256, D)
        grads = b.cot[s].reshape(256, D)
        lanes = lax.broadcasted_iota(jnp.int32, (256, 128), 1)
        gate = b.rows[s, :, :, D:WIDE].reshape(256, 128).astype(F32)
        gate = jnp.where((lanes == mine) | (lanes == mine + 8), gate, 0.0)
        gate = jnp.sum(gate, axis=1, keepdims=True)
        gate_grad = jnp.zeros((256, 1), F32)
        for part in range(3):
            if part < 2:
                at, width = part * 256, 256
                g = dot(tokens, b.full[:, :, :, at : at + 256].reshape(D, 256))
                u = dot(tokens, b.full[:, :, :, at + 512 : at + 768].reshape(D, 256))
                a = dot(grads, b.full[:, :, :, at + 1024 : at + 1280].reshape(D, 256))
                first, second, scale = at, at + 512, gate
            else:
                at, width = 512, 128
                gu = dot(tokens, b.nat[:, 1152:1408])
                g, u = gu[:, 0:128], gu[:, 128:256]
                a = dot(grads, b.nat[:, 1408:1536])
                first, second, scale = 1024, 1152, None
            g = g.astype(BF16).astype(F32)
            u = u.astype(BF16).astype(F32)
            sg = jax.nn.sigmoid(g)
            act = (g * sg * u).astype(BF16)
            if scale is not None:
                gate_grad = gate_grad + jnp.sum(act.astype(F32) * a, axis=1, keepdims=True)
                act = (act.astype(F32) * scale).astype(BF16)
                a = a * scale
            b.gated[s, :, at : at + width] = act
            b.joint[s, :, first : first + width] = (
                a * u * (sg * (1.0 + g * (1.0 - sg)))
            ).astype(BF16)
            b.joint[s, :, second : second + width] = (a * g * sg).astype(BF16)
        gate_high = gate_grad.astype(BF16).astype(F32)
        spread = jnp.where(lanes == mine, gate_high, 0.0)
        spread = spread + jnp.where(lanes == mine + 8, gate_grad - gate_high, 0.0)
        b.send_x[s, :, :, D:WIDE] = spread.astype(BF16).reshape(2, SEQ, 128)
        for n in range(2):
            rows = slice(n * 768, (n + 1) * 768)
            result = dot_nt(
                b.joint[s, :, 0:1024], b.full[4 * n : 4 * n + 4, :, :, 0:1024].reshape(768, 1024)
            ) + dot_nt(b.joint[s, :, 1024:1280], b.nat[rows, 1152:1408])
            b.send_x[s, :, :, rows] = result.astype(BF16).reshape(2, SEQ, 768)
            back_forward(s, d, n).start()
        for n in range(2):
            back_forward(s, d, n).wait_recv()
            b.send_x[s, c, :, parts[n]] = (
                b.send_x[s, c, :, parts[n]].astype(F32) + b.pair_x[s, :, parts[n]].astype(F32)
            ).astype(BF16)

            @pl.when(i > 0)
            def _():
                back_copy(d, n).start()

    e_got, e_last = (b.e_got0, b.e_got1), (b.e_last0, b.e_last1)
    e_z = links.take(4)
    e_y = links.take(16)
    e_z_copy = lambda step: links.copy(
        b.got.at[pl.ds(lax.rem(z + step, 4) * 4, 4), pl.ds(0, 48)],
        b.e_got0.at[step - 1],
        "z",
        step,
        e_z + step,
    )
    e_y_copy = lambda step, to: links.copy(
        b.got.at[to * 4 + lax.rem(y + step, 4), pl.ds(48, 48)],
        b.e_got1.at[step - 1, to],
        "y",
        step,
        e_y + 4 * step + to,
    )
    e_moves = []
    for low in range(2):
        for n in (2 * low, 2 * low + 1):
            cols = slice(n * 384, (n + 1) * 384)
            tokens = b.rows[:, :, :, cols].reshape(1024, 384)
            for at in (0, 512):
                result = dot_tn(tokens, b.joint[:, :, at : at + 512].reshape(1024, 512))
                b.full[2 * n : 2 * n + 2, :, :, at : at + 512] = result.astype(BF16).reshape(
                    2, 2, 96, 512
                )
            grads = b.cot[:, :, :, cols].reshape(1024, 384)
            result = dot_tn(grads, b.gated[:, :, 0:512].reshape(1024, 512))
            result = result.astype(BF16).reshape(2, 2, 2, 48, 512)
            for h in range(2):
                b.dense[8 * h + 2 * n : 8 * h + 2 * n + 2, :, :, 0:512] = result[:, :, h]
        four = pl.ds(4 * low, 4)
        target = pl.ds(8 * c + 4 * low, 4)
        wide, slim = pl.ds(0, 1024), pl.ds(1024, 512)
        moves = [
            links.send(b.full.at[four, other, :, wide], b.got.at[target, :, wide], "c", 1),
            links.local(b.full.at[four, c, :, wide], b.got.at[target, :, wide]),
        ]
        for h in range(2):
            rows, slots = pl.ds(48 * h, 48), pl.ds(8 * h + 4 * low, 4)
            moves += [
                links.send(
                    b.dense.at[slots, other, :, pl.ds(0, 512)], b.got.at[target, rows, slim], "c", 1
                ),
                links.local(b.dense.at[slots, c, :, pl.ds(0, 512)], b.got.at[target, rows, slim]),
            ]
        e_moves.append(moves)

    def e_start(low):
        finish(e_moves[low])
        for step in FAR_FIRST:

            @pl.when(lax.rem(z + step, 2) == low)
            def _():
                e_z_copy(step).start()

            for to in (low, low + 2):
                e_y_copy(step, to).start()

    e_start(0)

    for step in NEAR_FIRST:
        back_copy(step, 0).wait()
        back_copy(step, 1).wait()
    moe_back = b.send_x[x, c].astype(F32)
    for step in range(3):
        moe_back = moe_back + b.got_x[step].astype(F32)
    raw = moe_back[:, D:WIDE]
    router_probs = b.probs[...]
    prob_grad = b.chosen[...] * (raw + pltpu.roll(raw, 120, 1))
    logit_grad = router_probs * (
        prob_grad - jnp.sum(router_probs * prob_grad, axis=1, keepdims=True)
    )
    logit_grad = logit_grad.astype(BF16)
    gain_two = dot_nt((lane8 == 8).astype(BF16), b.nat[:, 1024:1152])[0:1]
    moe_in_grad = moe_back[:, 0:D] + dot_nt(logit_grad, b.nat[:, 1024:1152])
    hidden = b.hidden[...]
    inverse_two = lax.rsqrt(jnp.mean(hidden * hidden, axis=1, keepdims=True) + epsilon)
    scaled = gain_two * moe_in_grad
    hidden_grad = (
        b.out_grad[...].astype(F32)
        + inverse_two * scaled
        - hidden
        * (inverse_two * inverse_two * inverse_two)
        * jnp.mean(scaled * hidden, axis=1, keepdims=True)
    )
    b.tokens_grad[...] = hidden_grad
    b.low[x] = hidden_grad.astype(BF16)
    low_ring = RowRing(links, lambda s, rows: b.low.at[s, rows])
    for step in (1, 3):
        low_ring.near(step).start()
    e_start(1)
    misc_grad = dot_tn(b.rows[x, c, :, 0:D], logit_grad) + dot_tn(
        (moe_in_grad * hidden * inverse_two).astype(BF16), (lane == 8).astype(BF16)
    )
    b.nat[:, 1024:1152] = misc_grad.astype(BF16)

    @pl.loop(0, 4)
    def _(d):
        s = lax.rem(x + d, 4)
        for n in range(2):
            rows = slice(n * 768, (n + 1) * 768)
            result = dot_nt(
                b.gated[s, :, 0:512], b.full[4 * n : 4 * n + 4, :, :, 1024:1536].reshape(768, 512)
            ) + dot_nt(b.gated[s, :, 512:640], b.nat[rows, 1408:1536])
            b.send_y[s, :, :, rows] = result.astype(BF16).reshape(2, SEQ, 768)
        sum_forward(s, d).start()

    for n in range(4):
        cols = slice(n * 384, (n + 1) * 384)
        tokens = b.rows[:, :, :, cols].reshape(1024, 384)
        result = dot_tn(tokens, b.joint[:, :, 1024:1280].reshape(1024, 256))
        b.nat[cols, 1152:1408] = result.astype(BF16)
        grads = b.cot[:, :, :, cols].reshape(1024, 384)
        result = dot_tn(grads, b.gated[:, :, 512:640].reshape(1024, 128))
        b.nat[cols, 1408:1536] = result.astype(BF16)

    @pl.loop(0, 8)
    def _(j):
        to_blocks(j, b.dsh, pl.ds(0, 384), W_ATT)

    half = pl.ds(pl.multiple_of(c * 384, 128), 384)
    for k in range(2):
        cot_ring.near(2 * k + 1).wait_send()
        cot_ring.far(k).wait_send()
    for d in range(1, 4):
        forward_cot(lax.rem(x + d, 4), d).wait_send()
    s_give = links.send(b.dsh.at[:, other], b.shared.at[:, 0, :, half], "c", 1)
    s_keep = links.local(b.dsh.at[:, c], b.shared.at[:, 0, :, half])
    s_sum = lambda slots, half: b.shared.at[(slots, 0, *half)]
    s_give.wait()
    s_keep.wait()
    s_first = scatter_first(links, s_sum, (b.s_got0, b.s_got1), s_cut)

    low_ring.near(1).wait_recv()
    low_ring.far(0).start()
    low_ring.near(3).wait_recv()
    low_ring.far(1).start()
    norm_base = links.take(4)
    norm_copy = lambda step: links.copy(
        b.send_x.at[lax.rem(x + step, 4), 0, :, pl.ds(0, D)],
        b.got_x.at[step - 1, :, pl.ds(0, D)],
        "x",
        step,
        norm_base + step,
    )
    for d in range(4):
        for n in range(2):
            back_forward(lax.rem(x + d, 4), d, n).wait_send()

    @pl.loop(0, 4)
    def _(i):
        d = near(i)
        s = lax.rem(x + d, 4)

        @pl.when(i == 3)
        def _():
            low_ring.far(0).wait_recv()
            low_ring.far(1).wait_recv()

        mix_grad = dot(b.low[s], b.nat[:, 640:1024]).astype(BF16)
        key, value = b.qkv[s, :, 384:512], b.qkv[s, :, 512:640]
        key_grad = jnp.zeros((SEQ, HD), F32)
        value_grad = jnp.zeros((SEQ, HD), F32)
        for h in range(3):
            head = slice(h * HD, (h + 1) * HD)
            query = b.qkv[s, :, head]
            mixed = mix_grad[:, head]
            probs = causal_probs(query, key)
            dprob = dot_nt(mixed, value)
            value_grad = value_grad + dot_tn(probs.astype(BF16), mixed)
            delta = jnp.sum(probs * dprob, axis=1, keepdims=True)
            score_grad = (probs * (dprob - delta)).astype(BF16)
            b.qkv[s, :, head] = (dot(score_grad, key) * HD**-0.5).astype(BF16)
            key_grad = key_grad + dot_tn(score_grad, query)
        b.qkv[s, :, 384:512] = (key_grad * HD**-0.5).astype(BF16)
        b.qkv[s, :, 512:640] = value_grad.astype(BF16)
        for n in range(2):
            rows = slice(n * 768, (n + 1) * 768)
            b.send_x[s, 0, :, rows] = dot_nt(b.qkv[s], b.nat[rows, 0:640]).astype(BF16)

        @pl.when(i > 0)
        def _():
            norm_copy(d).start()

    for d in range(4):
        s = lax.rem(x + d, 4)
        sum_forward(s, d).wait()
        b.send_y[s, c] = (b.send_y[s, c].astype(F32) + b.pair_y[s].astype(F32)).astype(BF16)
        if d:
            sum_copy(d).start()

    e_first = [e_z_copy(step) for step in FAR_FIRST]
    e_first += [e_y_copy(step, to) for step in FAR_FIRST for to in range(4)]
    e_next = scatter_second(links, e_first, e_part, e_got, e_last, e_cut)

    d_base = links.take(8)

    def d_landing(j):
        rows = pl.ds(pl.multiple_of(lax.div(j, 4) * 48, 16), 48)
        return b.cot.at[lax.rem(j, 4), :, rows, pl.ds(0, W_ATT)]

    d_give = lambda j: links.copy(
        b.dense.at[pl.ds(2 * j, 2), other], d_landing(j), "c", 1, d_base + j
    )

    for n in range(4):
        cols = slice(n * 384, (n + 1) * 384)
        result = dot_tn(b.normed[:, :, cols].reshape(512, 384), b.qkv[...].reshape(512, 640))
        b.nat[cols, 0:640] = result.astype(BF16)
        result = dot_tn(b.low[:, :, cols].reshape(512, 384), b.mix[...].reshape(512, 384))
        b.nat[cols, 640:1024] = result.astype(BF16)

    @pl.loop(0, 8)
    def _(j):
        for part in range(3):
            to_blocks(j, b.dense, pl.ds(part * 384, 384), part * 384)
        d_give(j).start()

    @pl.loop(0, 8)
    def _(j):
        d_give(j).wait()
        total = b.dense[pl.ds(2 * j, 2), c].astype(F32) + d_landing(j)[...].astype(F32)
        b.dense[pl.ds(2 * j, 2), c] = total.astype(BF16)

    d_first = scatter_first(links, d_part, (b.d_got0, b.d_got1), d_cut)
    s_next = scatter_second(
        links, s_first, s_sum, (b.s_got0, b.s_got1), (b.s_last0, b.s_last1), s_cut
    )

    for step in NEAR_FIRST:
        norm_copy(step).wait()
    scaled = b.send_x[x, 0, :, 0:D].astype(F32)
    for step in range(3):
        scaled = scaled + b.got_x[step, :, 0:D].astype(F32)
    inputs = b.tokens[...].astype(F32)
    inverse_one = lax.rsqrt(jnp.mean(inputs * inputs, axis=1, keepdims=True) + epsilon)
    b.tokens_grad[...] = (
        b.tokens_grad[...]
        + inverse_one * scaled
        - inputs
        * (inverse_one * inverse_one * inverse_one)
        * jnp.mean(scaled * inputs, axis=1, keepdims=True)
    )
    for step in NEAR_FIRST:
        sum_copy(step).wait()
    result = b.hidden[...] + b.send_y[x, c].astype(F32)
    for step in range(3):
        result = result + b.got_y[step].astype(F32)
    b.block_out[...] = result.astype(BF16)

    received(e_next)
    for part in range(2):
        rows = slice(48 * part, 48 * part + 48)
        total = scatter_end(links, e_got, e_last, part)
        b.g_ein[rows] = total[:, 0:1024]
        b.g_eout[rows] = total[:, 1024:1536]
    received(s_next)
    for part in range(2):
        total = scatter_end(links, (b.s_got0, b.s_got1), (b.s_last0, b.s_last1), part)
        b.back[:, W_ATT + 384 * part : W_ATT + 384 * part + 384] = total.astype(BF16)
    d_next = scatter_second(
        links, d_first, d_part, (b.d_got0, b.d_got1), (b.d_last0, b.d_last1), d_cut
    )
    received(d_next)
    for part, cols in ((0, slice(0, 640)), (1, slice(640, 1152))):
        total = scatter_end(links, (b.d_got0, b.d_got1), (b.d_last0, b.d_last1), part)
        b.back[:, cols] = total.astype(BF16)
    pick = pick_matrix((64, 48), lambda row: jnp.where(row % 16 < ROWS, row // 16 * ROWS + row % 16, -1))
    for col in range(0, W_ALL, 384):
        b.pack[:, :, col : col + 384] = moved(pick, b.back[:, col : col + 384]).reshape(4, 16, 384)
    exchange = [
        links.send(b.pack.at[lax.rem(x + step, 4)], b.arrived.at[x], "x", step)
        for step in FAR_FIRST
    ]
    b.arrived[x] = b.pack[x]

    sent(normed_sends + e_first + s_first + d_first)
    for ring in (rows_ring, low_ring):
        for step in (1, 3):
            ring.near(step).wait_send()
        for h in range(2):
            ring.far(h).wait_send()
    for d in range(4):
        forward_rows(lax.rem(x + d, 4), d).wait_send()
    sent(e_next + s_next + d_next)
    received(exchange)
    gain_grad = jnp.zeros((ROWS, 1), F32)
    misc = jnp.zeros((ROWS, 128), F32)
    for k in range(4):
        piece = b.arrived[k].astype(F32)[0:ROWS]
        for start, width, at in ((k * 384, 384, 0), (D + k * 128, 128, 384), (2048 + k * 128, 128, 512)):
            raw = piece[:, at : at + width]
            gain_grad = gain_grad + jnp.sum(
                raw * b.w_qkv[:, start : start + width].astype(F32), axis=1, keepdims=True
            )
            b.g_qkv[:, start : start + width] = raw * gain_one
        b.g_out[:, k * 384 : k * 384 + 384] = piece[:, 640:1024]
        misc = misc + piece[:, 1024:1152]
        for core in range(2):
            at, unit = W_ATT + 384 * core, (2 * k + core) * 128
            b.g_sin[:, unit : unit + 128] = piece[:, at : at + 128]
            b.g_sin[:, SH + unit : SH + unit + 128] = piece[:, at + 128 : at + 256]
            b.g_sout[:, unit : unit + 128] = piece[:, at + 256 : at + 384]
    b.small[0:ROWS] = jnp.where(lane[0:ROWS] == 9, gain_grad, misc)
    small = b.small[...].T
    b.g_router[...] = small[0:EXPERTS, 0:ROWS]
    b.g_gain_two[...] = small[8:9, 0:ROWS]
    b.g_gain_one[...] = small[9:10, 0:ROWS]
    sent(exchange)


def hand_over(*refs):
    n = len(OUTS)
    for source, target in zip(refs[:n], refs[n:]):
        target[...] = source[...]


def local(
    tokens,
    expert_ids,
    attn_gain,
    w_qkv,
    w_out,
    moe_gain,
    w_router,
    w_shared_in,
    w_shared_out,
    w_expert_in,
    w_expert_out,
    out_grad,
):
    results = pl.pallas_call(
        kernel,
        out_shape=[jax.ShapeDtypeStruct(shape, dtype) for shape, dtype in OUTS.values()],
        in_specs=[pl.BlockSpec(memory_space=pltpu.VMEM)] * len(INS),
        out_specs=[pl.BlockSpec(memory_space=pltpu.VMEM)] * len(OUTS),
        scratch_shapes=[
            *[pltpu.VMEM(shape, dtype) for shape, dtype in SCRATCH.values()],
            pltpu.SemaphoreType.DMA((SEMS,)),
            pltpu.SemaphoreType.DMA((SEMS,)),
        ],
        compiler_params=pltpu.CompilerParams(
            collective_id=1, has_side_effects=True, vmem_limit_bytes=(64 << 20) - (1 << 16)
        ),
        cost_estimate=pl.CostEstimate(
            flops=23_000_000_000, bytes_accessed=10_000_000, transcendentals=2_000_000
        ),
        name="block",
    )(
        tokens,
        expert_ids.T,
        attn_gain[None],
        w_qkv,
        w_out,
        w_router.T,
        moe_gain[None],
        w_shared_in,
        w_shared_out,
        w_expert_in,
        w_expert_out,
        out_grad,
    )
    results = pl.pallas_call(
        hand_over,
        out_shape=[jax.ShapeDtypeStruct(shape, dtype) for shape, dtype in OUTS.values()],
        in_specs=[pl.BlockSpec(memory_space=pltpu.VMEM)] * len(OUTS),
        out_specs=[pl.BlockSpec(memory_space=pltpu.VMEM)] * len(OUTS),
        name="hand_over",
    )(*results)
    block_out, tokens_grad, gain_one, qkv, out, gain_two, router, sin, sout, ein, eout = results
    return (
        block_out,
        tokens_grad,
        gain_one[0],
        qkv,
        out,
        gain_two[0],
        router.T,
        sin,
        sout,
        ein,
        eout,
    )


def solution(mesh):
    wide, flat = P("fsdp", None), P("fsdp")
    return jax.shard_map(
        local,
        mesh=mesh,
        in_specs=(wide, wide, flat, wide, wide, flat, wide, wide, wide, wide, wide, wide),
        out_specs=(wide, wide, flat, wide, wide, flat, wide, wide, wide, wide, wide),
        check_vma=False,
    )
```

```python
import jax
import jax.numpy as jnp
from jax import lax
from jax.experimental import pallas as pl
from jax.experimental.pallas import tpu as pltpu
from jax.sharding import PartitionSpec as P

D = 1536
HD = 128
SH = 1024
EXPERTS = 8
TOP = 6
ROWS = 12
SEQ = 128
W_ATT = 1152
W_SHARED = 768
W_ALL = W_ATT + W_SHARED
WIDE = D + 128
epsilon = 1e-05
MESH = pl.DeviceIdType.MESH
F32 = jnp.float32
BF16 = jnp.bfloat16
STRIDE = {"x": (32, 4), "z": (8, 4), "y": (2, 4), "c": (1, 2)}
FAR_FIRST = (2, 1, 3)
NEAR_FIRST = (1, 3, 2)


def place(me, axis):
    stride, size = STRIDE[axis]
    return lax.rem(lax.div(me, stride), size)


def peer(me, axis, step):
    stride, size = STRIDE[axis]
    here = place(me, axis)
    return me + (lax.rem(here + step, size) - here) * stride


class Links:
    def __init__(self, send_sem, recv_sem):
        self.me = lax.axis_index("fsdp")
        self.send_sem, self.recv_sem = send_sem, recv_sem
        self.count = 0
        self.x, self.y, self.z, self.c = (place(self.me, axis) for axis in "xyzc")

    def take(self, number):
        first = self.count
        self.count += number
        return first

    def copy(self, src, dst, axis, step, sem):
        return pltpu.make_async_remote_copy(
            src_ref=src,
            dst_ref=dst,
            send_sem=self.send_sem.at[sem],
            recv_sem=self.recv_sem.at[sem],
            device_id=(peer(self.me, axis, step),),
            device_id_type=MESH,
        )

    def send(self, src, dst, axis, step):
        copy = self.copy(src, dst, axis, step, self.take(1))
        copy.start()
        return copy

    def local(self, src, dst):
        copy = pltpu.make_async_copy(src, dst, self.send_sem.at[self.take(1)])
        copy.start()
        return copy

    def greet(self, axes):
        barrier = pltpu.get_barrier_semaphore()
        total = 0
        for axis in axes:
            for step in range(1, STRIDE[axis][1]):
                pl.semaphore_signal(
                    barrier, inc=1, device_id=(peer(self.me, axis, step),), device_id_type=MESH
                )
                total += 1
        return lambda: pl.semaphore_wait(barrier, total)


def finish(copies):
    for copy in copies:
        copy.wait()


def received(copies):
    for copy in copies:
        copy.wait_recv()


def sent(copies):
    for copy in copies:
        copy.wait_send()


def dot(a, b):
    return jnp.dot(a, b, preferred_element_type=F32)


def dot_nt(a, b):
    return lax.dot_general(a, b, (((1,), (1,)), ((), ())), preferred_element_type=F32)


def dot_tn(a, b):
    return lax.dot_general(a, b, (((0,), (0,)), ((), ())), preferred_element_type=F32)


def pick_matrix(shape, source):
    row = lax.broadcasted_iota(jnp.int32, shape, 0)
    col = lax.broadcasted_iota(jnp.int32, shape, 1)
    return (col == source(row)).astype(BF16)


def moved(pick, rows):
    return dot(pick, rows).astype(BF16)


def gather_first(links, own, part, here, cut):
    first = []
    for axis, half in (("y", cut[0]), ("z", cut[1])):
        for step in FAR_FIRST:
            first.append(links.send(own.at[half], part(here, half), axis, step))
    return first


class PlaneRing:
    def __init__(self, links, first, part, cut):
        self.links, self.part, self.cut = links, part, cut
        received(first)
        self.near, self.far = {}, []
        for step, order in ((1, (0, 1)), (3, (1, 0))):
            for h in order:
                piece = part(pl.ds(links.z * 4 + 2 * h, 2), cut[0])
                self.near["z", step, h] = links.send(piece, piece, "z", step)
        for step, order in ((1, (0, 1, 2, 3)), (3, (2, 3, 0, 1))):
            for z in order:
                piece = part(z * 4 + links.y, cut[1])
                self.near["y", step, z] = links.send(piece, piece, "y", step)

    def pass_on(self):
        links, part, cut = self.links, self.part, self.cut
        for step, h in ((1, 0), (3, 1)):
            self.near["z", step, h].wait_recv()
            piece = part(pl.ds(lax.rem(links.z + 4 - step, 4) * 4 + 2 * h, 2), cut[0])
            self.far.append(links.send(piece, piece, "z", step))
        for step, z in ((1, 0), (1, 1), (3, 2), (3, 3)):
            self.near["y", step, z].wait_recv()
            piece = part(z * 4 + lax.rem(links.y + 4 - step, 4), cut[1])
            self.far.append(links.send(piece, piece, "y", step))

    def arrive(self):
        passed = (("z", 1, 0), ("z", 3, 1), ("y", 1, 0), ("y", 1, 1), ("y", 3, 2), ("y", 3, 3))
        for key, copy in self.near.items():
            if key not in passed:
                copy.wait_recv()
        received(self.far)
        sent(self.near.values())
        sent(self.far)


class RowRing:
    def __init__(self, links, part):
        self.links, self.part = links, part
        self.first = links.take(4)

    def near(self, step):
        piece = self.part(self.links.x, pl.ds(0, SEQ))
        return self.links.copy(piece, piece, "x", step, self.first + step)

    def start(self):
        self.near(1).start()
        self.near(3).start()

    def pass_on(self):
        for step, h in ((1, 0), (3, 1)):
            self.near(step).wait_recv()
            self.far(h).start()

    def arrive(self):
        self.far(0).wait_recv()
        self.far(1).wait_recv()

    def sent(self):
        for k in range(2):
            self.near(2 * k + 1).wait_send()
            self.far(k).wait_send()

    def far(self, h):
        step = 3 if h else 1
        piece = self.part(lax.rem(self.links.x + 4 - step, 4), pl.ds(64 * h, 64))
        return self.links.copy(piece, piece, "x", step, self.first + 2 * h)


class SumRing:
    def __init__(self, links, part, got):
        self.links, self.part, self.got = links, part, got
        self.first = links.take(6)

    def block(self, step):
        return lax.rem(self.links.x + step, 4)

    def far(self, h):
        rows = pl.ds(64 * h, 64)
        return self.links.copy(
            self.part(self.block(2), rows), self.got.at[1, rows], "x", 2 * h + 1, self.first + h
        )

    def near(self, step, early):
        h = 1 if (step == 1) == early else 0
        rows = pl.ds(64 * h, 64)
        return self.links.copy(
            self.part(self.block(step), rows),
            self.got.at[step - 1, rows],
            "x",
            step,
            self.first + 2 + (step - 1) + (0 if early else 1),
        )

    def start_far(self):
        self.far(0).start()
        self.far(1).start()

    def pass_on(self):
        for h, step in ((0, 1), (1, 3)):
            self.far(h).wait_recv()
            rows = pl.ds(64 * h, 64)
            target = self.part(self.block(step), rows)
            target[...] = (
                target[...].astype(F32) + self.got[1, rows].astype(F32)
            ).astype(BF16)
            self.near(step, False).start()

    def total(self, own):
        for step in (1, 3):
            for early in (True, False):
                self.near(step, early).wait()
        self.far(0).wait_send()
        self.far(1).wait_send()
        return own + self.got[0].astype(F32) + self.got[2].astype(F32)


def scatter_first(links, part, got, cut):
    first = []
    for step in FAR_FIRST:
        to = lax.rem(links.z + step, 4) * 4
        first.append(links.send(part(pl.ds(to, 4), cut[0]), got[0].at[step - 1], "z", step))
    for step in FAR_FIRST:
        to = lax.rem(links.y + step, 4)
        for z in range(4):
            first.append(
                links.send(part(z * 4 + to, cut[1]), got[1].at[step - 1, z], "y", step)
            )
    return first


def scatter_second(links, first, part, got, last, cut):
    second = []
    for half, axis in ((0, "y"), (1, "z")):
        received(first[3:] if half else first[:3])
        here = links.z if half else links.y

        @pl.loop(0, 4)
        def _(k):
            slot = k * 4 + links.y if half else links.z * 4 + k
            total = part(slot, cut[half])[...].astype(F32)
            for step in range(3):
                total = total + got[half][step, k].astype(F32)
            got[half][0, k] = total.astype(BF16)

        for step in FAR_FIRST:
            second.append(
                links.send(
                    got[half].at[0, lax.rem(here + step, 4)], last[half].at[step - 1], axis, step
                )
            )
    return second


def scatter_end(links, got, last, half):
    here = links.z if half else links.y
    total = got[half][0, here].astype(F32)
    for step in range(3):
        total = total + last[half][step].astype(F32)
    return total


INS = (
    "tokens",
    "ids",
    "gain_one",
    "w_qkv",
    "w_out",
    "w_router",
    "gain_two",
    "w_sin",
    "w_sout",
    "e_in",
    "e_out",
    "out_grad",
)
OUTS = {
    "block_out": ((SEQ, D), BF16),
    "tokens_grad": ((SEQ, D), F32),
    "g_gain_one": ((1, ROWS), F32),
    "g_qkv": ((ROWS, 2560), F32),
    "g_out": ((ROWS, D), F32),
    "g_gain_two": ((1, ROWS), F32),
    "g_router": ((EXPERTS, ROWS), F32),
    "g_sin": ((ROWS, 2 * SH), F32),
    "g_sout": ((ROWS, SH), F32),
    "g_ein": ((96, 1024), F32),
    "g_eout": ((96, 512), F32),
}
SCRATCH = {
    "small": ((128, 128), F32),
    "pack": ((4, 16, W_ALL), BF16),
    "arrived": ((4, 16, W_ALL), BF16),
    "dense": ((16, 2, 48, W_ATT), BF16),
    "shared": ((16, 2, 48, W_SHARED), BF16),
    "got": ((16, 96, D), BF16),
    "full": ((8, 2, 96, D), BF16),
    "nat": ((D, D), BF16),
    "normed": ((4, SEQ, D), BF16),
    "qkv": ((4, SEQ, 640), BF16),
    "mix": ((4, SEQ, 384), BF16),
    "send_y": ((4, 2, SEQ, D), BF16),
    "send_x": ((4, 2, SEQ, WIDE), BF16),
    "pair_y": ((4, SEQ, D), BF16),
    "pair_x": ((4, SEQ, WIDE), BF16),
    "got_y": ((3, SEQ, D), BF16),
    "got_x": ((3, SEQ, WIDE), BF16),
    "hidden": ((SEQ, D), F32),
    "probs": ((SEQ, 128), F32),
    "chosen": ((SEQ, 128), F32),
    "rows": ((4, 2, SEQ, WIDE), BF16),
    "cot": ((4, 2, SEQ, D), BF16),
    "gated": ((4, 256, 640), BF16),
    "joint": ((4, 256, 1280), BF16),
    "low": ((4, SEQ, D), BF16),
    "dsh": ((16, 2, 48, 384), BF16),
    "back": ((48, W_ALL), BF16),
    "e_got0": ((3, 4, 48, D), BF16),
    "e_got1": ((3, 4, 48, D), BF16),
    "e_last0": ((3, 48, D), BF16),
    "e_last1": ((3, 48, D), BF16),
    "d_got0": ((3, 4, 48, 640), BF16),
    "d_got1": ((3, 4, 48, 512), BF16),
    "d_last0": ((3, 48, 640), BF16),
    "d_last1": ((3, 48, 512), BF16),
    "s_got0": ((3, 4, 48, 384), BF16),
    "s_got1": ((3, 4, 48, 384), BF16),
    "s_last0": ((3, 48, 384), BF16),
    "s_last1": ((3, 48, 384), BF16),
}
SEMS = 320


class Bag:
    pass


def near(i):
    return jnp.where(i == 2, 3, jnp.where(i == 3, 2, i))


def far(i):
    return jnp.where(i == 0, 2, jnp.where(i == 3, 0, jnp.where(i == 2, 3, 1)))


def causal_probs(q, k):
    scores = dot_nt(q, k) * HD**-0.5
    row = lax.broadcasted_iota(jnp.int32, (SEQ, SEQ), 0)
    col = lax.broadcasted_iota(jnp.int32, (SEQ, SEQ), 1)
    scores = jnp.where(col <= row, scores, -1e30)
    exponent = jnp.exp(scores - jnp.max(scores, axis=1, keepdims=True))
    return exponent / jnp.sum(exponent, axis=1, keepdims=True)


def kernel(*refs):
    b = Bag()
    names = [*INS, *OUTS, *SCRATCH]
    for name, ref in zip(names, refs):
        setattr(b, name, ref)
    links = Links(*refs[len(names) :])
    x, y, z, c = links.x, links.y, links.z, links.c
    other = 1 - c
    here = z * 4 + y
    mine = 2 * x + c
    every = pl.ds(0, 48)
    e_cut = ((pl.ds(0, 48),), (pl.ds(48, 48),))
    d_cut = ((every, pl.ds(0, 640)), (every, pl.ds(640, 512)))
    s_cut = ((every, pl.ds(0, 384)), (every, pl.ds(384, 384)))
    d_part = lambda slots, half: b.dense.at[(slots, c, *half)]
    s_part = lambda slots, half: b.shared.at[(slots, c, *half)]
    e_part = lambda slots, half: b.got.at[(slots, *half)]

    greeted = links.greet("xyzc")
    b.got[here, :, 0:1024] = b.e_in[...]
    b.got[here, :, 1024:1536] = b.e_out[...]
    b.pack[...] = jnp.zeros_like(b.pack)
    b.small[...] = jnp.zeros_like(b.small)
    b.small[0:EXPERTS, 0:ROWS] = b.w_router[...].astype(F32)
    b.small[8:9, 0:ROWS] = b.gain_two[...].astype(F32)
    b.small[9:10, 0:ROWS] = b.gain_one[...].astype(F32)
    small = b.small[...].T
    lane = lax.broadcasted_iota(jnp.int32, (SEQ, 128), 1)
    row = lax.broadcasted_iota(jnp.int32, (SEQ, 128), 0)
    named = jnp.zeros((SEQ, 128), F32)
    for k in range(TOP):
        named = named + (b.ids[k : k + 1, :] == row).astype(F32)
    b.chosen[...] = named.T
    gain_one = small[0:ROWS, 9:10]
    for k in range(4):
        for start, width, at in ((k * 384, 384, 0), (D + k * 128, 128, 384), (2048 + k * 128, 128, 512)):
            b.pack[k, 0:ROWS, at : at + width] = (
                b.w_qkv[:, start : start + width].astype(F32) * gain_one
            ).astype(BF16)
        b.pack[k, 0:ROWS, 640:1024] = b.w_out[:, k * 384 : k * 384 + 384]
        b.pack[k, 0:ROWS, 1024:1152] = small[0:ROWS].astype(BF16)
        for core in range(2):
            at, unit = W_ATT + 384 * core, (2 * k + core) * 128
            b.pack[k, 0:ROWS, at : at + 128] = b.w_sin[:, unit : unit + 128]
            b.pack[k, 0:ROWS, at + 128 : at + 256] = b.w_sin[:, SH + unit : SH + unit + 128]
            b.pack[k, 0:ROWS, at + 256 : at + 384] = b.w_sout[:, unit : unit + 128]
    greeted()
    exchange = [
        links.send(b.pack.at[lax.rem(x + step, 4)], b.arrived.at[x], "x", step)
        for step in FAR_FIRST
    ]
    e_first = gather_first(links, b.got.at[here], e_part, here, e_cut)
    inputs = b.tokens[...].astype(F32)
    inverse_one = lax.rsqrt(jnp.mean(inputs * inputs, axis=1, keepdims=True) + epsilon)
    b.normed[x] = (inputs * inverse_one).astype(BF16)
    b.cot[x, c] = b.out_grad[...]
    cot_pair = links.send(b.cot.at[x, c], b.cot.at[x, c], "c", 1)
    b.arrived[x] = b.pack[x]
    finish(exchange)
    normed_ring = RowRing(links, lambda s, rows: b.normed.at[s, rows])
    cot_ring = RowRing(links, lambda s, rows: b.cot.at[s, c, rows])
    normed_ring.start()
    pick = pick_matrix((48, 64), lambda row: row // ROWS * 16 + row % ROWS)
    for col in range(0, W_ALL, 384):
        block = moved(pick, b.arrived[:, :, col : col + 384].reshape(64, 384))
        if col < W_ATT:
            b.dense[here, c, :, col : col + 384] = block
        else:
            b.shared[here, c, :, col - W_ATT : col - W_ATT + 384] = block

    d_first = gather_first(links, b.dense.at[here, c], d_part, here, d_cut)
    d_ring = PlaneRing(links, d_first, d_part, d_cut)
    s_first = gather_first(links, b.shared.at[here, c], s_part, here, s_cut)
    normed_ring.pass_on()
    cot_ring.start()
    d_ring.pass_on()
    d_ring.arrive()
    sent(d_first)
    d_pair = links.take(8)

    def d_forward(j):
        piece = b.dense.at[pl.ds(2 * j, 2), c]
        return links.copy(piece, piece, "c", 1, d_pair + j)

    for j in range(8):
        d_forward(j).start()
    e_ring = PlaneRing(links, e_first, e_part, e_cut)
    s_ring = PlaneRing(links, s_first, s_part, s_cut)
    normed_ring.arrive()

    order = pick_matrix(
        (192, 192), lambda row: row % 48 // ROWS * 48 + row // 48 * ROWS + row % ROWS
    )

    def to_rows(j, source, start, at):
        piece = source[pl.ds(2 * j, 2), :, :, start].reshape(192, 384)
        piece = moved(order, piece)
        for k in range(4):
            row = pl.multiple_of(k * 384 + j * 48, 16)
            b.nat[pl.ds(row, 48), at : at + 384] = piece[k * 48 : k * 48 + 48]

    def to_blocks(j, target, start, at):
        pieces = [
            b.nat[pl.ds(pl.multiple_of(k * 384 + j * 48, 16), 48), at : at + 384] for k in range(4)
        ]
        piece = moved(order, jnp.concatenate(pieces, axis=0))
        target[pl.ds(2 * j, 2), :, :, start] = piece.reshape(2, 2, 48, 384)

    @pl.loop(0, 8)
    def _(j):
        d_forward(j).wait()
        for part in range(3):
            to_rows(j, b.dense, pl.ds(part * 384, 384), part * 384)

    for at, width in ((0, 256), (256, 256), (512, 128)):
        result = dot(b.normed[...].reshape(512, D), b.nat[:, at : at + width])
        b.qkv[:, :, at : at + width] = result.astype(BF16).reshape(4, SEQ, width)
    mix_ring = SumRing(links, lambda s, rows: b.send_y.at[s, 0, rows], b.got_y)

    def attend(s):
        key, value = b.qkv[s, :, 384:512], b.qkv[s, :, 512:640]
        for h in range(3):
            head = slice(h * HD, (h + 1) * HD)
            probs = causal_probs(b.qkv[s, :, head], key)
            b.mix[s, :, head] = dot(probs.astype(BF16), value).astype(BF16)
        for n in range(2):
            rows = slice(n * 768, (n + 1) * 768)
            b.send_y[s, 0, :, rows] = dot_nt(b.mix[s], b.nat[rows, 640:1024]).astype(BF16)

    @pl.loop(0, 4)
    def _(i):
        @pl.when(i == 3)
        def _():
            mix_ring.pass_on()

        attend(lax.rem(x + far(i), 4))

        @pl.when(i == 0)
        def _():
            mix_ring.start_far()

        for k, step in ((1, 1), (2, 3)):

            @pl.when(i == k)
            def _():
                mix_ring.near(step, True).start()

    e_ring.pass_on()
    s_ring.pass_on()
    cot_ring.pass_on()

    hidden = mix_ring.total(b.tokens[...].astype(F32) + b.send_y[x, 0].astype(F32))
    b.hidden[...] = hidden
    inverse_two = lax.rsqrt(jnp.mean(hidden * hidden, axis=1, keepdims=True) + epsilon)
    lane8 = lax.broadcasted_iota(jnp.int32, (8, 128), 1)
    gain_two = dot_nt((lane8 == 8).astype(BF16), b.nat[:, 1024:1152])[0:1]
    moe_in = (hidden * inverse_two * gain_two).astype(BF16)
    b.rows[x, c, :, 0:D] = moe_in
    logits = jnp.where(lane < EXPERTS, dot(moe_in, b.nat[:, 1024:1152]), -1e30)
    exponent = jnp.exp(logits - jnp.max(logits, axis=1, keepdims=True))
    router_probs = exponent / jnp.sum(exponent, axis=1, keepdims=True)
    b.probs[...] = router_probs
    gates = b.chosen[...] * router_probs
    high = gates.astype(BF16).astype(F32)
    b.rows[x, c, :, D:WIDE] = (high + pltpu.roll(gates - high, 8, 1)).astype(BF16)
    rows_ring = RowRing(links, lambda s, rows: b.rows.at[s, c, rows])
    rows_ring.start()
    pair_rows = links.take(4)
    pair_cot = links.take(4)
    forward_rows = lambda s, d: links.copy(
        b.rows.at[s, c], b.rows.at[s, c], "c", 1, pair_rows + d
    )
    forward_cot = lambda s, d: links.copy(b.cot.at[s, c], b.cot.at[s, c], "c", 1, pair_cot + d)
    forward_rows(x, 0).start()
    e_ring.arrive()
    sent(e_first + s_first)
    e_pair = links.send(b.got.at[pl.ds(8 * other, 8)], b.full.at[:, c], "c", 1)
    e_own = links.local(b.got.at[pl.ds(8 * c, 8)], b.full.at[:, c])
    s_ring.arrive()
    half = pl.ds(pl.multiple_of(other * 384, 128), 384)
    s_pair = links.send(b.shared.at[:, c, :, half], b.shared.at[:, c, :, half], "c", 1)

    s_pair.wait()
    e_pair.wait()
    e_own.wait()

    @pl.loop(0, 8)
    def _(j):
        to_rows(j, b.shared, pl.ds(pl.multiple_of(c * 384, 128), 384), W_ATT)

    back_pair = links.take(8)
    back_base = links.take(8)
    sum_pair = links.take(4)
    parts = (pl.ds(0, 768), pl.ds(768, WIDE - 768))
    back_forward = lambda s, d, n: links.copy(
        b.send_x.at[s, other, :, parts[n]], b.pair_x.at[s, :, parts[n]], "c", 1, back_pair + 2 * d + n
    )
    sum_forward = lambda s, d: links.copy(
        b.send_y.at[s, other], b.pair_y.at[s], "c", 1, sum_pair + d
    )
    back_copy = lambda step, n: links.copy(
        b.send_x.at[lax.rem(x + step, 4), c, :, parts[n]],
        b.got_x.at[step - 1, :, parts[n]],
        "x",
        step,
        back_base + 2 * step + n,
    )
    sum_ring = SumRing(links, lambda s, rows: b.send_y.at[s, c, rows], b.got_y)
    cot_pair.wait()

    rows_ring.pass_on()
    for d in (1, 3):
        forward_rows(lax.rem(x + d, 4), d).start()
    cot_ring.arrive()
    for d in range(1, 4):
        forward_cot(lax.rem(x + d, 4), d).start()

    def add_pair(i):
        d = near(i)
        s = lax.rem(x + d, 4)
        for n in range(2):
            back_forward(s, d, n).wait_recv()
            b.send_x[s, c, :, parts[n]] = (
                b.send_x[s, c, :, parts[n]].astype(F32) + b.pair_x[s, :, parts[n]].astype(F32)
            ).astype(BF16)

            @pl.when(i > 0)
            def _():
                back_copy(d, n).start()

    @pl.loop(0, 4)
    def _(i):
        d = near(i)
        s = lax.rem(x + d, 4)

        @pl.when(i > 0)
        def _():
            forward_cot(s, d).wait_recv()

        forward_rows(s, d).wait_recv()
        tokens = b.rows[s, :, :, 0:D].reshape(256, D)
        grads = b.cot[s].reshape(256, D)
        lanes = lax.broadcasted_iota(jnp.int32, (256, 128), 1)
        gate = b.rows[s, :, :, D:WIDE].reshape(256, 128).astype(F32)
        gate = jnp.where((lanes == mine) | (lanes == mine + 8), gate, 0.0)
        gate = jnp.sum(gate, axis=1, keepdims=True)
        gate_grad = jnp.zeros((256, 1), F32)
        for part in range(3):
            if part < 2:
                at, width = part * 256, 256
                g = dot(tokens, b.full[:, :, :, at : at + 256].reshape(D, 256))
                u = dot(tokens, b.full[:, :, :, at + 512 : at + 768].reshape(D, 256))
                a = dot(grads, b.full[:, :, :, at + 1024 : at + 1280].reshape(D, 256))
                first, second, scale = at, at + 512, gate
            else:
                at, width = 512, 128
                gu = dot(tokens, b.nat[:, 1152:1408])
                g, u = gu[:, 0:128], gu[:, 128:256]
                a = dot(grads, b.nat[:, 1408:1536])
                first, second, scale = 1024, 1152, None
            g = g.astype(BF16).astype(F32)
            u = u.astype(BF16).astype(F32)
            sg = jax.nn.sigmoid(g)
            act = (g * sg * u).astype(BF16)
            if scale is not None:
                gate_grad = gate_grad + jnp.sum(act.astype(F32) * a, axis=1, keepdims=True)
                act = (act.astype(F32) * scale).astype(BF16)
                a = a * scale
            b.gated[s, :, at : at + width] = act
            b.joint[s, :, first : first + width] = (
                a * u * (sg * (1.0 + g * (1.0 - sg)))
            ).astype(BF16)
            b.joint[s, :, second : second + width] = (a * g * sg).astype(BF16)
            if part == 0:

                @pl.when(i > 0)
                def _():
                    add_pair(i - 1)

                @pl.when(i == 1)
                def _():
                    rows_ring.arrive()
                    forward_rows(lax.rem(x + 2, 4), 2).start()

        gate_high = gate_grad.astype(BF16).astype(F32)
        spread = jnp.where(lanes == mine, gate_high, 0.0)
        spread = spread + jnp.where(lanes == mine + 8, gate_grad - gate_high, 0.0)
        b.send_x[s, :, :, D:WIDE] = spread.astype(BF16).reshape(2, SEQ, 128)
        for n in range(2):
            rows = slice(n * 768, (n + 1) * 768)
            result = dot_nt(
                b.joint[s, :, 0:1024], b.full[4 * n : 4 * n + 4, :, :, 0:1024].reshape(768, 1024)
            ) + dot_nt(b.joint[s, :, 1024:1280], b.nat[rows, 1152:1408])
            b.send_x[s, :, :, rows] = result.astype(BF16).reshape(2, SEQ, 768)
            back_forward(s, d, n).start()

    add_pair(jnp.int32(3))

    e_got, e_last = (b.e_got0, b.e_got1), (b.e_last0, b.e_last1)
    e_z = links.take(4)
    e_y = links.take(16)
    e_z_copy = lambda step: links.copy(
        b.got.at[pl.ds(lax.rem(z + step, 4) * 4, 4), pl.ds(0, 48)],
        b.e_got0.at[step - 1],
        "z",
        step,
        e_z + step,
    )
    e_y_copy = lambda step, to: links.copy(
        b.got.at[to * 4 + lax.rem(y + step, 4), pl.ds(48, 48)],
        b.e_got1.at[step - 1, to],
        "y",
        step,
        e_y + 4 * step + to,
    )
    e_moves = []
    for low in range(2):
        for n in (2 * low, 2 * low + 1):
            cols = slice(n * 384, (n + 1) * 384)
            tokens = b.rows[:, :, :, cols].reshape(1024, 384)
            for at in (0, 512):
                result = dot_tn(tokens, b.joint[:, :, at : at + 512].reshape(1024, 512))
                b.full[2 * n : 2 * n + 2, :, :, at : at + 512] = result.astype(BF16).reshape(
                    2, 2, 96, 512
                )
            grads = b.cot[:, :, :, cols].reshape(1024, 384)
            result = dot_tn(grads, b.gated[:, :, 0:512].reshape(1024, 512))
            result = result.astype(BF16).reshape(2, 2, 2, 48, 512)
            for h in range(2):
                b.dense[8 * h + 2 * n : 8 * h + 2 * n + 2, :, :, 0:512] = result[:, :, h]
        four = pl.ds(4 * low, 4)
        target = pl.ds(8 * c + 4 * low, 4)
        wide, slim = pl.ds(0, 1024), pl.ds(1024, 512)
        moves = [
            links.send(b.full.at[four, other, :, wide], b.got.at[target, :, wide], "c", 1),
            links.local(b.full.at[four, c, :, wide], b.got.at[target, :, wide]),
        ]
        for h in range(2):
            rows, slots = pl.ds(48 * h, 48), pl.ds(8 * h + 4 * low, 4)
            moves += [
                links.send(
                    b.dense.at[slots, other, :, pl.ds(0, 512)], b.got.at[target, rows, slim], "c", 1
                ),
                links.local(b.dense.at[slots, c, :, pl.ds(0, 512)], b.got.at[target, rows, slim]),
            ]
        e_moves.append(moves)

    def e_start(low):
        finish(e_moves[low])
        for step in FAR_FIRST:

            @pl.when(lax.rem(z + step, 2) == low)
            def _():
                e_z_copy(step).start()

            for to in (low, low + 2):
                e_y_copy(step, to).start()

    e_start(0)
    e_start(1)

    for step in NEAR_FIRST:
        back_copy(step, 0).wait()
        back_copy(step, 1).wait()
    moe_back = b.send_x[x, c].astype(F32)
    for step in range(3):
        moe_back = moe_back + b.got_x[step].astype(F32)
    raw = moe_back[:, D:WIDE]
    router_probs = b.probs[...]
    prob_grad = b.chosen[...] * (raw + pltpu.roll(raw, 120, 1))
    logit_grad = router_probs * (
        prob_grad - jnp.sum(router_probs * prob_grad, axis=1, keepdims=True)
    )
    logit_grad = logit_grad.astype(BF16)
    gain_two = dot_nt((lane8 == 8).astype(BF16), b.nat[:, 1024:1152])[0:1]
    moe_in_grad = moe_back[:, 0:D] + dot_nt(logit_grad, b.nat[:, 1024:1152])
    hidden = b.hidden[...]
    inverse_two = lax.rsqrt(jnp.mean(hidden * hidden, axis=1, keepdims=True) + epsilon)
    scaled = gain_two * moe_in_grad
    hidden_grad = (
        b.out_grad[...].astype(F32)
        + inverse_two * scaled
        - hidden
        * (inverse_two * inverse_two * inverse_two)
        * jnp.mean(scaled * hidden, axis=1, keepdims=True)
    )
    b.tokens_grad[...] = hidden_grad
    b.low[x] = hidden_grad.astype(BF16)
    low_ring = RowRing(links, lambda s, rows: b.low.at[s, rows])
    low_ring.start()
    misc_grad = dot_tn(b.rows[x, c, :, 0:D], logit_grad) + dot_tn(
        (moe_in_grad * hidden * inverse_two).astype(BF16), (lane == 8).astype(BF16)
    )
    b.nat[:, 1024:1152] = misc_grad.astype(BF16)

    @pl.loop(0, 4)
    def _(d):
        s = lax.rem(x + d, 4)
        for n in range(2):
            rows = slice(n * 768, (n + 1) * 768)
            result = dot_nt(
                b.gated[s, :, 0:512], b.full[4 * n : 4 * n + 4, :, :, 1024:1536].reshape(768, 512)
            ) + dot_nt(b.gated[s, :, 512:640], b.nat[rows, 1408:1536])
            b.send_y[s, :, :, rows] = result.astype(BF16).reshape(2, SEQ, 768)
        sum_forward(s, d).start()

    for n in range(4):
        cols = slice(n * 384, (n + 1) * 384)
        tokens = b.rows[:, :, :, cols].reshape(1024, 384)
        result = dot_tn(tokens, b.joint[:, :, 1024:1280].reshape(1024, 256))
        b.nat[cols, 1152:1408] = result.astype(BF16)
        grads = b.cot[:, :, :, cols].reshape(1024, 384)
        result = dot_tn(grads, b.gated[:, :, 512:640].reshape(1024, 128))
        b.nat[cols, 1408:1536] = result.astype(BF16)

    @pl.loop(0, 8)
    def _(j):
        to_blocks(j, b.dsh, pl.ds(0, 384), W_ATT)

    half = pl.ds(pl.multiple_of(c * 384, 128), 384)
    cot_ring.sent()
    for d in range(1, 4):
        forward_cot(lax.rem(x + d, 4), d).wait_send()
    s_give = links.send(b.dsh.at[:, other], b.shared.at[:, 0, :, half], "c", 1)
    s_keep = links.local(b.dsh.at[:, c], b.shared.at[:, 0, :, half])
    s_sum = lambda slots, half: b.shared.at[(slots, 0, *half)]

    s_give.wait()
    s_keep.wait()
    s_first = scatter_first(links, s_sum, (b.s_got0, b.s_got1), s_cut)
    low_ring.pass_on()
    norm_base = links.take(4)
    norm_copy = lambda step: links.copy(
        b.send_x.at[lax.rem(x + step, 4), 0, :, pl.ds(0, D)],
        b.got_x.at[step - 1, :, pl.ds(0, D)],
        "x",
        step,
        norm_base + step,
    )
    for d in range(4):
        for n in range(2):
            back_forward(lax.rem(x + d, 4), d, n).wait_send()

    @pl.loop(0, 4)
    def _(i):
        d = near(i)
        s = lax.rem(x + d, 4)

        @pl.when(i == 3)
        def _():
            low_ring.arrive()

        mix_grad = dot(b.low[s], b.nat[:, 640:1024]).astype(BF16)
        key, value = b.qkv[s, :, 384:512], b.qkv[s, :, 512:640]
        key_grad = jnp.zeros((SEQ, HD), F32)
        value_grad = jnp.zeros((SEQ, HD), F32)
        for h in range(3):
            head = slice(h * HD, (h + 1) * HD)
            query = b.qkv[s, :, head]
            mixed = mix_grad[:, head]
            probs = causal_probs(query, key)
            dprob = dot_nt(mixed, value)
            value_grad = value_grad + dot_tn(probs.astype(BF16), mixed)
            delta = jnp.sum(probs * dprob, axis=1, keepdims=True)
            score_grad = (probs * (dprob - delta)).astype(BF16)
            b.qkv[s, :, head] = (dot(score_grad, key) * HD**-0.5).astype(BF16)
            key_grad = key_grad + dot_tn(score_grad, query)
        b.qkv[s, :, 384:512] = (key_grad * HD**-0.5).astype(BF16)
        b.qkv[s, :, 512:640] = value_grad.astype(BF16)
        for n in range(2):
            rows = slice(n * 768, (n + 1) * 768)
            b.send_x[s, 0, :, rows] = dot_nt(b.qkv[s], b.nat[rows, 0:640]).astype(BF16)

        @pl.when(i > 0)
        def _():
            norm_copy(d).start()

    e_first = [e_z_copy(step) for step in FAR_FIRST]
    e_first += [e_y_copy(step, to) for step in FAR_FIRST for to in range(4)]
    e_next = scatter_second(links, e_first, e_part, e_got, e_last, e_cut)
    d_base = links.take(8)

    def d_landing(j):
        rows = pl.ds(pl.multiple_of(lax.div(j, 4) * 48, 16), 48)
        return b.cot.at[lax.rem(j, 4), :, rows, pl.ds(0, W_ATT)]

    d_give = lambda j: links.copy(
        b.dense.at[pl.ds(2 * j, 2), other], d_landing(j), "c", 1, d_base + j
    )

    for n in range(4):
        cols = slice(n * 384, (n + 1) * 384)
        result = dot_tn(b.normed[:, :, cols].reshape(512, 384), b.qkv[...].reshape(512, 640))
        b.nat[cols, 0:640] = result.astype(BF16)
        result = dot_tn(b.low[:, :, cols].reshape(512, 384), b.mix[...].reshape(512, 384))
        b.nat[cols, 640:1024] = result.astype(BF16)

    @pl.loop(0, 8)
    def _(j):
        for part in range(3):
            to_blocks(j, b.dense, pl.ds(part * 384, 384), part * 384)
        d_give(j).start()

    s_next = scatter_second(
        links, s_first, s_sum, (b.s_got0, b.s_got1), (b.s_last0, b.s_last1), s_cut
    )

    @pl.loop(0, 8)
    def _(j):
        d_give(j).wait()
        total = b.dense[pl.ds(2 * j, 2), c].astype(F32) + d_landing(j)[...].astype(F32)
        b.dense[pl.ds(2 * j, 2), c] = total.astype(BF16)

    d_first = scatter_first(links, d_part, (b.d_got0, b.d_got1), d_cut)

    for d in (2, 1, 3, 0):
        s = lax.rem(x + d, 4)
        sum_forward(s, d).wait()
        b.send_y[s, c] = (b.send_y[s, c].astype(F32) + b.pair_y[s].astype(F32)).astype(BF16)
        if d == 2:
            sum_ring.start_far()
        elif d:
            sum_ring.near(d, True).start()

    for step in NEAR_FIRST:
        norm_copy(step).wait()
    scaled = b.send_x[x, 0, :, 0:D].astype(F32)
    for step in range(3):
        scaled = scaled + b.got_x[step, :, 0:D].astype(F32)
    inputs = b.tokens[...].astype(F32)
    inverse_one = lax.rsqrt(jnp.mean(inputs * inputs, axis=1, keepdims=True) + epsilon)
    b.tokens_grad[...] = (
        b.tokens_grad[...]
        + inverse_one * scaled
        - inputs
        * (inverse_one * inverse_one * inverse_one)
        * jnp.mean(scaled * inputs, axis=1, keepdims=True)
    )

    sum_ring.pass_on()

    d_next = scatter_second(
        links, d_first, d_part, (b.d_got0, b.d_got1), (b.d_last0, b.d_last1), d_cut
    )
    received(s_next)
    for part in range(2):
        total = scatter_end(links, (b.s_got0, b.s_got1), (b.s_last0, b.s_last1), part)
        b.back[:, W_ATT + 384 * part : W_ATT + 384 * part + 384] = total.astype(BF16)
    received(d_next)
    for part, cols in ((0, slice(0, 640)), (1, slice(640, 1152))):
        total = scatter_end(links, (b.d_got0, b.d_got1), (b.d_last0, b.d_last1), part)
        b.back[:, cols] = total.astype(BF16)
    pick = pick_matrix((64, 48), lambda row: jnp.where(row % 16 < ROWS, row // 16 * ROWS + row % 16, -1))
    for col in range(0, W_ALL, 384):
        b.pack[:, :, col : col + 384] = moved(pick, b.back[:, col : col + 384]).reshape(4, 16, 384)
    exchange = [
        links.send(b.pack.at[lax.rem(x + step, 4)], b.arrived.at[x], "x", step)
        for step in FAR_FIRST
    ]
    b.arrived[x] = b.pack[x]
    received(e_next)
    for part in range(2):
        rows = slice(48 * part, 48 * part + 48)
        total = scatter_end(links, e_got, e_last, part)
        b.g_ein[rows] = total[:, 0:1024]
        b.g_eout[rows] = total[:, 1024:1536]
    result = sum_ring.total(b.hidden[...] + b.send_y[x, c].astype(F32))
    b.block_out[...] = result.astype(BF16)

    sent(e_first + s_first + d_first)
    for ring in (normed_ring, rows_ring, low_ring):
        ring.sent()
    for d in range(4):
        forward_rows(lax.rem(x + d, 4), d).wait_send()
    sent(e_next + s_next + d_next)
    received(exchange)
    gain_grad = jnp.zeros((ROWS, 1), F32)
    misc = jnp.zeros((ROWS, 128), F32)
    for k in range(4):
        piece = b.arrived[k].astype(F32)[0:ROWS]
        for start, width, at in ((k * 384, 384, 0), (D + k * 128, 128, 384), (2048 + k * 128, 128, 512)):
            raw = piece[:, at : at + width]
            gain_grad = gain_grad + jnp.sum(
                raw * b.w_qkv[:, start : start + width].astype(F32), axis=1, keepdims=True
            )
            b.g_qkv[:, start : start + width] = raw * gain_one
        b.g_out[:, k * 384 : k * 384 + 384] = piece[:, 640:1024]
        misc = misc + piece[:, 1024:1152]
        for core in range(2):
            at, unit = W_ATT + 384 * core, (2 * k + core) * 128
            b.g_sin[:, unit : unit + 128] = piece[:, at : at + 128]
            b.g_sin[:, SH + unit : SH + unit + 128] = piece[:, at + 128 : at + 256]
            b.g_sout[:, unit : unit + 128] = piece[:, at + 256 : at + 384]
    b.small[0:ROWS] = jnp.where(lane[0:ROWS] == 9, gain_grad, misc)
    small = b.small[...].T
    b.g_router[...] = small[0:EXPERTS, 0:ROWS]
    b.g_gain_two[...] = small[8:9, 0:ROWS]
    b.g_gain_one[...] = small[9:10, 0:ROWS]
    sent(exchange)


def hand_over(*refs):
    n = len(OUTS)
    for source, target in zip(refs[:n], refs[n:]):
        target[...] = source[...]


def local(
    tokens,
    expert_ids,
    attn_gain,
    w_qkv,
    w_out,
    moe_gain,
    w_router,
    w_shared_in,
    w_shared_out,
    w_expert_in,
    w_expert_out,
    out_grad,
):
    results = pl.pallas_call(
        kernel,
        out_shape=[jax.ShapeDtypeStruct(shape, dtype) for shape, dtype in OUTS.values()],
        in_specs=[pl.BlockSpec(memory_space=pltpu.VMEM)] * len(INS),
        out_specs=[pl.BlockSpec(memory_space=pltpu.VMEM)] * len(OUTS),
        scratch_shapes=[
            *[pltpu.VMEM(shape, dtype) for shape, dtype in SCRATCH.values()],
            pltpu.SemaphoreType.DMA((SEMS,)),
            pltpu.SemaphoreType.DMA((SEMS,)),
        ],
        compiler_params=pltpu.CompilerParams(
            collective_id=1, has_side_effects=True, vmem_limit_bytes=(64 << 20) - (1 << 16)
        ),
        cost_estimate=pl.CostEstimate(
            flops=23_000_000_000, bytes_accessed=10_000_000, transcendentals=2_000_000
        ),
        name="block",
    )(
        tokens,
        expert_ids.T,
        attn_gain[None],
        w_qkv,
        w_out,
        w_router.T,
        moe_gain[None],
        w_shared_in,
        w_shared_out,
        w_expert_in,
        w_expert_out,
        out_grad,
    )
    results = pl.pallas_call(
        hand_over,
        out_shape=[jax.ShapeDtypeStruct(shape, dtype) for shape, dtype in OUTS.values()],
        in_specs=[pl.BlockSpec(memory_space=pltpu.VMEM)] * len(OUTS),
        out_specs=[pl.BlockSpec(memory_space=pltpu.VMEM)] * len(OUTS),
        name="hand_over",
    )(*results)
    block_out, tokens_grad, gain_one, qkv, out, gain_two, router, sin, sout, ein, eout = results
    return (
        block_out,
        tokens_grad,
        gain_one[0],
        qkv,
        out,
        gain_two[0],
        router.T,
        sin,
        sout,
        ein,
        eout,
    )


def solution(mesh):
    wide, flat = P("fsdp", None), P("fsdp")
    return jax.shard_map(
        local,
        mesh=mesh,
        in_specs=(wide, wide, flat, wide, wide, flat, wide, wide, wide, wide, wide, wide),
        out_specs=(wide, wide, flat, wide, wide, flat, wide, wide, wide, wide, wide),
        check_vma=False,
    )
```

```python
import jax
import jax.numpy as jnp
from jax import lax
from jax.experimental import pallas as pl
from jax.experimental.pallas import tpu as pltpu
from jax.sharding import PartitionSpec as P

D = 1536
HD = 128
SH = 1024
EXPERTS = 8
TOP = 6
ROWS = 12
SEQ = 128
W_ATT = 1152
W_SHARED = 768
W_ALL = W_ATT + W_SHARED
WIDE = D + 128
epsilon = 1e-05
MESH = pl.DeviceIdType.MESH
F32 = jnp.float32
BF16 = jnp.bfloat16
STRIDE = {"x": (32, 4), "z": (8, 4), "y": (2, 4), "c": (1, 2)}
FAR_FIRST = (2, 1, 3)
NEAR_FIRST = (1, 3, 2)


def place(me, axis):
    stride, size = STRIDE[axis]
    return lax.rem(lax.div(me, stride), size)


def peer(me, axis, step):
    stride, size = STRIDE[axis]
    here = place(me, axis)
    return me + (lax.rem(here + step, size) - here) * stride


class Links:
    def __init__(self, send_sem, recv_sem):
        self.me = lax.axis_index("fsdp")
        self.send_sem, self.recv_sem = send_sem, recv_sem
        self.count = 0
        self.x, self.y, self.z, self.c = (place(self.me, axis) for axis in "xyzc")

    def take(self, number):
        first = self.count
        self.count += number
        return first

    def copy(self, src, dst, axis, step, sem):
        return pltpu.make_async_remote_copy(
            src_ref=src,
            dst_ref=dst,
            send_sem=self.send_sem.at[sem],
            recv_sem=self.recv_sem.at[sem],
            device_id=(peer(self.me, axis, step),),
            device_id_type=MESH,
        )

    def send(self, src, dst, axis, step):
        copy = self.copy(src, dst, axis, step, self.take(1))
        copy.start()
        return copy

    def local(self, src, dst):
        copy = pltpu.make_async_copy(src, dst, self.send_sem.at[self.take(1)])
        copy.start()
        return copy

    def greet(self, axes):
        barrier = pltpu.get_barrier_semaphore()
        total = 0
        for axis in axes:
            for step in range(1, STRIDE[axis][1]):
                pl.semaphore_signal(
                    barrier, inc=1, device_id=(peer(self.me, axis, step),), device_id_type=MESH
                )
                total += 1
        return lambda: pl.semaphore_wait(barrier, total)


def finish(copies):
    for copy in copies:
        copy.wait()


def received(copies):
    for copy in copies:
        copy.wait_recv()


def sent(copies):
    for copy in copies:
        copy.wait_send()


def dot(a, b):
    return jnp.dot(a, b, preferred_element_type=F32)


def dot_nt(a, b):
    return lax.dot_general(a, b, (((1,), (1,)), ((), ())), preferred_element_type=F32)


def dot_tn(a, b):
    return lax.dot_general(a, b, (((0,), (0,)), ((), ())), preferred_element_type=F32)


def pick_matrix(shape, source):
    row = lax.broadcasted_iota(jnp.int32, shape, 0)
    col = lax.broadcasted_iota(jnp.int32, shape, 1)
    return (col == source(row)).astype(BF16)


def moved(pick, rows):
    return dot(pick, rows).astype(BF16)


def gather_first(links, own, part, here, cut):
    first = []
    for axis, half in (("y", cut[0]), ("z", cut[1])):
        for step in FAR_FIRST:
            first.append(links.send(own.at[half], part(here, half), axis, step))
    return first


class PlaneRing:
    def __init__(self, links, first, part, cut):
        self.links, self.part, self.cut = links, part, cut
        received(first)
        self.near, self.far = {}, []
        for step, order in ((1, (0, 1)), (3, (1, 0))):
            for h in order:
                piece = part(pl.ds(links.z * 4 + 2 * h, 2), cut[0])
                self.near["z", step, h] = links.send(piece, piece, "z", step)
        for step, order in ((1, (0, 1, 2, 3)), (3, (2, 3, 0, 1))):
            for z in order:
                piece = part(z * 4 + links.y, cut[1])
                self.near["y", step, z] = links.send(piece, piece, "y", step)

    def pass_on(self):
        links, part, cut = self.links, self.part, self.cut
        for step, h in ((1, 0), (3, 1)):
            self.near["z", step, h].wait_recv()
            piece = part(pl.ds(lax.rem(links.z + 4 - step, 4) * 4 + 2 * h, 2), cut[0])
            self.far.append(links.send(piece, piece, "z", step))
        for step, z in ((1, 0), (1, 1), (3, 2), (3, 3)):
            self.near["y", step, z].wait_recv()
            piece = part(z * 4 + lax.rem(links.y + 4 - step, 4), cut[1])
            self.far.append(links.send(piece, piece, "y", step))

    def arrive_near(self):
        passed = (("z", 1, 0), ("z", 3, 1), ("y", 1, 0), ("y", 1, 1), ("y", 3, 2), ("y", 3, 3))
        for key, copy in self.near.items():
            if key not in passed:
                copy.wait_recv()

    def arrive(self):
        received(self.far)
        sent(self.near.values())
        sent(self.far)


class RowRing:
    def __init__(self, links, part):
        self.links, self.part = links, part
        self.first = links.take(4)

    def near(self, step):
        piece = self.part(self.links.x, pl.ds(0, SEQ))
        return self.links.copy(piece, piece, "x", step, self.first + step)

    def start(self):
        self.near(1).start()
        self.near(3).start()

    def pass_on(self):
        for step, h in ((1, 0), (3, 1)):
            self.near(step).wait_recv()
            self.far(h).start()

    def arrive(self):
        self.far(0).wait_recv()
        self.far(1).wait_recv()

    def sent(self):
        for k in range(2):
            self.near(2 * k + 1).wait_send()
            self.far(k).wait_send()

    def far(self, h):
        step = 3 if h else 1
        piece = self.part(lax.rem(self.links.x + 4 - step, 4), pl.ds(64 * h, 64))
        return self.links.copy(piece, piece, "x", step, self.first + 2 * h)


class SumRing:
    def __init__(self, links, part, got):
        self.links, self.part, self.got = links, part, got
        self.first = links.take(6)

    def block(self, step):
        return lax.rem(self.links.x + step, 4)

    def far(self, h):
        rows = pl.ds(64 * h, 64)
        return self.links.copy(
            self.part(self.block(2), rows), self.got.at[1, rows], "x", 2 * h + 1, self.first + h
        )

    def near(self, step, early):
        h = 1 if (step == 1) == early else 0
        rows = pl.ds(64 * h, 64)
        return self.links.copy(
            self.part(self.block(step), rows),
            self.got.at[step - 1, rows],
            "x",
            step,
            self.first + 2 + (step - 1) + (0 if early else 1),
        )

    def start_far(self):
        self.far(0).start()
        self.far(1).start()

    def pass_on(self):
        for h, step in ((0, 1), (1, 3)):
            self.far(h).wait_recv()
            rows = pl.ds(64 * h, 64)
            target = self.part(self.block(step), rows)
            target[...] = (
                target[...].astype(F32) + self.got[1, rows].astype(F32)
            ).astype(BF16)
            self.near(step, False).start()

    def total(self, own):
        for step in (1, 3):
            for early in (True, False):
                self.near(step, early).wait()
        self.far(0).wait_send()
        self.far(1).wait_send()
        return own + self.got[0].astype(F32) + self.got[2].astype(F32)


class PlaneSum:
    def __init__(self, links, full, got):
        self.links, self.full, self.got = links, full, got
        self.first = links.take(24)

    def z_copy(self, step, q, far):
        at = lax.rem(self.links.z + (2 if far else step), 4) * 4 + 2 * q
        return self.links.copy(
            self.full.at[pl.ds(at, 2), pl.ds(0, 48)],
            self.got[0].at[1 if far else step - 1, pl.ds(2 * q, 2)],
            "z",
            step,
            self.first + 2 * (0 if far else step) + q,
        )

    def y_copy(self, step, z, far):
        at = z * 4 + lax.rem(self.links.y + (2 if far else step), 4)
        return self.links.copy(
            self.full.at[at, pl.ds(48, 48)],
            self.got[1].at[1 if far else step - 1, z],
            "y",
            step,
            self.first + 8 + 4 * (0 if far else step) + z,
        )

    def start(self, low):
        for z in (low, low + 2):
            through = 1 if z < 2 else 3
            self.y_copy(through, z, True).start()
            self.y_copy(4 - through, z, False).start()

        @pl.when(lax.rem(self.links.z, 2) == low)
        def _():
            self.z_copy(1, 0, True).start()
            self.z_copy(3, 1, True).start()

        @pl.when(lax.rem(self.links.z, 2) != low)
        def _():
            self.z_copy(1, 1, False).start()
            self.z_copy(3, 0, False).start()

    def pass_on(self):
        for q, step in ((0, 1), (1, 3)):
            self.z_copy(step, q, True).wait_recv()
            at = lax.rem(self.links.z + step, 4) * 4 + 2 * q
            for k in range(2):
                self.add(at + k, pl.ds(0, 48), self.got[0].at[1, 2 * q + k])
            self.z_copy(step, q, False).start()
        for z in range(4):
            step = 1 if z < 2 else 3
            self.y_copy(step, z, True).wait_recv()
            at = z * 4 + lax.rem(self.links.y + step, 4)
            self.add(at, pl.ds(48, 48), self.got[1].at[1, z])
            self.y_copy(step, z, False).start()

    def add(self, at, rows, what):
        self.full[at, rows] = (self.full[at, rows].astype(F32) + what[...].astype(F32)).astype(BF16)

    def second(self, last):
        links, second = self.links, []
        for step in (1, 3):
            for q in range(2):
                self.z_copy(step, q, False).wait()
            for z in range(4):
                self.y_copy(step, z, False).wait()
        for half, axis in ((0, "y"), (1, "z")):
            here = links.z if half else links.y

            @pl.loop(0, 4)
            def _(k):
                slot = k * 4 + links.y if half else links.z * 4 + k
                total = self.full[slot, pl.ds(48 * half, 48)].astype(F32)
                for step in (0, 2):
                    total = total + self.got[half][step, k].astype(F32)
                self.got[half][0, k] = total.astype(BF16)

            for step in FAR_FIRST:
                second.append(
                    links.send(
                        self.got[half].at[0, lax.rem(here + step, 4)],
                        last[half].at[step - 1],
                        axis,
                        step,
                    )
                )
        for q, step in ((0, 1), (1, 3)):
            self.z_copy(step, q, True).wait_send()
        for z in range(4):
            self.y_copy(1 if z < 2 else 3, z, True).wait_send()
        return second


def scatter_first(links, part, got, cut):
    first = []
    for step in FAR_FIRST:
        to = lax.rem(links.z + step, 4) * 4
        first.append(links.send(part(pl.ds(to, 4), cut[0]), got[0].at[step - 1], "z", step))
    for step in FAR_FIRST:
        to = lax.rem(links.y + step, 4)
        for z in range(4):
            first.append(
                links.send(part(z * 4 + to, cut[1]), got[1].at[step - 1, z], "y", step)
            )
    return first


def scatter_second(links, first, part, got, last, cut):
    second = []
    for half, axis in ((0, "y"), (1, "z")):
        received(first[3:] if half else first[:3])
        here = links.z if half else links.y

        @pl.loop(0, 4)
        def _(k):
            slot = k * 4 + links.y if half else links.z * 4 + k
            total = part(slot, cut[half])[...].astype(F32)
            for step in range(3):
                total = total + got[half][step, k].astype(F32)
            got[half][0, k] = total.astype(BF16)

        for step in FAR_FIRST:
            second.append(
                links.send(
                    got[half].at[0, lax.rem(here + step, 4)], last[half].at[step - 1], axis, step
                )
            )
    return second


def scatter_end(links, got, last, half):
    here = links.z if half else links.y
    total = got[half][0, here].astype(F32)
    for step in range(3):
        total = total + last[half][step].astype(F32)
    return total


INS = (
    "tokens",
    "ids",
    "gain_one",
    "w_qkv",
    "w_out",
    "w_router",
    "gain_two",
    "w_sin",
    "w_sout",
    "e_in",
    "e_out",
    "out_grad",
)
OUTS = {
    "block_out": ((SEQ, D), BF16),
    "tokens_grad": ((SEQ, D), F32),
    "g_gain_one": ((1, ROWS), F32),
    "g_qkv": ((ROWS, 2560), F32),
    "g_out": ((ROWS, D), F32),
    "g_gain_two": ((1, ROWS), F32),
    "g_router": ((EXPERTS, ROWS), F32),
    "g_sin": ((ROWS, 2 * SH), F32),
    "g_sout": ((ROWS, SH), F32),
    "g_ein": ((96, 1024), F32),
    "g_eout": ((96, 512), F32),
}
SCRATCH = {
    "small": ((128, 128), F32),
    "pack": ((4, 16, W_ALL), BF16),
    "arrived": ((4, 16, W_ALL), BF16),
    "dense": ((16, 2, 48, W_ATT), BF16),
    "shared": ((16, 2, 48, W_SHARED), BF16),
    "got": ((16, 96, D), BF16),
    "full": ((8, 2, 96, D), BF16),
    "nat": ((D, D), BF16),
    "normed": ((4, SEQ, D), BF16),
    "qkv": ((4, SEQ, 640), BF16),
    "mix": ((4, SEQ, 384), BF16),
    "send_y": ((4, 2, SEQ, D), BF16),
    "send_x": ((4, 2, SEQ, WIDE), BF16),
    "pair_y": ((4, SEQ, D), BF16),
    "pair_x": ((4, SEQ, WIDE), BF16),
    "got_y": ((3, SEQ, D), BF16),
    "got_x": ((3, SEQ, WIDE), BF16),
    "hidden": ((SEQ, D), F32),
    "probs": ((SEQ, 128), F32),
    "chosen": ((SEQ, 128), F32),
    "rows": ((4, 2, SEQ, WIDE), BF16),
    "cot": ((4, 2, SEQ, D), BF16),
    "gated": ((4, 2, SEQ, 640), BF16),
    "joint": ((4, 2, SEQ, 1280), BF16),
    "low": ((4, SEQ, D), BF16),
    "dsh": ((16, 2, 48, 384), BF16),
    "back": ((48, W_ALL), BF16),
    "e_got0": ((3, 4, 48, D), BF16),
    "e_got1": ((3, 4, 48, D), BF16),
    "e_last0": ((3, 48, D), BF16),
    "e_last1": ((3, 48, D), BF16),
    "d_got0": ((3, 4, 48, 640), BF16),
    "d_got1": ((3, 4, 48, 512), BF16),
    "d_last0": ((3, 48, 640), BF16),
    "d_last1": ((3, 48, 512), BF16),
    "s_got0": ((3, 4, 48, 384), BF16),
    "s_got1": ((3, 4, 48, 384), BF16),
    "s_last0": ((3, 48, 384), BF16),
    "s_last1": ((3, 48, 384), BF16),
}
SEMS = 400


class Bag:
    pass


def near(i):
    return jnp.where(i == 2, 3, jnp.where(i == 3, 2, i))


def far(i):
    return jnp.where(i == 0, 2, jnp.where(i == 3, 0, jnp.where(i == 2, 3, 1)))


def causal_probs(q, k):
    scores = dot_nt(q, k) * HD**-0.5
    row = lax.broadcasted_iota(jnp.int32, (SEQ, SEQ), 0)
    col = lax.broadcasted_iota(jnp.int32, (SEQ, SEQ), 1)
    scores = jnp.where(col <= row, scores, -1e30)
    exponent = jnp.exp(scores - jnp.max(scores, axis=1, keepdims=True))
    return exponent * (1.0 / jnp.sum(exponent, axis=1, keepdims=True))


def kernel(*refs):
    b = Bag()
    names = [*INS, *OUTS, *SCRATCH]
    for name, ref in zip(names, refs):
        setattr(b, name, ref)
    links = Links(*refs[len(names) :])
    x, y, z, c = links.x, links.y, links.z, links.c
    other = 1 - c
    here = z * 4 + y
    mine = 2 * x + c
    every = pl.ds(0, 48)
    e_cut = ((pl.ds(0, 48),), (pl.ds(48, 48),))
    d_cut = ((every, pl.ds(0, 640)), (every, pl.ds(640, 512)))
    s_cut = ((every, pl.ds(0, 384)), (every, pl.ds(384, 384)))
    d_part = lambda slots, half: b.dense.at[(slots, c, *half)]
    s_part = lambda slots, half: b.shared.at[(slots, c, *half)]
    e_part = lambda slots, half: b.got.at[(slots, *half)]

    greeted = links.greet("xyzc")
    b.got[here, :, 0:1024] = b.e_in[...]
    b.got[here, :, 1024:1536] = b.e_out[...]
    b.pack[...] = jnp.zeros_like(b.pack)
    b.small[...] = jnp.zeros_like(b.small)
    b.small[0:EXPERTS, 0:ROWS] = b.w_router[...].astype(F32)
    b.small[8:9, 0:ROWS] = b.gain_two[...].astype(F32)
    b.small[9:10, 0:ROWS] = b.gain_one[...].astype(F32)
    small = b.small[...].T
    lane = lax.broadcasted_iota(jnp.int32, (SEQ, 128), 1)
    row = lax.broadcasted_iota(jnp.int32, (SEQ, 128), 0)
    named = jnp.zeros((SEQ, 128), F32)
    for k in range(TOP):
        named = named + (b.ids[k : k + 1, :] == row).astype(F32)
    b.chosen[...] = named.T
    gain_one = small[0:ROWS, 9:10]
    for k in range(4):
        for start, width, at in ((k * 384, 384, 0), (D + k * 128, 128, 384), (2048 + k * 128, 128, 512)):
            b.pack[k, 0:ROWS, at : at + width] = (
                b.w_qkv[:, start : start + width].astype(F32) * gain_one
            ).astype(BF16)
        b.pack[k, 0:ROWS, 640:1024] = b.w_out[:, k * 384 : k * 384 + 384]
        b.pack[k, 0:ROWS, 1024:1152] = small[0:ROWS].astype(BF16)
        for core in range(2):
            at, unit = W_ATT + 384 * core, (2 * k + core) * 128
            b.pack[k, 0:ROWS, at : at + 128] = b.w_sin[:, unit : unit + 128]
            b.pack[k, 0:ROWS, at + 128 : at + 256] = b.w_sin[:, SH + unit : SH + unit + 128]
            b.pack[k, 0:ROWS, at + 256 : at + 384] = b.w_sout[:, unit : unit + 128]
    greeted()
    exchange = [
        links.send(b.pack.at[lax.rem(x + step, 4)], b.arrived.at[x], "x", step)
        for step in FAR_FIRST
    ]
    e_cols = lambda cols: tuple((rows, cols) for (rows,) in e_cut)
    e_first = gather_first(links, b.got.at[here], e_part, here, e_cols(pl.ds(0, 1024)))
    inputs = b.tokens[...].astype(F32)
    inverse_one = lax.rsqrt(jnp.mean(inputs * inputs, axis=1, keepdims=True) + epsilon)
    b.normed[x] = (inputs * inverse_one).astype(BF16)
    b.cot[x, c] = b.out_grad[...]
    cot_pair = links.send(b.cot.at[x, c], b.cot.at[x, c], "c", 1)
    b.arrived[x] = b.pack[x]
    finish(exchange)
    normed_ring = RowRing(links, lambda s, rows: b.normed.at[s, rows])
    cot_ring = RowRing(links, lambda s, rows: b.cot.at[s, c, rows])
    normed_ring.start()
    pick = pick_matrix((48, 64), lambda row: row // ROWS * 16 + row % ROWS)
    for col in range(0, W_ALL, 384):
        block = moved(pick, b.arrived[:, :, col : col + 384].reshape(64, 384))
        if col < W_ATT:
            b.dense[here, c, :, col : col + 384] = block
        else:
            b.shared[here, c, :, col - W_ATT : col - W_ATT + 384] = block

    d_first = gather_first(links, b.dense.at[here, c], d_part, here, d_cut)
    d_ring = PlaneRing(links, d_first, d_part, d_cut)
    normed_ring.pass_on()
    cot_ring.start()
    d_ring.pass_on()
    s_first = gather_first(links, b.shared.at[here, c], s_part, here, s_cut)
    e_first += gather_first(links, b.got.at[here], e_part, here, e_cols(pl.ds(1024, 512)))
    d_ring.arrive_near()
    d_ring.arrive()
    sent(d_first)
    d_pair = links.take(8)

    def d_forward(j):
        piece = b.dense.at[pl.ds(2 * j, 2), c]
        return links.copy(piece, piece, "c", 1, d_pair + j)

    for j in range(8):
        d_forward(j).start()
    e_ring = PlaneRing(links, e_first, e_part, e_cut)
    s_ring = PlaneRing(links, s_first, s_part, s_cut)
    normed_ring.arrive()

    order = pick_matrix(
        (192, 192), lambda row: row % 48 // ROWS * 48 + row // 48 * ROWS + row % ROWS
    )

    def to_rows(j, source, start, at):
        piece = source[pl.ds(2 * j, 2), :, :, start].reshape(192, 384)
        piece = moved(order, piece)
        for k in range(4):
            row = pl.multiple_of(k * 384 + j * 48, 16)
            b.nat[pl.ds(row, 48), at : at + 384] = piece[k * 48 : k * 48 + 48]

    def to_blocks(j, target, start, at):
        pieces = [
            b.nat[pl.ds(pl.multiple_of(k * 384 + j * 48, 16), 48), at : at + 384] for k in range(4)
        ]
        piece = moved(order, jnp.concatenate(pieces, axis=0))
        target[pl.ds(2 * j, 2), :, :, start] = piece.reshape(2, 2, 48, 384)

    @pl.loop(0, 8)
    def _(j):
        d_forward(j).wait()
        for part in range(3):
            to_rows(j, b.dense, pl.ds(part * 384, 384), part * 384)

    mix_ring = SumRing(links, lambda s, rows: b.send_y.at[s, 0, rows], b.got_y)

    def attend(s):
        b.qkv[s] = dot(b.normed[s], b.nat[:, 0:640]).astype(BF16)
        key, value = b.qkv[s, :, 384:512], b.qkv[s, :, 512:640]
        for h in range(3):
            head = slice(h * HD, (h + 1) * HD)
            probs = causal_probs(b.qkv[s, :, head], key)
            b.mix[s, :, head] = dot(probs.astype(BF16), value).astype(BF16)
        for n in range(2):
            rows = slice(n * 768, (n + 1) * 768)
            b.send_y[s, 0, :, rows] = dot_nt(b.mix[s], b.nat[rows, 640:1024]).astype(BF16)

    @pl.loop(0, 4)
    def _(i):
        @pl.when(i == 3)
        def _():
            mix_ring.pass_on()

        attend(lax.rem(x + far(i), 4))

        @pl.when(i == 0)
        def _():
            mix_ring.start_far()

        for k, step in ((1, 1), (2, 3)):

            @pl.when(i == k)
            def _():
                mix_ring.near(step, True).start()

    e_ring.pass_on()
    s_ring.pass_on()
    cot_ring.pass_on()

    hidden = mix_ring.total(b.tokens[...].astype(F32) + b.send_y[x, 0].astype(F32))
    b.hidden[...] = hidden
    inverse_two = lax.rsqrt(jnp.mean(hidden * hidden, axis=1, keepdims=True) + epsilon)
    lane8 = lax.broadcasted_iota(jnp.int32, (8, 128), 1)
    gain_two = dot_nt((lane8 == 8).astype(BF16), b.nat[:, 1024:1152])[0:1]
    moe_in = (hidden * inverse_two * gain_two).astype(BF16)
    b.rows[x, c, :, 0:D] = moe_in
    logits = jnp.where(lane < EXPERTS, dot(moe_in, b.nat[:, 1024:1152]), -1e30)
    exponent = jnp.exp(logits - jnp.max(logits, axis=1, keepdims=True))
    router_probs = exponent / jnp.sum(exponent, axis=1, keepdims=True)
    b.probs[...] = router_probs
    gates = b.chosen[...] * router_probs
    high = gates.astype(BF16).astype(F32)
    b.rows[x, c, :, D:WIDE] = (high + pltpu.roll(gates - high, 8, 1)).astype(BF16)
    rows_ring = RowRing(links, lambda s, rows: b.rows.at[s, c, rows])
    rows_ring.start()
    pair_rows = links.take(4)
    pair_cot = links.take(4)
    forward_rows = lambda s, d: links.copy(
        b.rows.at[s, c], b.rows.at[s, c], "c", 1, pair_rows + d
    )
    forward_cot = lambda s, d: links.copy(b.cot.at[s, c], b.cot.at[s, c], "c", 1, pair_cot + d)
    forward_rows(x, 0).start()
    e_hands = []
    lower, upper = pl.ds(0, 48), pl.ds(48, 48)
    for k in range(2):
        for half, to_other in ((other, True), (c, False)):
            at = 2 * half + k
            pieces = [
                (at == lax.rem(z + 2, 4), b.got.at[pl.ds(at * 4, 4), lower], pl.ds(4 * k, 4), lower)
            ]
            for to in range(4):
                pieces.append(
                    (to == lax.rem(y + 2, 4), b.got.at[at * 4 + to, upper], 4 * k + to, upper)
                )
            for is_far, source, slots, rows in pieces:
                target = b.full.at[slots, c, rows]
                if to_other:
                    copy = links.copy(source, target, "c", 1, links.take(1))
                else:
                    copy = pltpu.make_async_copy(source, target, links.send_sem.at[links.take(1)])
                e_hands.append((is_far, copy))

    def e_hand(far_ones):
        for is_far, copy in e_hands:

            @pl.when(is_far == far_ones)
            def _():
                copy.start()

    e_ring.arrive_near()
    e_hand(False)
    e_ring.arrive()
    e_hand(True)
    sent(e_first + s_first)
    s_ring.arrive_near()
    s_ring.arrive()
    half = pl.ds(pl.multiple_of(other * 384, 128), 384)
    s_pair = links.send(b.shared.at[:, c, :, half], b.shared.at[:, c, :, half], "c", 1)

    s_pair.wait()
    for _, copy in e_hands:
        copy.wait()

    @pl.loop(0, 8)
    def _(j):
        to_rows(j, b.shared, pl.ds(pl.multiple_of(c * 384, 128), 384), W_ATT)

    back_pair = links.take(8)
    back_base = links.take(8)
    sum_pair = links.take(4)
    parts = (pl.ds(0, 768), pl.ds(768, WIDE - 768))
    back_forward = lambda s, d, n: links.copy(
        b.send_x.at[s, other, :, parts[n]], b.pair_x.at[s, :, parts[n]], "c", 1, back_pair + 2 * d + n
    )
    sum_forward = lambda s, d: links.copy(
        b.send_y.at[s, other], b.pair_y.at[s], "c", 1, sum_pair + d
    )
    back_copy = lambda step, n: links.copy(
        b.send_x.at[lax.rem(x + step, 4), c, :, parts[n]],
        b.got_x.at[step - 1, :, parts[n]],
        "x",
        step,
        back_base + 2 * step + n,
    )
    sum_ring = SumRing(links, lambda s, rows: b.send_y.at[s, c, rows], b.got_y)
    cot_pair.wait()

    cot_ring.arrive()
    for d in range(1, 4):
        forward_cot(lax.rem(x + d, 4), d).start()
    forward_rows(x, 0).wait_recv()

    def which(i, core):
        sides = ((i == 1) & (core == 0)) | ((i == 2) & (core == 1))
        return ((0, i == 0), (1, sides), (3, sides), (2, i == 3))

    def give_pair(i, n):
        for d, now in which(i, other):

            @pl.when(now)
            def _():
                back_forward(lax.rem(x + d, 4), d, n).start()

    def add_pair(i):
        for d, now in which(i, c):
            s = lax.rem(x + d, 4)

            @pl.when(now)
            def _():
                for n in range(2):
                    back_forward(s, d, n).wait_recv()
                    b.send_x[s, c, :, parts[n]] = (
                        b.send_x[s, c, :, parts[n]].astype(F32)
                        + b.pair_x[s, :, parts[n]].astype(F32)
                    ).astype(BF16)
                    if d:
                        back_copy(d, n).start()

    @pl.loop(0, 4)
    def _(i):
        one = (lax.rem(x + jnp.where(i == 0, 0, jnp.where(i == 3, 2, 1)), 4), jnp.where(i == 2, 1, 0))
        two = (lax.rem(x + jnp.where(i == 0, 0, jnp.where(i == 3, 2, 3)), 4), jnp.where(i == 1, 0, 1))
        both = lambda ref, cols: jnp.concatenate([ref[(*one, slice(None), cols)], ref[(*two, slice(None), cols)]], axis=0)

        def keep(ref, cols, value):
            ref[(*one, slice(None), cols)] = value[0:SEQ]
            ref[(*two, slice(None), cols)] = value[SEQ:256]

        for k, far_ones in ((1, (1, 3)), (3, (2,))):

            @pl.when(i == k)
            def _():
                for d in far_ones:
                    forward_cot(lax.rem(x + d, 4), d).wait_recv()
                    forward_rows(lax.rem(x + d, 4), d).wait_recv()

        tokens = both(b.rows, slice(0, D))
        grads = both(b.cot, slice(0, D))
        lanes = lax.broadcasted_iota(jnp.int32, (256, 128), 1)
        gate = both(b.rows, slice(D, WIDE)).astype(F32)
        gate = jnp.where((lanes == mine) | (lanes == mine + 8), gate, 0.0)
        gate = jnp.sum(gate, axis=1, keepdims=True)
        gate_grad = jnp.zeros((256, 1), F32)
        for part in range(3):
            if part < 2:
                at, width = part * 256, 256
                g = dot(tokens, b.full[:, :, :, at : at + 256].reshape(D, 256))
                u = dot(tokens, b.full[:, :, :, at + 512 : at + 768].reshape(D, 256))
                a = dot(grads, b.full[:, :, :, at + 1024 : at + 1280].reshape(D, 256))
                first, second, scale = at, at + 512, gate
            else:
                at, width = 512, 128
                gu = dot(tokens, b.nat[:, 1152:1408])
                g, u = gu[:, 0:128], gu[:, 128:256]
                a = dot(grads, b.nat[:, 1408:1536])
                first, second, scale = 1024, 1152, None
            g = g.astype(BF16).astype(F32)
            u = u.astype(BF16).astype(F32)
            sg = jax.nn.sigmoid(g)
            act = (g * sg * u).astype(BF16)
            if scale is not None:
                gate_grad = gate_grad + jnp.sum(act.astype(F32) * a, axis=1, keepdims=True)
                act = (act.astype(F32) * scale).astype(BF16)
                a = a * scale
            keep(b.gated, slice(at, at + width), act)
            keep(
                b.joint,
                slice(first, first + width),
                (a * u * (sg * (1.0 + g * (1.0 - sg)))).astype(BF16),
            )
            keep(b.joint, slice(second, second + width), (a * g * sg).astype(BF16))
            if part == 0:

                @pl.when(i > 0)
                def _():
                    add_pair(i - 1)

                @pl.when(i == 2)
                def _():
                    rows_ring.arrive()
                    forward_rows(lax.rem(x + 2, 4), 2).start()


        @pl.when(i == 0)
        def _():
            rows_ring.pass_on()
            for d in (1, 3):
                forward_rows(lax.rem(x + d, 4), d).start()

        gate_high = gate_grad.astype(BF16).astype(F32)
        spread = jnp.where(lanes == mine, gate_high, 0.0)
        spread = spread + jnp.where(lanes == mine + 8, gate_grad - gate_high, 0.0)
        keep(b.send_x, slice(D, WIDE), spread.astype(BF16))
        slopes = both(b.joint, slice(0, 1280))
        for n in range(2):
            rows = slice(n * 768, (n + 1) * 768)
            result = dot_nt(
                slopes[:, 0:1024], b.full[4 * n : 4 * n + 4, :, :, 0:1024].reshape(768, 1024)
            ) + dot_nt(slopes[:, 1024:1280], b.nat[rows, 1152:1408])
            keep(b.send_x, rows, result.astype(BF16))
            give_pair(i, n)

    add_pair(3)

    e_got, e_last = (b.e_got0, b.e_got1), (b.e_last0, b.e_last1)
    e_sum = PlaneSum(links, b.got, e_got)
    e_moves = []
    for low in range(2):
        for n in (2 * low, 2 * low + 1):
            cols = slice(n * 384, (n + 1) * 384)
            tokens = b.rows[:, :, :, cols].reshape(1024, 384)
            for at in (0, 512):
                result = dot_tn(tokens, b.joint[:, :, :, at : at + 512].reshape(1024, 512))
                b.full[2 * n : 2 * n + 2, :, :, at : at + 512] = result.astype(BF16).reshape(
                    2, 2, 96, 512
                )
            grads = b.cot[:, :, :, cols].reshape(1024, 384)
            result = dot_tn(grads, b.gated[:, :, :, 0:512].reshape(1024, 512))
            result = result.astype(BF16).reshape(2, 2, 2, 48, 512)
            for h in range(2):
                b.dense[8 * h + 2 * n : 8 * h + 2 * n + 2, :, :, 0:512] = result[:, :, h]
        four = pl.ds(4 * low, 4)
        target = pl.ds(8 * c + 4 * low, 4)
        wide, slim = pl.ds(0, 1024), pl.ds(1024, 512)
        moves = [
            links.send(b.full.at[four, other, :, wide], b.got.at[target, :, wide], "c", 1),
            links.local(b.full.at[four, c, :, wide], b.got.at[target, :, wide]),
        ]
        for h in range(2):
            rows, slots = pl.ds(48 * h, 48), pl.ds(8 * h + 4 * low, 4)
            moves += [
                links.send(
                    b.dense.at[slots, other, :, pl.ds(0, 512)], b.got.at[target, rows, slim], "c", 1
                ),
                links.local(b.dense.at[slots, c, :, pl.ds(0, 512)], b.got.at[target, rows, slim]),
            ]
        e_moves.append(moves)

    def e_start(low):
        finish(e_moves[low])
        e_sum.start(low)

    e_start(0)
    e_start(1)

    for step in NEAR_FIRST:
        back_copy(step, 0).wait()
        back_copy(step, 1).wait()
    moe_back = b.send_x[x, c].astype(F32)
    for step in range(3):
        moe_back = moe_back + b.got_x[step].astype(F32)
    raw = moe_back[:, D:WIDE]
    router_probs = b.probs[...]
    prob_grad = b.chosen[...] * (raw + pltpu.roll(raw, 120, 1))
    logit_grad = router_probs * (
        prob_grad - jnp.sum(router_probs * prob_grad, axis=1, keepdims=True)
    )
    logit_grad = logit_grad.astype(BF16)
    gain_two = dot_nt((lane8 == 8).astype(BF16), b.nat[:, 1024:1152])[0:1]
    moe_in_grad = moe_back[:, 0:D] + dot_nt(logit_grad, b.nat[:, 1024:1152])
    hidden = b.hidden[...]
    inverse_two = lax.rsqrt(jnp.mean(hidden * hidden, axis=1, keepdims=True) + epsilon)
    scaled = gain_two * moe_in_grad
    hidden_grad = (
        b.out_grad[...].astype(F32)
        + inverse_two * scaled
        - hidden
        * (inverse_two * inverse_two * inverse_two)
        * jnp.mean(scaled * hidden, axis=1, keepdims=True)
    )
    b.tokens_grad[...] = hidden_grad
    b.low[x] = hidden_grad.astype(BF16)
    low_ring = RowRing(links, lambda s, rows: b.low.at[s, rows])
    low_ring.start()
    misc_grad = dot_tn(b.rows[x, c, :, 0:D], logit_grad) + dot_tn(
        (moe_in_grad * hidden * inverse_two).astype(BF16), (lane == 8).astype(BF16)
    )
    b.nat[:, 1024:1152] = misc_grad.astype(BF16)

    @pl.loop(0, 4)
    def _(d):
        s = lax.rem(x + d, 4)
        for n in range(2):
            rows = slice(n * 768, (n + 1) * 768)
            result = dot_nt(
                b.gated[s, :, :, 0:512].reshape(256, 512), b.full[4 * n : 4 * n + 4, :, :, 1024:1536].reshape(768, 512)
            ) + dot_nt(b.gated[s, :, :, 512:640].reshape(256, 128), b.nat[rows, 1408:1536])
            b.send_y[s, :, :, rows] = result.astype(BF16).reshape(2, SEQ, 768)
        sum_forward(s, d).start()

    for n in range(4):
        cols = slice(n * 384, (n + 1) * 384)
        tokens = b.rows[:, :, :, cols].reshape(1024, 384)
        result = dot_tn(tokens, b.joint[:, :, :, 1024:1280].reshape(1024, 256))
        b.nat[cols, 1152:1408] = result.astype(BF16)
        grads = b.cot[:, :, :, cols].reshape(1024, 384)
        result = dot_tn(grads, b.gated[:, :, :, 512:640].reshape(1024, 128))
        b.nat[cols, 1408:1536] = result.astype(BF16)

    @pl.loop(0, 8)
    def _(j):
        to_blocks(j, b.dsh, pl.ds(0, 384), W_ATT)

    half = pl.ds(pl.multiple_of(c * 384, 128), 384)
    cot_ring.sent()
    for d in range(1, 4):
        forward_cot(lax.rem(x + d, 4), d).wait_send()
    s_give = links.send(b.dsh.at[:, other], b.shared.at[:, 0, :, half], "c", 1)
    s_keep = links.local(b.dsh.at[:, c], b.shared.at[:, 0, :, half])
    s_sum = lambda slots, half: b.shared.at[(slots, 0, *half)]

    e_sum.pass_on()
    s_give.wait()
    s_keep.wait()
    s_first = scatter_first(links, s_sum, (b.s_got0, b.s_got1), s_cut)
    low_ring.pass_on()
    norm_base = links.take(4)
    norm_copy = lambda step: links.copy(
        b.send_x.at[lax.rem(x + step, 4), 0, :, pl.ds(0, D)],
        b.got_x.at[step - 1, :, pl.ds(0, D)],
        "x",
        step,
        norm_base + step,
    )
    for d in range(4):
        for n in range(2):
            back_forward(lax.rem(x + d, 4), d, n).wait_send()

    @pl.loop(0, 4)
    def _(i):
        d = near(i)
        s = lax.rem(x + d, 4)

        @pl.when(i == 3)
        def _():
            low_ring.arrive()

        mix_grad = dot(b.low[s], b.nat[:, 640:1024]).astype(BF16)
        key, value = b.qkv[s, :, 384:512], b.qkv[s, :, 512:640]
        key_grad = jnp.zeros((SEQ, HD), F32)
        value_grad = jnp.zeros((SEQ, HD), F32)
        for h in range(3):
            head = slice(h * HD, (h + 1) * HD)
            query = b.qkv[s, :, head]
            mixed = mix_grad[:, head]
            probs = causal_probs(query, key)
            dprob = dot_nt(mixed, value)
            value_grad = value_grad + dot_tn(probs.astype(BF16), mixed)
            delta = jnp.sum(probs * dprob, axis=1, keepdims=True)
            score_grad = (probs * (dprob - delta)).astype(BF16)
            b.qkv[s, :, head] = (dot(score_grad, key) * HD**-0.5).astype(BF16)
            key_grad = key_grad + dot_tn(score_grad, query)
        b.qkv[s, :, 384:512] = (key_grad * HD**-0.5).astype(BF16)
        b.qkv[s, :, 512:640] = value_grad.astype(BF16)
        for n in range(2):
            rows = slice(n * 768, (n + 1) * 768)
            b.send_x[s, 0, :, rows] = dot_nt(b.qkv[s], b.nat[rows, 0:640]).astype(BF16)

        @pl.when(i > 0)
        def _():
            norm_copy(d).start()

    d_base = links.take(8)

    def d_landing(j):
        rows = pl.ds(pl.multiple_of(lax.div(j, 4) * 48, 16), 48)
        return b.cot.at[lax.rem(j, 4), :, rows, pl.ds(0, W_ATT)]

    d_give = lambda j: links.copy(
        b.dense.at[pl.ds(2 * j, 2), other], d_landing(j), "c", 1, d_base + j
    )

    for n in range(4):
        cols = slice(n * 384, (n + 1) * 384)
        result = dot_tn(b.normed[:, :, cols].reshape(512, 384), b.qkv[...].reshape(512, 640))
        b.nat[cols, 0:640] = result.astype(BF16)
        result = dot_tn(b.low[:, :, cols].reshape(512, 384), b.mix[...].reshape(512, 384))
        b.nat[cols, 640:1024] = result.astype(BF16)

    e_next = e_sum.second(e_last)

    @pl.loop(0, 8)
    def _(j):
        for part in range(3):
            to_blocks(j, b.dense, pl.ds(part * 384, 384), part * 384)
        d_give(j).start()

    s_next = scatter_second(
        links, s_first, s_sum, (b.s_got0, b.s_got1), (b.s_last0, b.s_last1), s_cut
    )

    @pl.loop(0, 8)
    def _(j):
        d_give(j).wait()
        total = b.dense[pl.ds(2 * j, 2), c].astype(F32) + d_landing(j)[...].astype(F32)
        b.dense[pl.ds(2 * j, 2), c] = total.astype(BF16)

    d_first = scatter_first(links, d_part, (b.d_got0, b.d_got1), d_cut)

    for d in (2, 1, 3, 0):
        s = lax.rem(x + d, 4)
        sum_forward(s, d).wait()
        b.send_y[s, c] = (b.send_y[s, c].astype(F32) + b.pair_y[s].astype(F32)).astype(BF16)
        if d == 2:
            sum_ring.start_far()
        elif d:
            sum_ring.near(d, True).start()

    for step in NEAR_FIRST:
        norm_copy(step).wait()
    scaled = b.send_x[x, 0, :, 0:D].astype(F32)
    for step in range(3):
        scaled = scaled + b.got_x[step, :, 0:D].astype(F32)
    inputs = b.tokens[...].astype(F32)
    inverse_one = lax.rsqrt(jnp.mean(inputs * inputs, axis=1, keepdims=True) + epsilon)
    b.tokens_grad[...] = (
        b.tokens_grad[...]
        + inverse_one * scaled
        - inputs
        * (inverse_one * inverse_one * inverse_one)
        * jnp.mean(scaled * inputs, axis=1, keepdims=True)
    )

    sum_ring.pass_on()

    d_next = scatter_second(
        links, d_first, d_part, (b.d_got0, b.d_got1), (b.d_last0, b.d_last1), d_cut
    )
    received(s_next)
    for part in range(2):
        total = scatter_end(links, (b.s_got0, b.s_got1), (b.s_last0, b.s_last1), part)
        b.back[:, W_ATT + 384 * part : W_ATT + 384 * part + 384] = total.astype(BF16)
    received(d_next)
    for part, cols in ((0, slice(0, 640)), (1, slice(640, 1152))):
        total = scatter_end(links, (b.d_got0, b.d_got1), (b.d_last0, b.d_last1), part)
        b.back[:, cols] = total.astype(BF16)
    pick = pick_matrix((64, 48), lambda row: jnp.where(row % 16 < ROWS, row // 16 * ROWS + row % 16, -1))
    for col in range(0, W_ALL, 384):
        b.pack[:, :, col : col + 384] = moved(pick, b.back[:, col : col + 384]).reshape(4, 16, 384)
    exchange = [
        links.send(b.pack.at[lax.rem(x + step, 4)], b.arrived.at[x], "x", step)
        for step in FAR_FIRST
    ]
    b.arrived[x] = b.pack[x]
    received(e_next)
    for part in range(2):
        rows = slice(48 * part, 48 * part + 48)
        total = scatter_end(links, e_got, e_last, part)
        b.g_ein[rows] = total[:, 0:1024]
        b.g_eout[rows] = total[:, 1024:1536]
    result = sum_ring.total(b.hidden[...] + b.send_y[x, c].astype(F32))
    b.block_out[...] = result.astype(BF16)

    sent(s_first + d_first)
    for ring in (normed_ring, rows_ring, low_ring):
        ring.sent()
    for d in range(4):
        forward_rows(lax.rem(x + d, 4), d).wait_send()
    sent(e_next + s_next + d_next)
    received(exchange)
    gain_grad = jnp.zeros((ROWS, 1), F32)
    misc = jnp.zeros((ROWS, 128), F32)
    for k in range(4):
        piece = b.arrived[k].astype(F32)[0:ROWS]
        for start, width, at in ((k * 384, 384, 0), (D + k * 128, 128, 384), (2048 + k * 128, 128, 512)):
            raw = piece[:, at : at + width]
            gain_grad = gain_grad + jnp.sum(
                raw * b.w_qkv[:, start : start + width].astype(F32), axis=1, keepdims=True
            )
            b.g_qkv[:, start : start + width] = raw * gain_one
        b.g_out[:, k * 384 : k * 384 + 384] = piece[:, 640:1024]
        misc = misc + piece[:, 1024:1152]
        for core in range(2):
            at, unit = W_ATT + 384 * core, (2 * k + core) * 128
            b.g_sin[:, unit : unit + 128] = piece[:, at : at + 128]
            b.g_sin[:, SH + unit : SH + unit + 128] = piece[:, at + 128 : at + 256]
            b.g_sout[:, unit : unit + 128] = piece[:, at + 256 : at + 384]
    b.small[0:ROWS] = jnp.where(lane[0:ROWS] == 9, gain_grad, misc)
    small = b.small[...].T
    b.g_router[...] = small[0:EXPERTS, 0:ROWS]
    b.g_gain_two[...] = small[8:9, 0:ROWS]
    b.g_gain_one[...] = small[9:10, 0:ROWS]
    sent(exchange)


def hand_over(*refs):
    n = len(OUTS)
    for source, target in zip(refs[:n], refs[n:]):
        target[...] = source[...]


def local(
    tokens,
    expert_ids,
    attn_gain,
    w_qkv,
    w_out,
    moe_gain,
    w_router,
    w_shared_in,
    w_shared_out,
    w_expert_in,
    w_expert_out,
    out_grad,
):
    results = pl.pallas_call(
        kernel,
        out_shape=[jax.ShapeDtypeStruct(shape, dtype) for shape, dtype in OUTS.values()],
        in_specs=[pl.BlockSpec(memory_space=pltpu.VMEM)] * len(INS),
        out_specs=[pl.BlockSpec(memory_space=pltpu.VMEM)] * len(OUTS),
        scratch_shapes=[
            *[pltpu.VMEM(shape, dtype) for shape, dtype in SCRATCH.values()],
            pltpu.SemaphoreType.DMA((SEMS,)),
            pltpu.SemaphoreType.DMA((SEMS,)),
        ],
        compiler_params=pltpu.CompilerParams(
            collective_id=1, has_side_effects=True, vmem_limit_bytes=(64 << 20) - (1 << 16)
        ),
        cost_estimate=pl.CostEstimate(
            flops=23_000_000_000, bytes_accessed=10_000_000, transcendentals=2_000_000
        ),
        name="block",
    )(
        tokens,
        expert_ids.T,
        attn_gain[None],
        w_qkv,
        w_out,
        w_router.T,
        moe_gain[None],
        w_shared_in,
        w_shared_out,
        w_expert_in,
        w_expert_out,
        out_grad,
    )
    results = pl.pallas_call(
        hand_over,
        out_shape=[jax.ShapeDtypeStruct(shape, dtype) for shape, dtype in OUTS.values()],
        in_specs=[pl.BlockSpec(memory_space=pltpu.VMEM)] * len(OUTS),
        out_specs=[pl.BlockSpec(memory_space=pltpu.VMEM)] * len(OUTS),
        name="hand_over",
    )(*results)
    block_out, tokens_grad, gain_one, qkv, out, gain_two, router, sin, sout, ein, eout = results
    return (
        block_out,
        tokens_grad,
        gain_one[0],
        qkv,
        out,
        gain_two[0],
        router.T,
        sin,
        sout,
        ein,
        eout,
    )


def solution(mesh):
    wide, flat = P("fsdp", None), P("fsdp")
    return jax.shard_map(
        local,
        mesh=mesh,
        in_specs=(wide, wide, flat, wide, wide, flat, wide, wide, wide, wide, wide, wide),
        out_specs=(wide, wide, flat, wide, wide, flat, wide, wide, wide, wide, wide),
        check_vma=False,
    )
```

```python
import jax
import jax.numpy as jnp
from jax import lax
from jax.experimental import pallas as pl
from jax.experimental.pallas import tpu as pltpu
from jax.sharding import PartitionSpec as P

D = 1536
HD = 128
SH = 1024
EXPERTS = 8
TOP = 6
ROWS = 12
SEQ = 128
W_ATT = 1152
W_SHARED = 768
W_ALL = W_ATT + W_SHARED
WIDE = D + 128
epsilon = 1e-05
MESH = pl.DeviceIdType.MESH
F32 = jnp.float32
BF16 = jnp.bfloat16
STRIDE = {"x": (32, 4), "z": (8, 4), "y": (2, 4), "c": (1, 2)}
FAR_FIRST = (2, 1, 3)
NEAR_FIRST = (1, 3, 2)


def place(me, axis):
    stride, size = STRIDE[axis]
    return lax.rem(lax.div(me, stride), size)


def peer(me, axis, step):
    stride, size = STRIDE[axis]
    here = place(me, axis)
    return me + (lax.rem(here + step, size) - here) * stride


class Links:
    def __init__(self, send_sem, recv_sem):
        self.me = lax.axis_index("fsdp")
        self.send_sem, self.recv_sem = send_sem, recv_sem
        self.count = self.locals = 0
        self.again, self.kept = None, 12
        self.x, self.y, self.z, self.c = (place(self.me, axis) for axis in "xyzc")

    def take(self, number):
        first = self.count
        self.count += number
        return first

    def left(self):
        self.again = self.count

    def sender(self, sem):
        again = self.again is not None and (not isinstance(sem, int) or sem >= self.again)
        return self.send_sem.at[sem - self.again + self.kept if again else sem]

    def copy(self, src, dst, axis, step, sem):
        return pltpu.make_async_remote_copy(
            src_ref=src,
            dst_ref=dst,
            send_sem=self.sender(sem),
            recv_sem=self.recv_sem.at[sem],
            device_id=(peer(self.me, axis, step),),
            device_id_type=MESH,
        )

    def send(self, src, dst, axis, step):
        copy = self.copy(src, dst, axis, step, self.take(1))
        copy.start()
        return copy

    def local(self, src, dst):
        copy = self.local_copy(src, dst)
        copy.start()
        return copy

    def local_copy(self, src, dst):
        self.locals += 1
        return pltpu.make_async_copy(src, dst, self.send_sem.at[SENDS - self.locals])

    def greet(self, axes):
        barrier = pltpu.get_barrier_semaphore()
        total = 0
        for axis in axes:
            for step in range(1, STRIDE[axis][1]):
                pl.semaphore_signal(
                    barrier, inc=1, device_id=(peer(self.me, axis, step),), device_id_type=MESH
                )
                total += 1
        return lambda: pl.semaphore_wait(barrier, total)


def finish(copies):
    for copy in copies:
        copy.wait()


def received(copies):
    for copy in copies:
        copy.wait_recv()


def sent(copies):
    for copy in copies:
        copy.wait_send()


def dot(a, b):
    return jnp.dot(a, b, preferred_element_type=F32)


def dot_nt(a, b):
    return lax.dot_general(a, b, (((1,), (1,)), ((), ())), preferred_element_type=F32)


def dot_tn(a, b):
    return lax.dot_general(a, b, (((0,), (0,)), ((), ())), preferred_element_type=F32)


def pick_matrix(shape, source):
    row = lax.broadcasted_iota(jnp.int32, shape, 0)
    col = lax.broadcasted_iota(jnp.int32, shape, 1)
    return (col == source(row)).astype(BF16)


def moved(pick, rows):
    return dot(pick, rows).astype(BF16)


def gather_first(links, own, part, here, cut):
    first = []
    for axis, half in (("y", cut[0]), ("z", cut[1])):
        for step in FAR_FIRST:
            first.append(links.send(own.at[half], part(here, half), axis, step))
    return first


class PlaneRing:
    def __init__(self, links, first, part, cut):
        self.links, self.part, self.cut = links, part, cut
        received(first)
        self.near, self.far, self.left = {}, [], False
        for step, order in ((1, (0, 1)), (3, (1, 0))):
            for h in order:
                piece = part(pl.ds(links.z * 4 + 2 * h, 2), cut[0])
                self.near["z", step, h] = links.send(piece, piece, "z", step)
        for step, order in ((1, (0, 1, 2, 3)), (3, (2, 3, 0, 1))):
            for z in order:
                piece = part(z * 4 + links.y, cut[1])
                self.near["y", step, z] = links.send(piece, piece, "y", step)

    def pass_on(self):
        links, part, cut = self.links, self.part, self.cut
        for step, h in ((1, 0), (3, 1)):
            self.near["z", step, h].wait_recv()
            piece = part(pl.ds(lax.rem(links.z + 4 - step, 4) * 4 + 2 * h, 2), cut[0])
            self.far.append(links.send(piece, piece, "z", step))
        for step, z in ((1, 0), (1, 1), (3, 2), (3, 3)):
            self.near["y", step, z].wait_recv()
            piece = part(z * 4 + lax.rem(links.y + 4 - step, 4), cut[1])
            self.far.append(links.send(piece, piece, "y", step))

    def arrive_near(self):
        passed = (("z", 1, 0), ("z", 3, 1), ("y", 1, 0), ("y", 1, 1), ("y", 3, 2), ("y", 3, 3))
        for key, copy in self.near.items():
            if key not in passed:
                copy.wait_recv()

    def arrive(self):
        received(self.far)
        sent(self.near.values())
        if not self.left:
            sent(self.far)
            self.left = True

    def leave(self):
        sent(self.far)
        self.left = True


class RowRing:
    def __init__(self, links, part, first=None):
        self.links, self.part = links, part
        self.first = links.take(4) if first is None else first

    def near(self, step):
        piece = self.part(self.links.x, pl.ds(0, SEQ))
        return self.links.copy(piece, piece, "x", step, self.first + step)

    def start(self):
        self.near(1).start()
        self.near(3).start()

    def pass_on(self):
        for step, h in ((1, 0), (3, 1)):
            self.near(step).wait_recv()
            self.far(h).start()

    def arrive(self):
        self.far(0).wait_recv()
        self.far(1).wait_recv()

    def sent(self):
        for k in range(2):
            self.near(2 * k + 1).wait_send()
            self.far(k).wait_send()

    def far(self, h):
        step = 3 if h else 1
        piece = self.part(lax.rem(self.links.x + 4 - step, 4), pl.ds(64 * h, 64))
        return self.links.copy(piece, piece, "x", step, self.first + 2 * h)


class SumRing:
    def __init__(self, links, part, got):
        self.links, self.part, self.got = links, part, got
        self.first = links.take(6)

    def block(self, step):
        return lax.rem(self.links.x + step, 4)

    def far(self, h):
        rows = pl.ds(64 * h, 64)
        return self.links.copy(
            self.part(self.block(2), rows), self.got.at[1, rows], "x", 2 * h + 1, self.first + h
        )

    def near(self, step, early):
        h = 1 if (step == 1) == early else 0
        rows = pl.ds(64 * h, 64)
        return self.links.copy(
            self.part(self.block(step), rows),
            self.got.at[step - 1, rows],
            "x",
            step,
            self.first + 2 + (step - 1) + (0 if early else 1),
        )

    def start_far(self):
        self.far(0).start()
        self.far(1).start()

    def pass_on(self):
        for h, step in ((0, 1), (1, 3)):
            self.far(h).wait_recv()
            rows = pl.ds(64 * h, 64)
            target = self.part(self.block(step), rows)
            target[...] = (
                target[...].astype(F32) + self.got[1, rows].astype(F32)
            ).astype(BF16)
            self.near(step, False).start()

    def total(self, own):
        for step in (1, 3):
            for early in (True, False):
                self.near(step, early).wait()
        self.far(0).wait_send()
        self.far(1).wait_send()
        return own + self.got[0].astype(F32) + self.got[2].astype(F32)


class PlaneSum:
    def __init__(self, links, part, got, last):
        self.links, self.part, self.got, self.last = links, part, got, last
        self.first = links.take(24)

    def last_copy(self, half, step):
        here = self.links.z if half else self.links.y
        return self.links.copy(
            self.got[half].at[0, lax.rem(here + step, 4)],
            self.last[half].at[step - 1],
            "z" if half else "y",
            step,
            self.first + 17 + 3 * half + step,
        )

    def z_copy(self, step, q, far):
        at = lax.rem(self.links.z + (2 if far else step), 4) * 4 + 2 * q
        return self.links.copy(
            self.part(pl.ds(at, 2), 0),
            self.got[0].at[1 if far else step - 1, pl.ds(2 * q, 2)],
            "z",
            step,
            self.first + 2 * (0 if far else (step + 1) // 2) + q,
        )

    def y_copy(self, step, z, far):
        at = z * 4 + lax.rem(self.links.y + (2 if far else step), 4)
        return self.links.copy(
            self.part(at, 1),
            self.got[1].at[1 if far else step - 1, z],
            "y",
            step,
            self.first + 6 + 4 * (0 if far else (step + 1) // 2) + z,
        )

    def start_far(self, low):
        for z in (low, low + 2):
            self.y_copy(1 if z < 2 else 3, z, True).start()

        @pl.when(lax.rem(self.links.z, 2) == low)
        def _():
            self.z_copy(1, 0, True).start()
            self.z_copy(3, 1, True).start()

    def start_near(self):
        self.z_copy(1, 1, False).start()
        self.z_copy(3, 0, False).start()
        for z in range(4):
            self.y_copy(3 if z < 2 else 1, z, False).start()

    def start(self):
        self.z_copy(1, 0, True).start()
        self.z_copy(3, 1, True).start()
        for z in range(4):
            self.y_copy(1 if z < 2 else 3, z, True).start()
        self.start_near()

    def start_direct(self):
        for step in FAR_FIRST:
            for q in range(2):
                self.z_copy(step, q, step == 2).start()
            for z in range(4):
                self.y_copy(step, z, step == 2).start()

    def pass_on(self):
        for q, step in ((0, 1), (1, 3)):
            self.z_copy(step, q, True).wait_recv()
            at = lax.rem(self.links.z + step, 4) * 4 + 2 * q
            for k in range(2):
                self.add(self.part(at + k, 0), self.got[0].at[1, 2 * q + k])
            self.z_copy(step, q, False).start()
        for z in range(4):
            step = 1 if z < 2 else 3
            self.y_copy(step, z, True).wait_recv()
            at = z * 4 + lax.rem(self.links.y + step, 4)
            self.add(self.part(at, 1), self.got[1].at[1, z])
            self.y_copy(step, z, False).start()

    def add(self, target, what):
        target[...] = (target[...].astype(F32) + what[...].astype(F32)).astype(BF16)

    def second(self, direct=False):
        links, steps = self.links, FAR_FIRST if direct else (1, 3)
        for half in range(2):
            for step in steps:
                if half:
                    for z in range(4):
                        self.y_copy(step, z, step == 2).wait_recv()
                else:
                    for q in range(2):
                        self.z_copy(step, q, step == 2).wait_recv()
            for k in range(4):
                slot = k * 4 + links.y if half else links.z * 4 + k
                total = self.part(slot, half)[...].astype(F32)
                for step in steps:
                    total = total + self.got[half][step - 1, k].astype(F32)
                self.got[half][0, k] = total.astype(BF16)

            for step in FAR_FIRST:
                self.last_copy(half, step).start()

    def total(self, half):
        here = self.links.z if half else self.links.y
        received([self.last_copy(half, step) for step in FAR_FIRST])
        total = self.got[half][0, here].astype(F32)
        for step in range(3):
            total = total + self.last[half][step].astype(F32)
        return total

    def sent(self):
        for far in (True, False):
            for q, step in ((0, 1), (1, 3)):
                self.z_copy(step, q, far).wait_send()
                if not far:
                    self.z_copy(4 - step, q, far).wait_send()
            for z in range(4):
                step = 1 if z < 2 else 3
                self.y_copy(step, z, far).wait_send()
                if not far:
                    self.y_copy(4 - step, z, far).wait_send()
        sent([self.last_copy(half, step) for half in range(2) for step in FAR_FIRST])


INS = (
    "tokens",
    "ids",
    "gain_one",
    "w_qkv",
    "w_out",
    "w_router",
    "gain_two",
    "w_sin",
    "w_sout",
    "e_in",
    "e_out",
    "out_grad",
)
OUTS = {
    "block_out": ((SEQ, D), BF16),
    "tokens_grad": ((SEQ, D), F32),
    "g_gain_one": ((1, ROWS), F32),
    "g_qkv": ((ROWS, 2560), F32),
    "g_out": ((ROWS, D), F32),
    "g_gain_two": ((1, ROWS), F32),
    "g_router": ((EXPERTS, ROWS), F32),
    "g_sin": ((ROWS, 2 * SH), F32),
    "g_sout": ((ROWS, SH), F32),
    "g_ein": ((96, 1024), F32),
    "g_eout": ((96, 512), F32),
}
SCRATCH = {
    "small": ((128, 128), F32),
    "pack": ((4, 16, W_ALL), BF16),
    "arrived": ((4, 16, W_ALL), BF16),
    "dense": ((16, 2, 48, W_ATT), BF16),
    "shared": ((16, 2, 48, W_SHARED), BF16),
    "got": ((16, 96, D), BF16),
    "full": ((8, 2, 96, D), BF16),
    "nat": ((D, D), BF16),
    "normed": ((4, SEQ, D), BF16),
    "qkv": ((4, SEQ, 640), BF16),
    "mix": ((4, SEQ, 384), BF16),
    "send_y": ((4, 2, SEQ, D), BF16),
    "send_x": ((4, 2, SEQ, WIDE), BF16),
    "pair_y": ((4, SEQ, D), BF16),
    "pair_x": ((4, SEQ, WIDE), BF16),
    "got_y": ((3, SEQ, D), BF16),
    "got_x": ((3, SEQ, WIDE), BF16),
    "hidden": ((SEQ, D), F32),
    "probs": ((SEQ, 128), F32),
    "chosen": ((SEQ, 128), F32),
    "rows": ((4, 2, SEQ, WIDE), BF16),
    "cot": ((4, 2, SEQ, D), BF16),
    "gated": ((4, 2, SEQ, 640), BF16),
    "joint": ((4, 2, SEQ, 1280), BF16),
    "low": ((4, SEQ, D), BF16),
    "dsh": ((16, 2, 48, 384), BF16),
    "back": ((48, W_ALL), BF16),
    "e_got0": ((3, 4, 48, D), BF16),
    "e_got1": ((3, 4, 48, D), BF16),
    "e_last0": ((3, 48, D), BF16),
    "e_last1": ((3, 48, D), BF16),
    "d_got0": ((3, 4, 48, 640), BF16),
    "d_got1": ((3, 4, 48, 512), BF16),
    "d_last0": ((3, 48, 640), BF16),
    "d_last1": ((3, 48, 512), BF16),
    "s_got0": ((3, 4, 48, 384), BF16),
    "s_got1": ((3, 4, 48, 384), BF16),
    "s_last0": ((3, 48, 384), BF16),
    "s_last1": ((3, 48, 384), BF16),
}
SENDS, RECEIVES = 164, 254
PAIRS = (((0, 0), (0, 1)), ((1, 0), (3, 0)), ((2, 0), (2, 1)), ((1, 1), (3, 1)))


class Bag:
    pass


def causal_probs(q, k):
    scores = dot_nt(q, k) * HD**-0.5
    row = lax.broadcasted_iota(jnp.int32, (SEQ, SEQ), 0)
    col = lax.broadcasted_iota(jnp.int32, (SEQ, SEQ), 1)
    scores = jnp.where(col <= row, scores, -1e30)
    exponent = jnp.exp(scores - jnp.max(scores, axis=1, keepdims=True))
    return exponent * (1.0 / jnp.sum(exponent, axis=1, keepdims=True))


def kernel(*refs):
    b = Bag()
    names = [*INS, *(name + "_result" for name in OUTS), *OUTS, *SCRATCH]
    for name, ref in zip(names, refs):
        setattr(b, name, ref)
    links = Links(*refs[len(names) :])
    x, y, z, c = links.x, links.y, links.z, links.c
    other = 1 - c
    results = []
    kept = links.take(links.kept)

    def deliver(*ready):
        for name in ready:
            results.append(links.local(getattr(b, name), getattr(b, name + "_result")))

    here = z * 4 + y
    mine = 2 * x + c
    every = pl.ds(0, 48)
    e_cut = ((pl.ds(0, 48),), (pl.ds(48, 48),))
    d_cut = ((every, pl.ds(0, 640)), (every, pl.ds(640, 512)))
    s_cut = ((every, pl.ds(0, 384)), (every, pl.ds(384, 384)))
    d_part = lambda slots, half: b.dense.at[(slots, c, *half)]
    s_part = lambda slots, half: b.shared.at[(slots, c, *half)]
    e_part = lambda slots, half: b.got.at[(slots, *half)]

    greeted = links.greet("xyzc")
    b.got[here, :, 0:1024] = b.e_in[...]
    b.got[here, :, 1024:1536] = b.e_out[...]
    b.pack[...] = jnp.zeros_like(b.pack)
    b.small[...] = jnp.zeros_like(b.small)
    b.small[0:EXPERTS, 0:ROWS] = b.w_router[...].astype(F32)
    b.small[8:9, 0:ROWS] = b.gain_two[...].astype(F32)
    b.small[9:10, 0:ROWS] = b.gain_one[...].astype(F32)
    small = b.small[...].T
    lane = lax.broadcasted_iota(jnp.int32, (SEQ, 128), 1)
    row = lax.broadcasted_iota(jnp.int32, (SEQ, 128), 0)
    named = jnp.zeros((SEQ, 128), F32)
    for k in range(TOP):
        named = named + (b.ids[k : k + 1, :] == row).astype(F32)
    b.chosen[...] = named.T
    gain_one = small[0:ROWS, 9:10]
    for k in range(4):
        for start, width, at in ((k * 384, 384, 0), (D + k * 128, 128, 384), (2048 + k * 128, 128, 512)):
            b.pack[k, 0:ROWS, at : at + width] = (
                b.w_qkv[:, start : start + width].astype(F32) * gain_one
            ).astype(BF16)
        b.pack[k, 0:ROWS, 640:1024] = b.w_out[:, k * 384 : k * 384 + 384]
        b.pack[k, 0:ROWS, 1024:1152] = small[0:ROWS].astype(BF16)
        for core in range(2):
            at, unit = W_ATT + 384 * core, (2 * k + core) * 128
            b.pack[k, 0:ROWS, at : at + 128] = b.w_sin[:, unit : unit + 128]
            b.pack[k, 0:ROWS, at + 128 : at + 256] = b.w_sin[:, SH + unit : SH + unit + 128]
            b.pack[k, 0:ROWS, at + 256 : at + 384] = b.w_sout[:, unit : unit + 128]
    greeted()

    def exchange(cols):
        return [
            links.send(
                b.pack.at[lax.rem(x + step, 4), :, cols], b.arrived.at[x, :, cols], "x", step
            )
            for step in FAR_FIRST
        ]

    exchanged = exchange(pl.ds(0, W_ATT))
    e_cols = lambda cols: tuple((rows, cols) for (rows,) in e_cut)
    e_first = gather_first(links, b.got.at[here], e_part, here, e_cols(pl.ds(0, 1024)))
    inputs = b.tokens[...].astype(F32)
    inverse_one = lax.rsqrt(jnp.mean(inputs * inputs, axis=1, keepdims=True) + epsilon)
    b.normed[x] = (inputs * inverse_one).astype(BF16)
    b.cot[x, c] = b.out_grad[...]
    cot_pair = links.send(b.cot.at[x, c], b.cot.at[x, c], "c", 1)
    b.arrived[x] = b.pack[x]
    finish(exchanged)
    exchanged = exchange(pl.ds(W_ATT, W_SHARED))
    normed_ring = RowRing(links, lambda s, rows: b.normed.at[s, rows])
    cot_ring = RowRing(links, lambda s, rows: b.cot.at[s, c, rows])
    normed_ring.start()
    pick = pick_matrix((48, 64), lambda row: row // ROWS * 16 + row % ROWS)
    for col in range(0, W_ATT, 384):
        block = moved(pick, b.arrived[:, :, col : col + 384].reshape(64, 384))
        b.dense[here, c, :, col : col + 384] = block

    d_first = gather_first(links, b.dense.at[here, c], d_part, here, d_cut)
    sent(d_first)
    e_first += gather_first(links, b.got.at[here], e_part, here, e_cols(pl.ds(1024, 512)))
    d_ring = PlaneRing(links, d_first, d_part, d_cut)
    normed_ring.pass_on()
    cot_ring.start()
    d_ring.pass_on()
    d_ring.leave()
    finish(exchanged)
    for col in range(W_ATT, W_ALL, 384):
        block = moved(pick, b.arrived[:, :, col : col + 384].reshape(64, 384))
        b.shared[here, c, :, col - W_ATT : col - W_ATT + 384] = block
    s_first = gather_first(links, b.shared.at[here, c], s_part, here, s_cut)
    d_ring.arrive_near()
    d_ring.arrive()
    d_pair = links.take(8)

    def d_forward(j):
        piece = b.dense.at[pl.ds(2 * j, 2), c]
        return links.copy(piece, piece, "c", 1, d_pair + j)

    for j in range(8):
        d_forward(j).start()
    e_ring = PlaneRing(links, e_first, e_part, e_cut)
    s_ring = PlaneRing(links, s_first, s_part, s_cut)
    normed_ring.arrive()

    order = pick_matrix(
        (192, 192), lambda row: row % 48 // ROWS * 48 + row // 48 * ROWS + row % ROWS
    )

    def to_rows(j, source, start, at, width):
        piece = source[pl.ds(2 * j, 2), :, :, start].reshape(192, width)
        piece = moved(order, piece)
        for k in range(4):
            row = pl.multiple_of(k * 384 + j * 48, 16)
            b.nat[pl.ds(row, 48), at : at + width] = piece[k * 48 : k * 48 + 48]

    def to_blocks(j, target, at, width):
        pieces = [
            b.nat[pl.ds(pl.multiple_of(k * 384 + j * 48, 16), 48), at : at + width]
            for k in range(4)
        ]
        piece = moved(order, jnp.concatenate(pieces, axis=0))
        target[pl.ds(2 * j, 2)] = piece.reshape(2, 2, 48, width)

    @pl.loop(0, 8)
    def _(j):
        d_forward(j).wait()
        to_rows(j, b.dense, pl.ds(0, W_ATT), 0, W_ATT)

    mix_ring = SumRing(links, lambda s, rows: b.send_y.at[s, 0, rows], b.got_y)

    def attend(sequences):
        for s in sequences:
            b.qkv[s] = dot(b.normed[s], b.nat[:, 0:640]).astype(BF16)
        for h in range(3):
            head = slice(h * HD, (h + 1) * HD)
            for s in sequences:
                probs = causal_probs(b.qkv[s, :, head], b.qkv[s, :, 384:512])
                b.mix[s, :, head] = dot(probs.astype(BF16), b.qkv[s, :, 512:640]).astype(BF16)
        for s in sequences:
            for n in range(2):
                rows = slice(n * 768, (n + 1) * 768)
                b.send_y[s, 0, :, rows] = dot_nt(b.mix[s], b.nat[rows, 640:1024]).astype(BF16)

    right, left, far = (lax.rem(x + step, 4) for step in (1, 3, 2))
    attend([far])
    mix_ring.start_far()
    attend([right, left])
    mix_ring.near(1, True).start()
    mix_ring.near(3, True).start()
    mix_ring.pass_on()
    attend([x])

    e_ring.pass_on()
    s_ring.pass_on()
    cot_ring.pass_on()
    e_hands = []
    lower, upper = pl.ds(0, 48), pl.ds(48, 48)
    for k in range(2):
        for half, to_other in ((other, True), (c, False)):
            at = 2 * half + k
            pieces = [
                (at == lax.rem(z + 2, 4), b.got.at[pl.ds(at * 4, 4), lower], pl.ds(4 * k, 4), lower)
            ]
            for to in range(4):
                pieces.append(
                    (to == lax.rem(y + 2, 4), b.got.at[at * 4 + to, upper], 4 * k + to, upper)
                )
            for is_far, source, slots, rows in pieces:
                target = b.full.at[slots, c, rows]
                if to_other:
                    copy = links.copy(source, target, "c", 1, links.take(1))
                else:
                    copy = links.local_copy(source, target)
                e_hands.append((is_far, copy))

    def e_hand(far_ones):
        for is_far, copy in e_hands:

            @pl.when(is_far == far_ones)
            def _():
                copy.start()

    e_ring.arrive_near()
    e_hand(False)

    hidden = mix_ring.total(b.tokens[...].astype(F32) + b.send_y[x, 0].astype(F32))
    b.hidden[...] = hidden
    inverse_two = lax.rsqrt(jnp.mean(hidden * hidden, axis=1, keepdims=True) + epsilon)
    lane8 = lax.broadcasted_iota(jnp.int32, (8, 128), 1)
    gain_two = dot_nt((lane8 == 8).astype(BF16), b.nat[:, 1024:1152])[0:1]
    moe_in = (hidden * inverse_two * gain_two).astype(BF16)
    b.rows[x, c, :, 0:D] = moe_in
    logits = jnp.where(lane < EXPERTS, dot(moe_in, b.nat[:, 1024:1152]), -1e30)
    exponent = jnp.exp(logits - jnp.max(logits, axis=1, keepdims=True))
    router_probs = exponent / jnp.sum(exponent, axis=1, keepdims=True)
    b.probs[...] = router_probs
    gates = b.chosen[...] * router_probs
    high = gates.astype(BF16).astype(F32)
    b.rows[x, c, :, D:WIDE] = (high + pltpu.roll(gates - high, 8, 1)).astype(BF16)
    rows_ring = RowRing(links, lambda s, rows: b.rows.at[s, c, rows], kept)
    rows_ring.start()
    pair_rows, pair_cot = kept + 4, kept + 8
    forward_rows = lambda s, d: links.copy(
        b.rows.at[s, c], b.rows.at[s, c], "c", 1, pair_rows + d
    )
    forward_cot = lambda s, d: links.copy(b.cot.at[s, c], b.cot.at[s, c], "c", 1, pair_cot + d)
    forward_rows(x, 0).start()
    e_ring.arrive()
    e_hand(True)
    sent(e_first + s_first)
    s_ring.arrive_near()
    s_ring.arrive()
    half = pl.ds(pl.multiple_of(other * 384, 128), 384)
    s_pair = links.send(b.shared.at[:, c, :, half], b.shared.at[:, c, :, half], "c", 1)

    for _, copy in e_hands:
        copy.wait()

    def shared_rows():
        s_pair.wait()

        @pl.loop(0, 8)
        def _(j):
            to_rows(j, b.shared, pl.ds(pl.multiple_of(c * 384, 128), 384), W_ATT, 384)

    links.left()
    back_pair = links.take(8)
    sum_pair = links.take(4)
    parts = (pl.ds(0, 768), pl.ds(768, WIDE - 768))
    back_forward = lambda s, d, n: links.copy(
        b.send_x.at[s, other, :, parts[n]], b.pair_x.at[s, :, parts[n]], "c", 1, back_pair + 2 * d + n
    )
    sum_forward = lambda s, d: links.copy(
        b.send_y.at[s, other], b.pair_y.at[s], "c", 1, sum_pair + d
    )
    back_ring = SumRing(links, lambda s, rows: b.send_x.at[s, c, rows], b.got_x)
    sum_ring = SumRing(links, lambda s, rows: b.send_y.at[s, c, rows], b.got_y)
    cot_pair.wait()

    normed_ring.sent()
    cot_ring.sent()
    cot_ring.arrive()
    for d in range(1, 4):
        forward_cot(lax.rem(x + d, 4), d).start()
    forward_rows(x, 0).wait_recv()

    def which(i, core):
        sides = ((i == 1) & (core == 0)) | ((i == 3) & (core == 1))
        return ((0, i == 0), (1, sides), (3, sides), (2, i == 2))

    def give_pair(i, n):
        for d, now in which(i, other):

            @pl.when(now)
            def _():
                back_forward(lax.rem(x + d, 4), d, n).start()

    def add_pair(i, n):
        for d, now in which(i, c):
            s = lax.rem(x + d, 4)

            @pl.when(now)
            def _():
                back_forward(s, d, n).wait_recv()
                b.send_x[s, c, :, parts[n]] = (
                    b.send_x[s, c, :, parts[n]].astype(F32) + b.pair_x[s, :, parts[n]].astype(F32)
                ).astype(BF16)
                if n and d == 2:
                    back_ring.start_far()
                elif n and d:
                    back_ring.near(d, True).start()

    def pair_of(i):
        def chosen(k, what):
            values = [PAIRS[step][k][what] for step in range(4)]
            result = values[3]
            for step in range(3):
                result = jnp.where(i == step, values[step], result)
            return result

        return [(lax.rem(x + chosen(k, 0), 4), chosen(k, 1)) for k in range(2)]

    def both(i, ref, cols):
        return jnp.concatenate([ref[s, core, :, cols] for s, core in pair_of(i)], axis=0)

    def keep(i, ref, cols, value):
        for k, (s, core) in enumerate(pair_of(i)):
            ref[s, core, :, cols] = value[k * SEQ : (k + 1) * SEQ]

    def row_grads(i):
        slopes = both(i, b.joint, slice(0, 1280))
        for n in range(2):
            rows = slice(n * 768, (n + 1) * 768)
            result = dot_nt(
                slopes[:, 0:1024], b.full[4 * n : 4 * n + 4, :, :, 0:1024].reshape(768, 1024)
            ) + dot_nt(slopes[:, 1024:1280], b.nat[rows, 1152:1408])
            keep(i, b.send_x, rows, result.astype(BF16))
            give_pair(i, n)
            if n == 0:

                @pl.when(i == 1)
                def _():
                    rows_ring.arrive()
                    forward_rows(lax.rem(x + 2, 4), 2).start()

    @pl.loop(0, 4)
    def _(i):
        for k, far_ones in ((1, (1, 3)), (2, (2,))):

            @pl.when(i == k)
            def _():
                for d in far_ones:
                    forward_cot(lax.rem(x + d, 4), d).wait_recv()
                    forward_rows(lax.rem(x + d, 4), d).wait_recv()

        @pl.when(i > 0)
        def _():
            add_pair(i - 1, 0)

        tokens = both(i, b.rows, slice(0, D))
        grads = both(i, b.cot, slice(0, D))
        lanes = lax.broadcasted_iota(jnp.int32, (256, 128), 1)
        gate = both(i, b.rows, slice(D, WIDE)).astype(F32)
        gate = jnp.where((lanes == mine) | (lanes == mine + 8), gate, 0.0)
        gate = jnp.sum(gate, axis=1, keepdims=True)
        gate_grad = jnp.zeros((256, 1), F32)
        for part in range(3):
            if part < 2:
                at, width = part * 256, 256
                g = dot(tokens, b.full[:, :, :, at : at + 256].reshape(D, 256))
                u = dot(tokens, b.full[:, :, :, at + 512 : at + 768].reshape(D, 256))
                a = dot(grads, b.full[:, :, :, at + 1024 : at + 1280].reshape(D, 256))
                first, second, scale = at, at + 512, gate
            else:

                @pl.when(i == 0)
                def _():
                    shared_rows()

                at, width = 512, 128
                gu = dot(tokens, b.nat[:, 1152:1408])
                g, u = gu[:, 0:128], gu[:, 128:256]
                a = dot(grads, b.nat[:, 1408:1536])
                first, second, scale = 1024, 1152, None
            g = g.astype(BF16).astype(F32)
            u = u.astype(BF16).astype(F32)
            sg = jax.nn.sigmoid(g)
            act = (g * sg * u).astype(BF16)
            if scale is not None:
                gate_grad = gate_grad + jnp.sum(act.astype(F32) * a, axis=1, keepdims=True)
                act = (act.astype(F32) * scale).astype(BF16)
                a = a * scale
            keep(i, b.gated, slice(at, at + width), act)
            keep(
                i,
                b.joint,
                slice(first, first + width),
                (a * u * (sg * (1.0 + g * (1.0 - sg)))).astype(BF16),
            )
            keep(i, b.joint, slice(second, second + width), (a * g * sg).astype(BF16))
        gate_high = gate_grad.astype(BF16).astype(F32)
        spread = jnp.where(lanes == mine, gate_high, 0.0)
        spread = spread + jnp.where(lanes == mine + 8, gate_grad - gate_high, 0.0)
        keep(i, b.send_x, slice(D, WIDE), spread.astype(BF16))

        @pl.when(i > 0)
        def _():
            add_pair(i - 1, 1)

        @pl.when(i == 0)
        def _():
            rows_ring.pass_on()
            for d in (1, 3):
                forward_rows(lax.rem(x + d, 4), d).start()

        row_grads(i)

    add_pair(3, 0)
    add_pair(3, 1)


    e_sum = PlaneSum(
        links,
        lambda slots, half: b.got.at[slots, pl.ds(48 * half, 48)],
        (b.e_got0, b.e_got1),
        (b.e_last0, b.e_last1),
    )
    e_moves = []

    def e_start(low):
        finish(e_moves[low])
        e_sum.start_far(low)

    for low in range(2):
        for n in (2 * low, 2 * low + 1):
            if n == 3:
                e_start(0)
            cols = slice(n * 384, (n + 1) * 384)
            tokens = b.rows[:, :, :, cols].reshape(1024, 384)
            for at in (0, 512):
                result = dot_tn(tokens, b.joint[:, :, :, at : at + 512].reshape(1024, 512))
                b.full[2 * n : 2 * n + 2, :, :, at : at + 512] = result.astype(BF16).reshape(
                    2, 2, 96, 512
                )
            grads = b.cot[:, :, :, cols].reshape(1024, 384)
            result = dot_tn(grads, b.gated[:, :, :, 0:512].reshape(1024, 512))
            result = result.astype(BF16).reshape(2, 2, 2, 48, 512)
            for h in range(2):
                b.dense[8 * h + 2 * n : 8 * h + 2 * n + 2, :, :, 0:512] = result[:, :, h]
        four = pl.ds(4 * low, 4)
        target = pl.ds(8 * c + 4 * low, 4)
        wide, slim = pl.ds(0, 1024), pl.ds(1024, 512)
        moves = [
            links.send(b.full.at[four, other, :, wide], b.got.at[target, :, wide], "c", 1),
            links.local(b.full.at[four, c, :, wide], b.got.at[target, :, wide]),
        ]
        for h in range(2):
            rows, slots = pl.ds(48 * h, 48), pl.ds(8 * h + 4 * low, 4)
            moves += [
                links.send(
                    b.dense.at[slots, other, :, pl.ds(0, 512)], b.got.at[target, rows, slim], "c", 1
                ),
                links.local(b.dense.at[slots, c, :, pl.ds(0, 512)], b.got.at[target, rows, slim]),
            ]
        e_moves.append(moves)
        if not low:
            back_ring.pass_on()

    e_start(1)

    moe_back = back_ring.total(b.send_x[x, c].astype(F32))
    raw = moe_back[:, D:WIDE]
    router_probs = b.probs[...]
    prob_grad = b.chosen[...] * (raw + pltpu.roll(raw, 120, 1))
    logit_grad = router_probs * (
        prob_grad - jnp.sum(router_probs * prob_grad, axis=1, keepdims=True)
    )
    logit_grad = logit_grad.astype(BF16)
    gain_two = dot_nt((lane8 == 8).astype(BF16), b.nat[:, 1024:1152])[0:1]
    moe_in_grad = moe_back[:, 0:D] + dot_nt(logit_grad, b.nat[:, 1024:1152])
    hidden = b.hidden[...]
    inverse_two = lax.rsqrt(jnp.mean(hidden * hidden, axis=1, keepdims=True) + epsilon)
    scaled = gain_two * moe_in_grad
    hidden_grad = (
        b.out_grad[...].astype(F32)
        + inverse_two * scaled
        - hidden
        * (inverse_two * inverse_two * inverse_two)
        * jnp.mean(scaled * hidden, axis=1, keepdims=True)
    )
    b.tokens_grad[...] = hidden_grad
    b.low[x] = hidden_grad.astype(BF16)
    low_ring = RowRing(links, lambda s, rows: b.low.at[s, rows])
    low_ring.start()
    e_sum.start_near()
    misc_grad = dot_tn(b.rows[x, c, :, 0:D], logit_grad) + dot_tn(
        (moe_in_grad * hidden * inverse_two).astype(BF16), (lane == 8).astype(BF16)
    )
    b.nat[:, 1024:1152] = misc_grad.astype(BF16)

    @pl.loop(0, 4)
    def _(d):
        s = lax.rem(x + d, 4)
        for n in range(2):
            rows = slice(n * 768, (n + 1) * 768)
            result = dot_nt(
                b.gated[s, :, :, 0:512].reshape(256, 512), b.full[4 * n : 4 * n + 4, :, :, 1024:1536].reshape(768, 512)
            ) + dot_nt(b.gated[s, :, :, 512:640].reshape(256, 128), b.nat[rows, 1408:1536])
            b.send_y[s, :, :, rows] = result.astype(BF16).reshape(2, SEQ, 768)
        sum_forward(s, d).start()

    for n in range(4):
        cols = slice(n * 384, (n + 1) * 384)
        tokens = b.rows[:, :, :, cols].reshape(1024, 384)
        result = dot_tn(tokens, b.joint[:, :, :, 1024:1280].reshape(1024, 256))
        b.nat[cols, 1152:1408] = result.astype(BF16)
        grads = b.cot[:, :, :, cols].reshape(1024, 384)
        result = dot_tn(grads, b.gated[:, :, :, 512:640].reshape(1024, 128))
        b.nat[cols, 1408:1536] = result.astype(BF16)

    @pl.loop(0, 8)
    def _(j):
        to_blocks(j, b.dsh, W_ATT, 384)

    half = pl.ds(pl.multiple_of(c * 384, 128), 384)
    for d in range(1, 4):
        forward_cot(lax.rem(x + d, 4), d).wait_send()
    s_give = links.send(b.dsh.at[:, other], b.shared.at[:, 0, :, half], "c", 1)
    s_keep = links.local(b.dsh.at[:, c], b.shared.at[:, 0, :, half])
    s_sum = PlaneSum(
        links,
        lambda slots, half: b.shared.at[slots, 0, :, pl.ds(384 * half, 384)],
        (b.s_got0, b.s_got1),
        (b.s_last0, b.s_last1),
    )

    e_sum.pass_on()
    norm_ring = SumRing(
        links,
        lambda s, rows: b.send_x.at[s, 0, rows, pl.ds(0, D)],
        b.got_x.at[:, :, pl.ds(0, D)],
    )
    for d in range(4):
        for n in range(2):
            back_forward(lax.rem(x + d, 4), d, n).wait_send()

    def attend_back(sequences):
        mix_grads, parts_of = [], []
        for s in sequences:
            mix_grads.append(dot(b.low[s], b.nat[:, 640:1024]).astype(BF16))
            parts_of.append((jnp.zeros((SEQ, HD), F32), jnp.zeros((SEQ, HD), F32)))
        for h in range(3):
            head = slice(h * HD, (h + 1) * HD)
            for k, s in enumerate(sequences):
                key_grad, value_grad = parts_of[k]
                key, value = b.qkv[s, :, 384:512], b.qkv[s, :, 512:640]
                query = b.qkv[s, :, head]
                mixed = mix_grads[k][:, head]
                probs = causal_probs(query, key)
                dprob = dot_nt(mixed, value)
                value_grad = value_grad + dot_tn(probs.astype(BF16), mixed)
                delta = jnp.sum(probs * dprob, axis=1, keepdims=True)
                score_grad = (probs * (dprob - delta)).astype(BF16)
                b.qkv[s, :, head] = (dot(score_grad, key) * HD**-0.5).astype(BF16)
                parts_of[k] = (key_grad + dot_tn(score_grad, query), value_grad)
        for k, s in enumerate(sequences):
            key_grad, value_grad = parts_of[k]
            b.qkv[s, :, 384:512] = (key_grad * HD**-0.5).astype(BF16)
            b.qkv[s, :, 512:640] = value_grad.astype(BF16)

    def normed_back(sequences):
        for s in sequences:
            for n in range(2):
                rows = slice(n * 768, (n + 1) * 768)
                b.send_x[s, 0, :, rows] = dot_nt(b.qkv[s], b.nat[rows, 0:640]).astype(BF16)

    attend_back([x])
    low_ring.pass_on()
    normed_back([x])
    attend_back([right, left])
    normed_back([right, left])
    norm_ring.near(1, True).start()
    norm_ring.near(3, True).start()
    s_give.wait()
    s_keep.wait()
    s_sum.start()
    low_ring.arrive()
    attend_back([far])
    normed_back([far])
    norm_ring.start_far()

    for d in (2, 1, 3, 0):
        s = lax.rem(x + d, 4)
        sum_forward(s, d).wait()
        b.send_y[s, c] = (b.send_y[s, c].astype(F32) + b.pair_y[s].astype(F32)).astype(BF16)
        if d == 2:
            sum_ring.start_far()
        elif d:
            sum_ring.near(d, True).start()
    e_sum.second()
    d_base = links.take(8)

    def d_landing(j):
        rows = pl.ds(pl.multiple_of(lax.div(j, 4) * 48, 16), 48)
        return b.cot.at[lax.rem(j, 4), :, rows, pl.ds(0, W_ATT)]

    d_give = lambda j: links.copy(
        b.dense.at[pl.ds(2 * j, 2), other], d_landing(j), "c", 1, d_base + j
    )

    for n in range(4):
        cols = slice(n * 384, (n + 1) * 384)
        result = dot_tn(b.normed[:, :, cols].reshape(512, 384), b.qkv[...].reshape(512, 640))
        b.nat[cols, 0:640] = result.astype(BF16)
        result = dot_tn(b.low[:, :, cols].reshape(512, 384), b.mix[...].reshape(512, 384))
        b.nat[cols, 640:1024] = result.astype(BF16)

    @pl.loop(0, 8)
    def _(j):
        to_blocks(j, b.dense, 0, W_ATT)
        d_give(j).start()

    s_sum.pass_on()

    @pl.loop(0, 8)
    def _(j):
        d_give(j).wait()
        total = b.dense[pl.ds(2 * j, 2), c].astype(F32) + d_landing(j)[...].astype(F32)
        b.dense[pl.ds(2 * j, 2), c] = total.astype(BF16)

    d_sum = PlaneSum(
        links,
        lambda slots, half: d_part(slots, d_cut[half]),
        (b.d_got0, b.d_got1),
        (b.d_last0, b.d_last1),
    )
    d_sum.start_direct()

    s_sum.second()
    norm_ring.pass_on()

    scaled = norm_ring.total(b.send_x[x, 0, :, 0:D].astype(F32))
    inputs = b.tokens[...].astype(F32)
    inverse_one = lax.rsqrt(jnp.mean(inputs * inputs, axis=1, keepdims=True) + epsilon)
    b.tokens_grad[...] = (
        b.tokens_grad[...]
        + inverse_one * scaled
        - inputs
        * (inverse_one * inverse_one * inverse_one)
        * jnp.mean(scaled * inputs, axis=1, keepdims=True)
    )
    deliver("tokens_grad")


    d_sum.second(direct=True)
    sum_ring.pass_on()
    for part in range(2):
        at = W_ATT + 384 * part
        b.back[:, at : at + 384] = s_sum.total(part).astype(BF16)
    for part, cols in ((0, slice(0, 640)), (1, slice(640, 1152))):
        b.back[:, cols] = d_sum.total(part).astype(BF16)
    pick = pick_matrix((64, 48), lambda row: jnp.where(row % 16 < ROWS, row // 16 * ROWS + row % 16, -1))
    for col in range(0, W_ALL, 384):
        b.pack[:, :, col : col + 384] = moved(pick, b.back[:, col : col + 384]).reshape(4, 16, 384)
    exchanged = exchange(pl.ds(0, W_ALL))
    b.arrived[x] = b.pack[x]
    for part in range(2):
        rows = slice(48 * part, 48 * part + 48)
        total = e_sum.total(part)
        b.g_ein[rows] = total[:, 0:1024]
        b.g_eout[rows] = total[:, 1024:1536]
    deliver("g_ein", "g_eout")
    result = sum_ring.total(b.hidden[...] + b.send_y[x, c].astype(F32))
    b.block_out[...] = result.astype(BF16)
    deliver("block_out")

    for ring in (rows_ring, low_ring):
        ring.sent()
    for d in range(4):
        forward_rows(lax.rem(x + d, 4), d).wait_send()
    for plane_sum in (e_sum, s_sum, d_sum):
        plane_sum.sent()
    received(exchanged)
    gain_grad = jnp.zeros((ROWS, 1), F32)
    misc = jnp.zeros((ROWS, 128), F32)
    for k in range(4):
        piece = b.arrived[k].astype(F32)[0:ROWS]
        for start, width, at in ((k * 384, 384, 0), (D + k * 128, 128, 384), (2048 + k * 128, 128, 512)):
            raw = piece[:, at : at + width]
            gain_grad = gain_grad + jnp.sum(
                raw * b.w_qkv[:, start : start + width].astype(F32), axis=1, keepdims=True
            )
            b.g_qkv[:, start : start + width] = raw * gain_one
        b.g_out[:, k * 384 : k * 384 + 384] = piece[:, 640:1024]
        misc = misc + piece[:, 1024:1152]
        for core in range(2):
            at, unit = W_ATT + 384 * core, (2 * k + core) * 128
            b.g_sin[:, unit : unit + 128] = piece[:, at : at + 128]
            b.g_sin[:, SH + unit : SH + unit + 128] = piece[:, at + 128 : at + 256]
            b.g_sout[:, unit : unit + 128] = piece[:, at + 256 : at + 384]
    b.small[0:ROWS] = jnp.where(lane[0:ROWS] == 9, gain_grad, misc)
    small = b.small[...].T
    b.g_router[...] = small[0:EXPERTS, 0:ROWS]
    b.g_gain_two[...] = small[8:9, 0:ROWS]
    b.g_gain_one[...] = small[9:10, 0:ROWS]
    sent(exchanged)
    deliver("g_gain_one", "g_qkv", "g_out", "g_gain_two", "g_router", "g_sin", "g_sout")
    finish(results)


def hand_over(*refs):
    n = len(OUTS)
    sources, targets, held, sems = refs[:n], refs[n : 2 * n], refs[2 * n : 3 * n], refs[3 * n]
    reads = [pltpu.make_async_copy(sources[i], held[i], sems.at[0, i]) for i in range(n)]
    writes = [pltpu.make_async_copy(held[i], targets[i], sems.at[1, i]) for i in range(n)]
    for read in reads:
        read.start()
    for read, write in zip(reads, writes):
        read.wait()
        write.start()
    finish(writes)


def local(
    tokens,
    expert_ids,
    attn_gain,
    w_qkv,
    w_out,
    moe_gain,
    w_router,
    w_shared_in,
    w_shared_out,
    w_expert_in,
    w_expert_out,
    out_grad,
):
    results = pl.pallas_call(
        kernel,
        out_shape=[jax.ShapeDtypeStruct(shape, dtype) for shape, dtype in OUTS.values()],
        in_specs=[pl.BlockSpec(memory_space=pltpu.VMEM)] * len(INS),
        out_specs=[pl.BlockSpec(memory_space=pl.ANY)] * len(OUTS),
        scratch_shapes=[
            *[pltpu.VMEM(shape, dtype) for shape, dtype in OUTS.values()],
            *[pltpu.VMEM(shape, dtype) for shape, dtype in SCRATCH.values()],
            pltpu.SemaphoreType.DMA((SENDS,)),
            pltpu.SemaphoreType.DMA((RECEIVES,)),
        ],
        compiler_params=pltpu.CompilerParams(
            collective_id=1, has_side_effects=True, vmem_limit_bytes=(64 << 20) - (1 << 16)
        ),
        cost_estimate=pl.CostEstimate(
            flops=23_000_000_000, bytes_accessed=10_000_000, transcendentals=2_000_000
        ),
        name="block",
    )(
        tokens,
        expert_ids.T,
        attn_gain[None],
        w_qkv,
        w_out,
        w_router.T,
        moe_gain[None],
        w_shared_in,
        w_shared_out,
        w_expert_in,
        w_expert_out,
        out_grad,
    )
    results = pl.pallas_call(
        hand_over,
        out_shape=[jax.ShapeDtypeStruct(shape, dtype) for shape, dtype in OUTS.values()],
        in_specs=[pl.BlockSpec(memory_space=pl.ANY)] * len(OUTS),
        out_specs=[pl.BlockSpec(memory_space=pl.ANY)] * len(OUTS),
        scratch_shapes=[
            *[pltpu.VMEM(shape, dtype) for shape, dtype in OUTS.values()],
            pltpu.SemaphoreType.DMA((2, len(OUTS))),
        ],
        name="hand_over",
    )(*results)
    block_out, tokens_grad, gain_one, qkv, out, gain_two, router, sin, sout, ein, eout = results
    return (
        block_out,
        tokens_grad,
        gain_one[0],
        qkv,
        out,
        gain_two[0],
        router.T,
        sin,
        sout,
        ein,
        eout,
    )


def solution(mesh):
    wide, flat = P("fsdp", None), P("fsdp")
    return jax.shard_map(
        local,
        mesh=mesh,
        in_specs=(wide, wide, flat, wide, wide, flat, wide, wide, wide, wide, wide, wide),
        out_specs=(wide, wide, flat, wide, wide, flat, wide, wide, wide, wide, wide),
        check_vma=False,
    )
```

```python
import jax
import jax.numpy as jnp
from jax import lax
from jax.experimental import pallas as pl
from jax.experimental.pallas import tpu as pltpu
from jax.sharding import PartitionSpec as P

D = 1536
HD = 128
SH = 1024
EXPERTS = 8
TOP = 6
ROWS = 12
SEQ = 128
W_ATT = 1152
W_SHARED = 768
W_ALL = W_ATT + W_SHARED
WIDE = D + 128
epsilon = 1e-05
MESH = pl.DeviceIdType.MESH
F32 = jnp.float32
BF16 = jnp.bfloat16
STRIDE = {"x": (32, 4), "z": (8, 4), "y": (2, 4), "c": (1, 2)}
FAR_FIRST = (2, 1, 3)
NEAR_FIRST = (1, 3, 2)


def place(me, axis):
    stride, size = STRIDE[axis]
    return lax.rem(lax.div(me, stride), size)


def peer(me, axis, step):
    stride, size = STRIDE[axis]
    here = place(me, axis)
    return me + (lax.rem(here + step, size) - here) * stride


class Links:
    def __init__(self, send_sem, recv_sem):
        self.me = lax.axis_index("fsdp")
        self.send_sem, self.recv_sem = send_sem, recv_sem
        self.count = self.locals = 0
        self.again, self.kept = None, 12
        self.x, self.y, self.z, self.c = (place(self.me, axis) for axis in "xyzc")

    def take(self, number):
        first = self.count
        self.count += number
        return first

    def left(self):
        self.again = self.count

    def sender(self, sem):
        again = self.again is not None and (not isinstance(sem, int) or sem >= self.again)
        return self.send_sem.at[sem - self.again + self.kept if again else sem]

    def copy(self, src, dst, axis, step, sem):
        return pltpu.make_async_remote_copy(
            src_ref=src,
            dst_ref=dst,
            send_sem=self.sender(sem),
            recv_sem=self.recv_sem.at[sem],
            device_id=(peer(self.me, axis, step),),
            device_id_type=MESH,
        )

    def send(self, src, dst, axis, step):
        copy = self.copy(src, dst, axis, step, self.take(1))
        copy.start()
        return copy

    def local(self, src, dst):
        copy = self.local_copy(src, dst)
        copy.start()
        return copy

    def local_copy(self, src, dst):
        self.locals += 1
        return pltpu.make_async_copy(src, dst, self.send_sem.at[SENDS - self.locals])

    def greet(self, axes):
        barrier = pltpu.get_barrier_semaphore()
        total = 0
        for axis in axes:
            for step in range(1, STRIDE[axis][1]):
                pl.semaphore_signal(
                    barrier, inc=1, device_id=(peer(self.me, axis, step),), device_id_type=MESH
                )
                total += 1
        return lambda: pl.semaphore_wait(barrier, total)


def finish(copies):
    for copy in copies:
        copy.wait()


def received(copies):
    for copy in copies:
        copy.wait_recv()


def sent(copies):
    for copy in copies:
        copy.wait_send()


def dot(a, b):
    return jnp.dot(a, b, preferred_element_type=F32)


def dot_nt(a, b):
    return lax.dot_general(a, b, (((1,), (1,)), ((), ())), preferred_element_type=F32)


def dot_tn(a, b):
    return lax.dot_general(a, b, (((0,), (0,)), ((), ())), preferred_element_type=F32)


def pick_matrix(shape, source):
    row = lax.broadcasted_iota(jnp.int32, shape, 0)
    col = lax.broadcasted_iota(jnp.int32, shape, 1)
    return (col == source(row)).astype(BF16)


def moved(pick, rows):
    return dot(pick, rows).astype(BF16)


def gather_first(links, own, part, here, cut):
    first = []
    for axis, half in (("y", cut[0]), ("z", cut[1])):
        for step in FAR_FIRST:
            first.append(links.send(own.at[half], part(here, half), axis, step))
    return first


class PlaneRing:
    def __init__(self, links, first, part, cut):
        self.links, self.part, self.cut = links, part, cut
        received(first)
        self.near, self.far, self.left = {}, [], False
        for step, order in ((1, (0, 1)), (3, (1, 0))):
            for h in order:
                piece = part(pl.ds(links.z * 4 + 2 * h, 2), cut[0])
                self.near["z", step, h] = links.send(piece, piece, "z", step)
        for step, order in ((1, (0, 1, 2, 3)), (3, (2, 3, 0, 1))):
            for z in order:
                piece = part(z * 4 + links.y, cut[1])
                self.near["y", step, z] = links.send(piece, piece, "y", step)

    def pass_on(self):
        links, part, cut = self.links, self.part, self.cut
        for step, h in ((1, 0), (3, 1)):
            self.near["z", step, h].wait_recv()
            piece = part(pl.ds(lax.rem(links.z + 4 - step, 4) * 4 + 2 * h, 2), cut[0])
            self.far.append(links.send(piece, piece, "z", step))
        for step, z in ((1, 0), (1, 1), (3, 2), (3, 3)):
            self.near["y", step, z].wait_recv()
            piece = part(z * 4 + lax.rem(links.y + 4 - step, 4), cut[1])
            self.far.append(links.send(piece, piece, "y", step))

    def arrive_near(self):
        passed = (("z", 1, 0), ("z", 3, 1), ("y", 1, 0), ("y", 1, 1), ("y", 3, 2), ("y", 3, 3))
        for key, copy in self.near.items():
            if key not in passed:
                copy.wait_recv()

    def arrive(self):
        received(self.far)
        sent(self.near.values())
        if not self.left:
            sent(self.far)
            self.left = True

    def leave(self):
        sent(self.far)
        self.left = True


class RowRing:
    def __init__(self, links, part, first=None):
        self.links, self.part = links, part
        self.first = links.take(4) if first is None else first

    def near(self, step):
        piece = self.part(self.links.x, pl.ds(0, SEQ))
        return self.links.copy(piece, piece, "x", step, self.first + step)

    def start(self):
        self.near(1).start()
        self.near(3).start()

    def pass_on(self):
        for step, h in ((1, 0), (3, 1)):
            self.near(step).wait_recv()
            self.far(h).start()

    def arrive(self):
        self.far(0).wait_recv()
        self.far(1).wait_recv()

    def sent(self):
        for k in range(2):
            self.near(2 * k + 1).wait_send()
            self.far(k).wait_send()

    def far(self, h):
        step = 3 if h else 1
        piece = self.part(lax.rem(self.links.x + 4 - step, 4), pl.ds(64 * h, 64))
        return self.links.copy(piece, piece, "x", step, self.first + 2 * h)


class SumRing:
    def __init__(self, links, part, got):
        self.links, self.part, self.got = links, part, got
        self.first = links.take(6)

    def block(self, step):
        return lax.rem(self.links.x + step, 4)

    def far(self, h):
        rows = pl.ds(64 * h, 64)
        return self.links.copy(
            self.part(self.block(2), rows), self.got.at[1, rows], "x", 2 * h + 1, self.first + h
        )

    def near(self, step, early):
        h = 1 if (step == 1) == early else 0
        rows = pl.ds(64 * h, 64)
        return self.links.copy(
            self.part(self.block(step), rows),
            self.got.at[step - 1, rows],
            "x",
            step,
            self.first + 2 + (step - 1) + (0 if early else 1),
        )

    def start_far(self):
        self.far(0).start()
        self.far(1).start()

    def pass_on(self):
        for h, step in ((0, 1), (1, 3)):
            self.far(h).wait_recv()
            rows = pl.ds(64 * h, 64)
            target = self.part(self.block(step), rows)
            target[...] = (
                target[...].astype(F32) + self.got[1, rows].astype(F32)
            ).astype(BF16)
            self.near(step, False).start()

    def total(self, own):
        for step in (1, 3):
            for early in (True, False):
                self.near(step, early).wait()
        self.far(0).wait_send()
        self.far(1).wait_send()
        return own + self.got[0].astype(F32) + self.got[2].astype(F32)


class PlaneSum:
    def __init__(self, links, part, got, last):
        self.links, self.part, self.got, self.last = links, part, got, last
        self.first = links.take(24)

    def last_copy(self, half, step):
        here = self.links.z if half else self.links.y
        return self.links.copy(
            self.got[half].at[0, lax.rem(here + step, 4)],
            self.last[half].at[step - 1],
            "z" if half else "y",
            step,
            self.first + 17 + 3 * half + step,
        )

    def z_copy(self, step, q, far):
        at = lax.rem(self.links.z + (2 if far else step), 4) * 4 + 2 * q
        return self.links.copy(
            self.part(pl.ds(at, 2), 0),
            self.got[0].at[1 if far else step - 1, pl.ds(2 * q, 2)],
            "z",
            step,
            self.first + 2 * (0 if far else (step + 1) // 2) + q,
        )

    def y_copy(self, step, z, far):
        at = z * 4 + lax.rem(self.links.y + (2 if far else step), 4)
        return self.links.copy(
            self.part(at, 1),
            self.got[1].at[1 if far else step - 1, z],
            "y",
            step,
            self.first + 6 + 4 * (0 if far else (step + 1) // 2) + z,
        )

    def start_far(self, low):
        for z in (low, low + 2):
            self.y_copy(1 if z < 2 else 3, z, True).start()

        @pl.when(lax.rem(self.links.z, 2) == low)
        def _():
            self.z_copy(1, 0, True).start()
            self.z_copy(3, 1, True).start()

    def start_near(self):
        self.z_copy(1, 1, False).start()
        self.z_copy(3, 0, False).start()
        for z in range(4):
            self.y_copy(3 if z < 2 else 1, z, False).start()

    def start(self):
        self.z_copy(1, 0, True).start()
        self.z_copy(3, 1, True).start()
        for z in range(4):
            self.y_copy(1 if z < 2 else 3, z, True).start()
        self.start_near()

    def start_direct(self):
        for step in FAR_FIRST:
            for q in range(2):
                self.z_copy(step, q, step == 2).start()
            for z in range(4):
                self.y_copy(step, z, step == 2).start()

    def pass_on(self):
        for q, step in ((0, 1), (1, 3)):
            self.z_copy(step, q, True).wait_recv()
            at = lax.rem(self.links.z + step, 4) * 4 + 2 * q
            for k in range(2):
                self.add(self.part(at + k, 0), self.got[0].at[1, 2 * q + k])
            self.z_copy(step, q, False).start()
        for z in range(4):
            step = 1 if z < 2 else 3
            self.y_copy(step, z, True).wait_recv()
            at = z * 4 + lax.rem(self.links.y + step, 4)
            self.add(self.part(at, 1), self.got[1].at[1, z])
            self.y_copy(step, z, False).start()

    def add(self, target, what):
        target[...] = (target[...].astype(F32) + what[...].astype(F32)).astype(BF16)

    def second(self, direct=False):
        links, steps = self.links, FAR_FIRST if direct else (1, 3)
        for half in range(2):
            for step in steps:
                if half:
                    for z in range(4):
                        self.y_copy(step, z, step == 2).wait_recv()
                else:
                    for q in range(2):
                        self.z_copy(step, q, step == 2).wait_recv()
            for k in range(4):
                slot = k * 4 + links.y if half else links.z * 4 + k
                total = self.part(slot, half)[...].astype(F32)
                for step in steps:
                    total = total + self.got[half][step - 1, k].astype(F32)
                self.got[half][0, k] = total.astype(BF16)

            for step in FAR_FIRST:
                self.last_copy(half, step).start()

    def total(self, half):
        here = self.links.z if half else self.links.y
        received([self.last_copy(half, step) for step in FAR_FIRST])
        total = self.got[half][0, here].astype(F32)
        for step in range(3):
            total = total + self.last[half][step].astype(F32)
        return total

    def sent(self):
        for far in (True, False):
            for q, step in ((0, 1), (1, 3)):
                self.z_copy(step, q, far).wait_send()
                if not far:
                    self.z_copy(4 - step, q, far).wait_send()
            for z in range(4):
                step = 1 if z < 2 else 3
                self.y_copy(step, z, far).wait_send()
                if not far:
                    self.y_copy(4 - step, z, far).wait_send()
        sent([self.last_copy(half, step) for half in range(2) for step in FAR_FIRST])


INS = (
    "tokens",
    "ids",
    "gain_one",
    "w_qkv",
    "w_out",
    "w_router",
    "gain_two",
    "w_sin",
    "w_sout",
    "e_in",
    "e_out",
    "out_grad",
)
HELD = {
    "tokens": ((SEQ, D), BF16),
    "ids": ((TOP, SEQ), jnp.int32),
    "gain_one": ((1, ROWS), BF16),
    "w_qkv": ((ROWS, 2560), BF16),
    "w_out": ((ROWS, D), BF16),
    "w_router": ((EXPERTS, ROWS), BF16),
    "gain_two": ((1, ROWS), BF16),
    "w_sin": ((ROWS, 2 * SH), BF16),
    "w_sout": ((ROWS, SH), BF16),
}
OUTS = {
    "block_out": ((SEQ, D), BF16),
    "tokens_grad": ((SEQ, D), F32),
    "g_gain_one": ((1, ROWS), F32),
    "g_qkv": ((ROWS, 2560), F32),
    "g_out": ((ROWS, D), F32),
    "g_gain_two": ((1, ROWS), F32),
    "g_router": ((EXPERTS, ROWS), F32),
    "g_sin": ((ROWS, 2 * SH), F32),
    "g_sout": ((ROWS, SH), F32),
    "g_ein": ((96, 1024), F32),
    "g_eout": ((96, 512), F32),
}
SCRATCH = {
    "small": ((128, 128), F32),
    "pack": ((4, 16, W_ALL), BF16),
    "arrived": ((4, 16, W_ALL), BF16),
    "dense": ((16, 2, 48, W_ATT), BF16),
    "shared": ((16, 2, 48, W_SHARED), BF16),
    "got": ((16, 96, D), BF16),
    "full": ((8, 2, 96, D), BF16),
    "nat": ((D, D), BF16),
    "normed": ((4, SEQ, D), BF16),
    "qkv": ((4, SEQ, 640), BF16),
    "mix": ((4, SEQ, 384), BF16),
    "send_y": ((4, 2, SEQ, D), BF16),
    "send_x": ((4, 2, SEQ, WIDE), BF16),
    "pair_y": ((4, SEQ, D), BF16),
    "pair_x": ((4, SEQ, WIDE), BF16),
    "got_y": ((3, SEQ, D), BF16),
    "got_x": ((3, SEQ, WIDE), BF16),
    "hidden": ((SEQ, D), F32),
    "probs": ((SEQ, 128), F32),
    "chosen": ((SEQ, 128), F32),
    "rows": ((4, 2, SEQ, WIDE), BF16),
    "cot": ((4, 2, SEQ, D), BF16),
    "gated": ((4, 2, SEQ, 640), BF16),
    "joint": ((4, 2, SEQ, 1280), BF16),
    "low": ((4, SEQ, D), BF16),
    "dsh": ((16, 2, 48, 384), BF16),
    "back": ((48, W_ALL), BF16),
    "e_got0": ((3, 4, 48, D), BF16),
    "e_got1": ((3, 4, 48, D), BF16),
    "e_last0": ((3, 48, D), BF16),
    "e_last1": ((3, 48, D), BF16),
    "d_got0": ((3, 4, 48, 640), BF16),
    "d_got1": ((3, 4, 48, 512), BF16),
    "d_last0": ((3, 48, 640), BF16),
    "d_last1": ((3, 48, 512), BF16),
    "s_got0": ((3, 4, 48, 384), BF16),
    "s_got1": ((3, 4, 48, 384), BF16),
    "s_last0": ((3, 48, 384), BF16),
    "s_last1": ((3, 48, 384), BF16),
}
SENDS, RECEIVES = 164, 254
PAIRS = (((0, 0), (0, 1)), ((1, 0), (3, 0)), ((2, 0), (2, 1)), ((1, 1), (3, 1)))


class Bag:
    pass


def causal_probs(q, k):
    scores = dot_nt(q, k) * HD**-0.5
    row = lax.broadcasted_iota(jnp.int32, (SEQ, SEQ), 0)
    col = lax.broadcasted_iota(jnp.int32, (SEQ, SEQ), 1)
    scores = jnp.where(col <= row, scores, -1e30)
    exponent = jnp.exp(scores - jnp.max(scores, axis=1, keepdims=True))
    return exponent * (1.0 / jnp.sum(exponent, axis=1, keepdims=True))


def kernel(*refs):
    b = Bag()
    names = [
        *(name + "_given" for name in INS),
        *(name + "_result" for name in OUTS),
        *OUTS,
        *HELD,
        *SCRATCH,
    ]
    for name, ref in zip(names, refs):
        setattr(b, name, ref)
    links = Links(*refs[len(names) :])
    x, y, z, c = links.x, links.y, links.z, links.c
    other = 1 - c
    results = []
    kept = links.take(links.kept)

    def deliver(*ready):
        for name in ready:
            results.append(links.local(getattr(b, name), getattr(b, name + "_result")))

    here = z * 4 + y
    mine = 2 * x + c
    every = pl.ds(0, 48)
    e_cut = ((pl.ds(0, 48),), (pl.ds(48, 48),))
    d_cut = ((every, pl.ds(0, 640)), (every, pl.ds(640, 512)))
    s_cut = ((every, pl.ds(0, 384)), (every, pl.ds(384, 384)))
    d_part = lambda slots, half: b.dense.at[(slots, c, *half)]
    s_part = lambda slots, half: b.shared.at[(slots, c, *half)]
    e_part = lambda slots, half: b.got.at[(slots, *half)]

    greeted = links.greet("xyzc")
    loads = [links.local(getattr(b, name + "_given"), getattr(b, name)) for name in HELD]
    loads += [
        links.local(b.e_in_given, b.got.at[here, :, pl.ds(0, 1024)]),
        links.local(b.e_out_given, b.got.at[here, :, pl.ds(1024, 512)]),
        links.local(b.out_grad_given, b.cot.at[x, c]),
    ]
    b.pack[...] = jnp.zeros_like(b.pack)
    b.small[...] = jnp.zeros_like(b.small)
    finish(loads)
    links.locals = 0
    b.small[0:EXPERTS, 0:ROWS] = b.w_router[...].astype(F32)
    b.small[8:9, 0:ROWS] = b.gain_two[...].astype(F32)
    b.small[9:10, 0:ROWS] = b.gain_one[...].astype(F32)
    small = b.small[...].T
    lane = lax.broadcasted_iota(jnp.int32, (SEQ, 128), 1)
    row = lax.broadcasted_iota(jnp.int32, (SEQ, 128), 0)
    named = jnp.zeros((SEQ, 128), F32)
    for k in range(TOP):
        named = named + (b.ids[k : k + 1, :] == row).astype(F32)
    b.chosen[...] = named.T
    gain_one = small[0:ROWS, 9:10]
    for k in range(4):
        for start, width, at in ((k * 384, 384, 0), (D + k * 128, 128, 384), (2048 + k * 128, 128, 512)):
            b.pack[k, 0:ROWS, at : at + width] = (
                b.w_qkv[:, start : start + width].astype(F32) * gain_one
            ).astype(BF16)
        b.pack[k, 0:ROWS, 640:1024] = b.w_out[:, k * 384 : k * 384 + 384]
        b.pack[k, 0:ROWS, 1024:1152] = small[0:ROWS].astype(BF16)
        for core in range(2):
            at, unit = W_ATT + 384 * core, (2 * k + core) * 128
            b.pack[k, 0:ROWS, at : at + 128] = b.w_sin[:, unit : unit + 128]
            b.pack[k, 0:ROWS, at + 128 : at + 256] = b.w_sin[:, SH + unit : SH + unit + 128]
            b.pack[k, 0:ROWS, at + 256 : at + 384] = b.w_sout[:, unit : unit + 128]
    greeted()

    def exchange(cols):
        return [
            links.send(
                b.pack.at[lax.rem(x + step, 4), :, cols], b.arrived.at[x, :, cols], "x", step
            )
            for step in FAR_FIRST
        ]

    exchanged = exchange(pl.ds(0, W_ATT))
    e_cols = lambda cols: tuple((rows, cols) for (rows,) in e_cut)
    e_first = gather_first(links, b.got.at[here], e_part, here, e_cols(pl.ds(0, 1024)))
    inputs = b.tokens[...].astype(F32)
    inverse_one = lax.rsqrt(jnp.mean(inputs * inputs, axis=1, keepdims=True) + epsilon)
    b.normed[x] = (inputs * inverse_one).astype(BF16)
    cot_pair = links.send(b.cot.at[x, c], b.cot.at[x, c], "c", 1)
    b.arrived[x] = b.pack[x]
    finish(exchanged)
    exchanged = exchange(pl.ds(W_ATT, W_SHARED))
    normed_ring = RowRing(links, lambda s, rows: b.normed.at[s, rows])
    cot_ring = RowRing(links, lambda s, rows: b.cot.at[s, c, rows])
    normed_ring.start()
    pick = pick_matrix((48, 64), lambda row: row // ROWS * 16 + row % ROWS)
    for col in range(0, W_ATT, 384):
        block = moved(pick, b.arrived[:, :, col : col + 384].reshape(64, 384))
        b.dense[here, c, :, col : col + 384] = block

    d_first = gather_first(links, b.dense.at[here, c], d_part, here, d_cut)
    sent(d_first)
    e_first += gather_first(links, b.got.at[here], e_part, here, e_cols(pl.ds(1024, 512)))
    d_ring = PlaneRing(links, d_first, d_part, d_cut)
    normed_ring.pass_on()
    cot_ring.start()
    d_ring.pass_on()
    d_ring.leave()
    finish(exchanged)
    for col in range(W_ATT, W_ALL, 384):
        block = moved(pick, b.arrived[:, :, col : col + 384].reshape(64, 384))
        b.shared[here, c, :, col - W_ATT : col - W_ATT + 384] = block
    s_first = gather_first(links, b.shared.at[here, c], s_part, here, s_cut)
    d_ring.arrive_near()
    d_ring.arrive()
    d_pair = links.take(8)

    def d_forward(j):
        piece = b.dense.at[pl.ds(2 * j, 2), c]
        return links.copy(piece, piece, "c", 1, d_pair + j)

    for j in range(8):
        d_forward(j).start()
    e_ring = PlaneRing(links, e_first, e_part, e_cut)
    normed_ring.arrive()

    order = pick_matrix(
        (192, 192), lambda row: row % 48 // ROWS * 48 + row // 48 * ROWS + row % ROWS
    )

    def to_rows(j, source, start, at, width):
        piece = source[pl.ds(2 * j, 2), :, :, start].reshape(192, width)
        piece = moved(order, piece)
        for k in range(4):
            row = pl.multiple_of(k * 384 + j * 48, 16)
            b.nat[pl.ds(row, 48), at : at + width] = piece[k * 48 : k * 48 + 48]

    def to_blocks(j, target, at, width):
        pieces = [
            b.nat[pl.ds(pl.multiple_of(k * 384 + j * 48, 16), 48), at : at + width]
            for k in range(4)
        ]
        piece = moved(order, jnp.concatenate(pieces, axis=0))
        target[pl.ds(2 * j, 2)] = piece.reshape(2, 2, 48, width)

    @pl.loop(0, 8)
    def _(j):
        d_forward(j).wait()
        to_rows(j, b.dense, pl.ds(0, W_ATT), 0, W_ATT)

    s_ring = PlaneRing(links, s_first, s_part, s_cut)

    mix_ring = SumRing(links, lambda s, rows: b.send_y.at[s, 0, rows], b.got_y)

    def attend(sequences):
        for s in sequences:
            b.qkv[s] = dot(b.normed[s], b.nat[:, 0:640]).astype(BF16)
        for h in range(3):
            head = slice(h * HD, (h + 1) * HD)
            for s in sequences:
                probs = causal_probs(b.qkv[s, :, head], b.qkv[s, :, 384:512])
                b.mix[s, :, head] = dot(probs.astype(BF16), b.qkv[s, :, 512:640]).astype(BF16)
        for s in sequences:
            for n in range(2):
                rows = slice(n * 768, (n + 1) * 768)
                b.send_y[s, 0, :, rows] = dot_nt(b.mix[s], b.nat[rows, 640:1024]).astype(BF16)

    right, left, far = (lax.rem(x + step, 4) for step in (1, 3, 2))
    attend([far])
    mix_ring.start_far()
    attend([right, left])
    mix_ring.near(1, True).start()
    mix_ring.near(3, True).start()
    mix_ring.pass_on()
    attend([x])

    e_ring.pass_on()
    cot_ring.pass_on()
    e_hands = []
    lower, upper = pl.ds(0, 48), pl.ds(48, 48)
    for k in range(2):
        for half, to_other in ((other, True), (c, False)):
            at = 2 * half + k
            pieces = [
                (at == lax.rem(z + 2, 4), b.got.at[pl.ds(at * 4, 4), lower], pl.ds(4 * k, 4), lower)
            ]
            for to in range(4):
                pieces.append(
                    (to == lax.rem(y + 2, 4), b.got.at[at * 4 + to, upper], 4 * k + to, upper)
                )
            for is_far, source, slots, rows in pieces:
                target = b.full.at[slots, c, rows]
                if to_other:
                    copy = links.copy(source, target, "c", 1, links.take(1))
                else:
                    copy = links.local_copy(source, target)
                e_hands.append((is_far, copy))

    def e_hand(far_ones):
        for is_far, copy in e_hands:

            @pl.when(is_far == far_ones)
            def _():
                copy.start()

    e_ring.arrive_near()
    e_hand(False)

    hidden = mix_ring.total(b.tokens[...].astype(F32) + b.send_y[x, 0].astype(F32))
    b.hidden[...] = hidden
    inverse_two = lax.rsqrt(jnp.mean(hidden * hidden, axis=1, keepdims=True) + epsilon)
    lane8 = lax.broadcasted_iota(jnp.int32, (8, 128), 1)
    gain_two = dot_nt((lane8 == 8).astype(BF16), b.nat[:, 1024:1152])[0:1]
    moe_in = (hidden * inverse_two * gain_two).astype(BF16)
    b.rows[x, c, :, 0:D] = moe_in
    logits = jnp.where(lane < EXPERTS, dot(moe_in, b.nat[:, 1024:1152]), -1e30)
    exponent = jnp.exp(logits - jnp.max(logits, axis=1, keepdims=True))
    router_probs = exponent / jnp.sum(exponent, axis=1, keepdims=True)
    b.probs[...] = router_probs
    gates = b.chosen[...] * router_probs
    high = gates.astype(BF16).astype(F32)
    b.rows[x, c, :, D:WIDE] = (high + pltpu.roll(gates - high, 8, 1)).astype(BF16)
    rows_ring = RowRing(links, lambda s, rows: b.rows.at[s, c, rows], kept)
    rows_ring.start()
    pair_rows, pair_cot = kept + 4, kept + 8
    forward_rows = lambda s, d: links.copy(
        b.rows.at[s, c], b.rows.at[s, c], "c", 1, pair_rows + d
    )
    forward_cot = lambda s, d: links.copy(b.cot.at[s, c], b.cot.at[s, c], "c", 1, pair_cot + d)
    forward_rows(x, 0).start()
    s_ring.pass_on()
    e_ring.arrive()
    e_hand(True)
    sent(e_first + s_first)
    s_ring.arrive_near()
    s_ring.arrive()
    half = pl.ds(pl.multiple_of(other * 384, 128), 384)
    s_pair = links.send(b.shared.at[:, c, :, half], b.shared.at[:, c, :, half], "c", 1)

    for _, copy in e_hands:
        copy.wait()

    def shared_rows():
        s_pair.wait()

        @pl.loop(0, 8)
        def _(j):
            to_rows(j, b.shared, pl.ds(pl.multiple_of(c * 384, 128), 384), W_ATT, 384)

    links.left()
    back_pair = links.take(8)
    sum_pair = links.take(4)
    parts = (pl.ds(0, 768), pl.ds(768, WIDE - 768))
    back_forward = lambda s, d, n: links.copy(
        b.send_x.at[s, other, :, parts[n]], b.pair_x.at[s, :, parts[n]], "c", 1, back_pair + 2 * d + n
    )
    sum_forward = lambda s, d: links.copy(
        b.send_y.at[s, other], b.pair_y.at[s], "c", 1, sum_pair + d
    )
    back_ring = SumRing(links, lambda s, rows: b.send_x.at[s, c, rows], b.got_x)
    sum_ring = SumRing(links, lambda s, rows: b.send_y.at[s, c, rows], b.got_y)
    cot_pair.wait()

    normed_ring.sent()
    cot_ring.sent()
    cot_ring.arrive()
    for d in range(1, 4):
        forward_cot(lax.rem(x + d, 4), d).start()
    forward_rows(x, 0).wait_recv()

    def which(i, core):
        sides = ((i == 1) & (core == 0)) | ((i == 3) & (core == 1))
        return ((0, i == 0), (1, sides), (3, sides), (2, i == 2))

    def give_pair(i, n):
        for d, now in which(i, other):

            @pl.when(now)
            def _():
                back_forward(lax.rem(x + d, 4), d, n).start()

    def add_pair(i, n):
        for d, now in which(i, c):
            s = lax.rem(x + d, 4)

            @pl.when(now)
            def _():
                back_forward(s, d, n).wait_recv()
                b.send_x[s, c, :, parts[n]] = (
                    b.send_x[s, c, :, parts[n]].astype(F32) + b.pair_x[s, :, parts[n]].astype(F32)
                ).astype(BF16)
                if n and d == 2:
                    back_ring.start_far()
                elif n and d:
                    back_ring.near(d, True).start()

    def pair_of(i):
        def chosen(k, what):
            values = [PAIRS[step][k][what] for step in range(4)]
            result = values[3]
            for step in range(3):
                result = jnp.where(i == step, values[step], result)
            return result

        return [(lax.rem(x + chosen(k, 0), 4), chosen(k, 1)) for k in range(2)]

    def both(i, ref, cols):
        return jnp.concatenate([ref[s, core, :, cols] for s, core in pair_of(i)], axis=0)

    def keep(i, ref, cols, value):
        for k, (s, core) in enumerate(pair_of(i)):
            ref[s, core, :, cols] = value[k * SEQ : (k + 1) * SEQ]

    def row_grads(i):
        slopes = both(i, b.joint, slice(0, 1280))
        for n in range(2):
            rows = slice(n * 768, (n + 1) * 768)
            result = dot_nt(
                slopes[:, 0:1024], b.full[4 * n : 4 * n + 4, :, :, 0:1024].reshape(768, 1024)
            ) + dot_nt(slopes[:, 1024:1280], b.nat[rows, 1152:1408])
            keep(i, b.send_x, rows, result.astype(BF16))
            give_pair(i, n)
            if n == 0:

                @pl.when(i == 1)
                def _():
                    rows_ring.arrive()
                    forward_rows(lax.rem(x + 2, 4), 2).start()

    @pl.loop(0, 4)
    def _(i):
        for k, far_ones in ((1, (1, 3)), (2, (2,))):

            @pl.when(i == k)
            def _():
                for d in far_ones:
                    forward_cot(lax.rem(x + d, 4), d).wait_recv()
                    forward_rows(lax.rem(x + d, 4), d).wait_recv()

        @pl.when(i > 0)
        def _():
            add_pair(i - 1, 0)

        tokens = both(i, b.rows, slice(0, D))
        grads = both(i, b.cot, slice(0, D))
        lanes = lax.broadcasted_iota(jnp.int32, (256, 128), 1)
        gate = both(i, b.rows, slice(D, WIDE)).astype(F32)
        gate = jnp.where((lanes == mine) | (lanes == mine + 8), gate, 0.0)
        gate = jnp.sum(gate, axis=1, keepdims=True)
        gate_grad = jnp.zeros((256, 1), F32)
        for part in range(3):
            if part < 2:
                at, width = part * 256, 256
                g = dot(tokens, b.full[:, :, :, at : at + 256].reshape(D, 256))
                u = dot(tokens, b.full[:, :, :, at + 512 : at + 768].reshape(D, 256))
                a = dot(grads, b.full[:, :, :, at + 1024 : at + 1280].reshape(D, 256))
                first, second, scale = at, at + 512, gate
            else:

                @pl.when(i == 0)
                def _():
                    shared_rows()

                at, width = 512, 128
                gu = dot(tokens, b.nat[:, 1152:1408])
                g, u = gu[:, 0:128], gu[:, 128:256]
                a = dot(grads, b.nat[:, 1408:1536])
                first, second, scale = 1024, 1152, None
            g = g.astype(BF16).astype(F32)
            u = u.astype(BF16).astype(F32)
            sg = jax.nn.sigmoid(g)
            act = (g * sg * u).astype(BF16)
            if scale is not None:
                gate_grad = gate_grad + jnp.sum(act.astype(F32) * a, axis=1, keepdims=True)
                act = (act.astype(F32) * scale).astype(BF16)
                a = a * scale
            keep(i, b.gated, slice(at, at + width), act)
            keep(
                i,
                b.joint,
                slice(first, first + width),
                (a * u * (sg * (1.0 + g * (1.0 - sg)))).astype(BF16),
            )
            keep(i, b.joint, slice(second, second + width), (a * g * sg).astype(BF16))
        gate_high = gate_grad.astype(BF16).astype(F32)
        spread = jnp.where(lanes == mine, gate_high, 0.0)
        spread = spread + jnp.where(lanes == mine + 8, gate_grad - gate_high, 0.0)
        keep(i, b.send_x, slice(D, WIDE), spread.astype(BF16))

        @pl.when(i > 0)
        def _():
            add_pair(i - 1, 1)

        @pl.when(i == 0)
        def _():
            rows_ring.pass_on()
            for d in (1, 3):
                forward_rows(lax.rem(x + d, 4), d).start()

        row_grads(i)

    add_pair(3, 0)
    add_pair(3, 1)


    e_sum = PlaneSum(
        links,
        lambda slots, half: b.got.at[slots, pl.ds(48 * half, 48)],
        (b.e_got0, b.e_got1),
        (b.e_last0, b.e_last1),
    )
    e_moves = []

    def e_start(low):
        finish(e_moves[low])
        e_sum.start_far(low)

    for low in range(2):
        for n in (2 * low, 2 * low + 1):
            if n == 3:
                e_start(0)
            cols = slice(n * 384, (n + 1) * 384)
            tokens = b.rows[:, :, :, cols].reshape(1024, 384)
            for at in (0, 512):
                result = dot_tn(tokens, b.joint[:, :, :, at : at + 512].reshape(1024, 512))
                b.full[2 * n : 2 * n + 2, :, :, at : at + 512] = result.astype(BF16).reshape(
                    2, 2, 96, 512
                )
            grads = b.cot[:, :, :, cols].reshape(1024, 384)
            result = dot_tn(grads, b.gated[:, :, :, 0:512].reshape(1024, 512))
            result = result.astype(BF16).reshape(2, 2, 2, 48, 512)
            for h in range(2):
                b.dense[8 * h + 2 * n : 8 * h + 2 * n + 2, :, :, 0:512] = result[:, :, h]
        four = pl.ds(4 * low, 4)
        target = pl.ds(8 * c + 4 * low, 4)
        wide, slim = pl.ds(0, 1024), pl.ds(1024, 512)
        moves = [
            links.send(b.full.at[four, other, :, wide], b.got.at[target, :, wide], "c", 1),
            links.local(b.full.at[four, c, :, wide], b.got.at[target, :, wide]),
        ]
        for h in range(2):
            rows, slots = pl.ds(48 * h, 48), pl.ds(8 * h + 4 * low, 4)
            moves += [
                links.send(
                    b.dense.at[slots, other, :, pl.ds(0, 512)], b.got.at[target, rows, slim], "c", 1
                ),
                links.local(b.dense.at[slots, c, :, pl.ds(0, 512)], b.got.at[target, rows, slim]),
            ]
        e_moves.append(moves)
        if not low:
            back_ring.pass_on()

    e_start(1)

    moe_back = back_ring.total(b.send_x[x, c].astype(F32))
    raw = moe_back[:, D:WIDE]
    router_probs = b.probs[...]
    prob_grad = b.chosen[...] * (raw + pltpu.roll(raw, 120, 1))
    logit_grad = router_probs * (
        prob_grad - jnp.sum(router_probs * prob_grad, axis=1, keepdims=True)
    )
    logit_grad = logit_grad.astype(BF16)
    gain_two = dot_nt((lane8 == 8).astype(BF16), b.nat[:, 1024:1152])[0:1]
    moe_in_grad = moe_back[:, 0:D] + dot_nt(logit_grad, b.nat[:, 1024:1152])
    hidden = b.hidden[...]
    inverse_two = lax.rsqrt(jnp.mean(hidden * hidden, axis=1, keepdims=True) + epsilon)
    scaled = gain_two * moe_in_grad
    hidden_grad = (
        b.cot[x, c].astype(F32)
        + inverse_two * scaled
        - hidden
        * (inverse_two * inverse_two * inverse_two)
        * jnp.mean(scaled * hidden, axis=1, keepdims=True)
    )
    b.tokens_grad[...] = hidden_grad
    b.low[x] = hidden_grad.astype(BF16)
    low_ring = RowRing(links, lambda s, rows: b.low.at[s, rows])
    low_ring.start()
    e_sum.start_near()
    misc_grad = dot_tn(b.rows[x, c, :, 0:D], logit_grad) + dot_tn(
        (moe_in_grad * hidden * inverse_two).astype(BF16), (lane == 8).astype(BF16)
    )
    b.nat[:, 1024:1152] = misc_grad.astype(BF16)

    @pl.loop(0, 4)
    def _(d):
        s = lax.rem(x + d, 4)
        for n in range(2):
            rows = slice(n * 768, (n + 1) * 768)
            result = dot_nt(
                b.gated[s, :, :, 0:512].reshape(256, 512), b.full[4 * n : 4 * n + 4, :, :, 1024:1536].reshape(768, 512)
            ) + dot_nt(b.gated[s, :, :, 512:640].reshape(256, 128), b.nat[rows, 1408:1536])
            b.send_y[s, :, :, rows] = result.astype(BF16).reshape(2, SEQ, 768)
        sum_forward(s, d).start()

    for n in range(4):
        cols = slice(n * 384, (n + 1) * 384)
        tokens = b.rows[:, :, :, cols].reshape(1024, 384)
        result = dot_tn(tokens, b.joint[:, :, :, 1024:1280].reshape(1024, 256))
        b.nat[cols, 1152:1408] = result.astype(BF16)
        grads = b.cot[:, :, :, cols].reshape(1024, 384)
        result = dot_tn(grads, b.gated[:, :, :, 512:640].reshape(1024, 128))
        b.nat[cols, 1408:1536] = result.astype(BF16)

    @pl.loop(0, 8)
    def _(j):
        to_blocks(j, b.dsh, W_ATT, 384)

    half = pl.ds(pl.multiple_of(c * 384, 128), 384)
    for d in range(1, 4):
        forward_cot(lax.rem(x + d, 4), d).wait_send()
    s_give = links.send(b.dsh.at[:, other], b.shared.at[:, 0, :, half], "c", 1)
    s_keep = links.local(b.dsh.at[:, c], b.shared.at[:, 0, :, half])
    s_sum = PlaneSum(
        links,
        lambda slots, half: b.shared.at[slots, 0, :, pl.ds(384 * half, 384)],
        (b.s_got0, b.s_got1),
        (b.s_last0, b.s_last1),
    )

    e_sum.pass_on()
    norm_ring = SumRing(
        links,
        lambda s, rows: b.send_x.at[s, 0, rows, pl.ds(0, D)],
        b.got_x.at[:, :, pl.ds(0, D)],
    )
    for d in range(4):
        for n in range(2):
            back_forward(lax.rem(x + d, 4), d, n).wait_send()

    def attend_back(sequences):
        mix_grads, parts_of = [], []
        for s in sequences:
            mix_grads.append(dot(b.low[s], b.nat[:, 640:1024]).astype(BF16))
            parts_of.append((jnp.zeros((SEQ, HD), F32), jnp.zeros((SEQ, HD), F32)))
        for h in range(3):
            head = slice(h * HD, (h + 1) * HD)
            for k, s in enumerate(sequences):
                key_grad, value_grad = parts_of[k]
                key, value = b.qkv[s, :, 384:512], b.qkv[s, :, 512:640]
                query = b.qkv[s, :, head]
                mixed = mix_grads[k][:, head]
                probs = causal_probs(query, key)
                dprob = dot_nt(mixed, value)
                value_grad = value_grad + dot_tn(probs.astype(BF16), mixed)
                delta = jnp.sum(probs * dprob, axis=1, keepdims=True)
                score_grad = (probs * (dprob - delta)).astype(BF16)
                b.qkv[s, :, head] = (dot(score_grad, key) * HD**-0.5).astype(BF16)
                parts_of[k] = (key_grad + dot_tn(score_grad, query), value_grad)
        for k, s in enumerate(sequences):
            key_grad, value_grad = parts_of[k]
            b.qkv[s, :, 384:512] = (key_grad * HD**-0.5).astype(BF16)
            b.qkv[s, :, 512:640] = value_grad.astype(BF16)

    def normed_back(sequences):
        for s in sequences:
            for n in range(2):
                rows = slice(n * 768, (n + 1) * 768)
                b.send_x[s, 0, :, rows] = dot_nt(b.qkv[s], b.nat[rows, 0:640]).astype(BF16)

    attend_back([x])
    low_ring.pass_on()
    normed_back([x])
    attend_back([right, left])
    normed_back([right, left])
    norm_ring.near(1, True).start()
    norm_ring.near(3, True).start()
    s_give.wait()
    s_keep.wait()
    s_sum.start()
    low_ring.arrive()
    attend_back([far])
    normed_back([far])
    norm_ring.start_far()

    for d in (2, 1, 3, 0):
        s = lax.rem(x + d, 4)
        sum_forward(s, d).wait()
        b.send_y[s, c] = (b.send_y[s, c].astype(F32) + b.pair_y[s].astype(F32)).astype(BF16)
        if d == 2:
            sum_ring.start_far()
        elif d:
            sum_ring.near(d, True).start()
    e_sum.second()
    d_base = links.take(8)

    def d_landing(j):
        rows = pl.ds(pl.multiple_of(lax.div(j, 4) * 48, 16), 48)
        return b.cot.at[lax.rem(j, 4), :, rows, pl.ds(0, W_ATT)]

    d_give = lambda j: links.copy(
        b.dense.at[pl.ds(2 * j, 2), other], d_landing(j), "c", 1, d_base + j
    )

    for n in range(4):
        cols = slice(n * 384, (n + 1) * 384)
        result = dot_tn(b.normed[:, :, cols].reshape(512, 384), b.qkv[...].reshape(512, 640))
        b.nat[cols, 0:640] = result.astype(BF16)
        result = dot_tn(b.low[:, :, cols].reshape(512, 384), b.mix[...].reshape(512, 384))
        b.nat[cols, 640:1024] = result.astype(BF16)

    @pl.loop(0, 8)
    def _(j):
        to_blocks(j, b.dense, 0, W_ATT)
        d_give(j).start()

    s_sum.pass_on()

    @pl.loop(0, 8)
    def _(j):
        d_give(j).wait()
        total = b.dense[pl.ds(2 * j, 2), c].astype(F32) + d_landing(j)[...].astype(F32)
        b.dense[pl.ds(2 * j, 2), c] = total.astype(BF16)

    d_sum = PlaneSum(
        links,
        lambda slots, half: d_part(slots, d_cut[half]),
        (b.d_got0, b.d_got1),
        (b.d_last0, b.d_last1),
    )
    d_sum.start_direct()

    s_sum.second()
    norm_ring.pass_on()

    scaled = norm_ring.total(b.send_x[x, 0, :, 0:D].astype(F32))
    inputs = b.tokens[...].astype(F32)
    inverse_one = lax.rsqrt(jnp.mean(inputs * inputs, axis=1, keepdims=True) + epsilon)
    b.tokens_grad[...] = (
        b.tokens_grad[...]
        + inverse_one * scaled
        - inputs
        * (inverse_one * inverse_one * inverse_one)
        * jnp.mean(scaled * inputs, axis=1, keepdims=True)
    )
    deliver("tokens_grad")


    d_sum.second(direct=True)
    sum_ring.pass_on()
    for part in range(2):
        at = W_ATT + 384 * part
        b.back[:, at : at + 384] = s_sum.total(part).astype(BF16)
    for part, cols in ((0, slice(0, 640)), (1, slice(640, 1152))):
        b.back[:, cols] = d_sum.total(part).astype(BF16)
    pick = pick_matrix((64, 48), lambda row: jnp.where(row % 16 < ROWS, row // 16 * ROWS + row % 16, -1))
    for col in range(0, W_ALL, 384):
        b.pack[:, :, col : col + 384] = moved(pick, b.back[:, col : col + 384]).reshape(4, 16, 384)
    exchanged = exchange(pl.ds(0, W_ALL))
    b.arrived[x] = b.pack[x]
    for part in range(2):
        rows = slice(48 * part, 48 * part + 48)
        total = e_sum.total(part)
        b.g_ein[rows] = total[:, 0:1024]
        b.g_eout[rows] = total[:, 1024:1536]
    deliver("g_ein", "g_eout")
    result = sum_ring.total(b.hidden[...] + b.send_y[x, c].astype(F32))
    b.block_out[...] = result.astype(BF16)
    deliver("block_out")

    for ring in (rows_ring, low_ring):
        ring.sent()
    for d in range(4):
        forward_rows(lax.rem(x + d, 4), d).wait_send()
    for plane_sum in (e_sum, s_sum, d_sum):
        plane_sum.sent()
    received(exchanged)
    gain_grad = jnp.zeros((ROWS, 1), F32)
    misc = jnp.zeros((ROWS, 128), F32)
    for k in range(4):
        piece = b.arrived[k].astype(F32)[0:ROWS]
        for start, width, at in ((k * 384, 384, 0), (D + k * 128, 128, 384), (2048 + k * 128, 128, 512)):
            raw = piece[:, at : at + width]
            gain_grad = gain_grad + jnp.sum(
                raw * b.w_qkv[:, start : start + width].astype(F32), axis=1, keepdims=True
            )
            b.g_qkv[:, start : start + width] = raw * gain_one
        b.g_out[:, k * 384 : k * 384 + 384] = piece[:, 640:1024]
        misc = misc + piece[:, 1024:1152]
        for core in range(2):
            at, unit = W_ATT + 384 * core, (2 * k + core) * 128
            b.g_sin[:, unit : unit + 128] = piece[:, at : at + 128]
            b.g_sin[:, SH + unit : SH + unit + 128] = piece[:, at + 128 : at + 256]
            b.g_sout[:, unit : unit + 128] = piece[:, at + 256 : at + 384]
    b.small[0:ROWS] = jnp.where(lane[0:ROWS] == 9, gain_grad, misc)
    small = b.small[...].T
    b.g_router[...] = small[0:EXPERTS, 0:ROWS]
    b.g_gain_two[...] = small[8:9, 0:ROWS]
    b.g_gain_one[...] = small[9:10, 0:ROWS]
    sent(exchanged)
    deliver("g_gain_one", "g_qkv", "g_out", "g_gain_two", "g_router", "g_sin", "g_sout")
    finish(results)


def hand_over(*refs):
    n = len(OUTS)
    sources, targets, held, sems = refs[:n], refs[n : 2 * n], refs[2 * n : 3 * n], refs[3 * n]
    reads = [pltpu.make_async_copy(sources[i], held[i], sems.at[0, i]) for i in range(n)]
    writes = [pltpu.make_async_copy(held[i], targets[i], sems.at[1, i]) for i in range(n)]
    for read in reads:
        read.start()
    for read, write in zip(reads, writes):
        read.wait()
        write.start()
    finish(writes)


def local(
    tokens,
    expert_ids,
    attn_gain,
    w_qkv,
    w_out,
    moe_gain,
    w_router,
    w_shared_in,
    w_shared_out,
    w_expert_in,
    w_expert_out,
    out_grad,
):
    results = pl.pallas_call(
        kernel,
        out_shape=[jax.ShapeDtypeStruct(shape, dtype) for shape, dtype in OUTS.values()],
        in_specs=[pl.BlockSpec(memory_space=pl.ANY)] * len(INS),
        out_specs=[pl.BlockSpec(memory_space=pl.ANY)] * len(OUTS),
        scratch_shapes=[
            *[
                pltpu.VMEM(shape, dtype)
                for shape, dtype in (*OUTS.values(), *HELD.values(), *SCRATCH.values())
            ],
            pltpu.SemaphoreType.DMA((SENDS,)),
            pltpu.SemaphoreType.DMA((RECEIVES,)),
        ],
        compiler_params=pltpu.CompilerParams(
            collective_id=1, has_side_effects=True, vmem_limit_bytes=(64 << 20) - (1 << 16)
        ),
        cost_estimate=pl.CostEstimate(
            flops=23_000_000_000, bytes_accessed=10_000_000, transcendentals=2_000_000
        ),
        name="block",
    )(
        tokens,
        expert_ids.T,
        attn_gain[None],
        w_qkv,
        w_out,
        w_router.T,
        moe_gain[None],
        w_shared_in,
        w_shared_out,
        w_expert_in,
        w_expert_out,
        out_grad,
    )
    results = pl.pallas_call(
        hand_over,
        out_shape=[jax.ShapeDtypeStruct(shape, dtype) for shape, dtype in OUTS.values()],
        in_specs=[pl.BlockSpec(memory_space=pl.ANY)] * len(OUTS),
        out_specs=[pl.BlockSpec(memory_space=pl.ANY)] * len(OUTS),
        scratch_shapes=[
            *[pltpu.VMEM(shape, dtype) for shape, dtype in OUTS.values()],
            pltpu.SemaphoreType.DMA((2, len(OUTS))),
        ],
        name="hand_over",
    )(*results)
    block_out, tokens_grad, gain_one, qkv, out, gain_two, router, sin, sout, ein, eout = results
    return (
        block_out,
        tokens_grad,
        gain_one[0],
        qkv,
        out,
        gain_two[0],
        router.T,
        sin,
        sout,
        ein,
        eout,
    )


def solution(mesh):
    wide, flat = P("fsdp", None), P("fsdp")
    return jax.shard_map(
        local,
        mesh=mesh,
        in_specs=(wide, wide, flat, wide, wide, flat, wide, wide, wide, wide, wide, wide),
        out_specs=(wide, wide, flat, wide, wide, flat, wide, wide, wide, wide, wide),
        check_vma=False,
    )
```

```python
import jax
import jax.numpy as jnp
from jax import lax
from jax.experimental import pallas as pl
from jax.experimental.pallas import tpu as pltpu
from jax.sharding import PartitionSpec as P

D = 1536
HD = 128
SH = 1024
EXPERTS = 8
TOP = 6
ROWS = 12
SEQ = 128
W_ATT = 1152
W_SHARED = 768
W_ALL = W_ATT + W_SHARED
WIDE = D + 128
epsilon = 1e-05
MESH = pl.DeviceIdType.MESH
F32 = jnp.float32
BF16 = jnp.bfloat16
STRIDE = {"x": (32, 4), "z": (8, 4), "y": (2, 4), "c": (1, 2)}
FAR_FIRST = (2, 1, 3)
NEAR_FIRST = (1, 3, 2)


def place(me, axis):
    stride, size = STRIDE[axis]
    return lax.rem(lax.div(me, stride), size)


def peer(me, axis, step):
    stride, size = STRIDE[axis]
    here = place(me, axis)
    return me + (lax.rem(here + step, size) - here) * stride


class Links:
    def __init__(self, send_sem, recv_sem):
        self.me = lax.axis_index("fsdp")
        self.send_sem, self.recv_sem = send_sem, recv_sem
        self.count = self.locals = 0
        self.again, self.kept = None, 12
        self.x, self.y, self.z, self.c = (place(self.me, axis) for axis in "xyzc")

    def take(self, number):
        first = self.count
        self.count += number
        return first

    def left(self):
        self.again = self.count

    def sender(self, sem):
        again = self.again is not None and (not isinstance(sem, int) or sem >= self.again)
        return self.send_sem.at[sem - self.again + self.kept if again else sem]

    def copy(self, src, dst, axis, step, sem):
        return pltpu.make_async_remote_copy(
            src_ref=src,
            dst_ref=dst,
            send_sem=self.sender(sem),
            recv_sem=self.recv_sem.at[sem],
            device_id=(peer(self.me, axis, step),),
            device_id_type=MESH,
        )

    def send(self, src, dst, axis, step):
        copy = self.copy(src, dst, axis, step, self.take(1))
        copy.start()
        return copy

    def local(self, src, dst):
        copy = self.local_copy(src, dst)
        copy.start()
        return copy

    def local_copy(self, src, dst):
        self.locals += 1
        return pltpu.make_async_copy(src, dst, self.send_sem.at[SENDS - self.locals])

    def greet(self, axes):
        barrier = pltpu.get_barrier_semaphore()
        total = 0
        for axis in axes:
            for step in range(1, STRIDE[axis][1]):
                pl.semaphore_signal(
                    barrier, inc=1, device_id=(peer(self.me, axis, step),), device_id_type=MESH
                )
                total += 1
        return lambda: pl.semaphore_wait(barrier, total)


def finish(copies):
    for copy in copies:
        copy.wait()


def received(copies):
    for copy in copies:
        copy.wait_recv()


def sent(copies):
    for copy in copies:
        copy.wait_send()


def dot(a, b):
    return jnp.dot(a, b, preferred_element_type=F32)


def dot_nt(a, b):
    return lax.dot_general(a, b, (((1,), (1,)), ((), ())), preferred_element_type=F32)


def dot_tn(a, b):
    return lax.dot_general(a, b, (((0,), (0,)), ((), ())), preferred_element_type=F32)


def pick_matrix(shape, source):
    row = lax.broadcasted_iota(jnp.int32, shape, 0)
    col = lax.broadcasted_iota(jnp.int32, shape, 1)
    return (col == source(row)).astype(BF16)


def moved(pick, rows):
    return dot(pick, rows).astype(BF16)


def gather_first(links, own, part, here, cut):
    first = []
    for axis, half in (("y", cut[0]), ("z", cut[1])):
        for step in FAR_FIRST:
            first.append(links.send(own.at[half], part(here, half), axis, step))
    return first


class PlaneRing:
    def __init__(self, links, first, part, cut):
        self.links, self.part, self.cut = links, part, cut
        received(first)
        self.near, self.far, self.left = {}, [], False
        for step, order in ((1, (0, 1)), (3, (1, 0))):
            for h in order:
                piece = part(pl.ds(links.z * 4 + 2 * h, 2), cut[0])
                self.near["z", step, h] = links.send(piece, piece, "z", step)
        for step, order in ((1, (0, 1, 2, 3)), (3, (2, 3, 0, 1))):
            for z in order:
                piece = part(z * 4 + links.y, cut[1])
                self.near["y", step, z] = links.send(piece, piece, "y", step)

    def pass_on(self):
        links, part, cut = self.links, self.part, self.cut
        for step, h in ((1, 0), (3, 1)):
            self.near["z", step, h].wait_recv()
            piece = part(pl.ds(lax.rem(links.z + 4 - step, 4) * 4 + 2 * h, 2), cut[0])
            self.far.append(links.send(piece, piece, "z", step))
        for step, z in ((1, 0), (1, 1), (3, 2), (3, 3)):
            self.near["y", step, z].wait_recv()
            piece = part(z * 4 + lax.rem(links.y + 4 - step, 4), cut[1])
            self.far.append(links.send(piece, piece, "y", step))

    def arrive_near(self):
        passed = (("z", 1, 0), ("z", 3, 1), ("y", 1, 0), ("y", 1, 1), ("y", 3, 2), ("y", 3, 3))
        for key, copy in self.near.items():
            if key not in passed:
                copy.wait_recv()

    def arrive(self):
        received(self.far)
        sent(self.near.values())
        if not self.left:
            sent(self.far)
            self.left = True

    def leave(self):
        sent(self.far)
        self.left = True


class RowRing:
    def __init__(self, links, part, first=None):
        self.links, self.part = links, part
        self.first = links.take(4) if first is None else first

    def near(self, step):
        piece = self.part(self.links.x, pl.ds(0, SEQ))
        return self.links.copy(piece, piece, "x", step, self.first + step)

    def start(self):
        self.near(1).start()
        self.near(3).start()

    def pass_on(self):
        for step, h in ((1, 0), (3, 1)):
            self.near(step).wait_recv()
            self.far(h).start()

    def arrive(self):
        self.far(0).wait_recv()
        self.far(1).wait_recv()

    def sent(self):
        for k in range(2):
            self.near(2 * k + 1).wait_send()
            self.far(k).wait_send()

    def far(self, h):
        step = 3 if h else 1
        piece = self.part(lax.rem(self.links.x + 4 - step, 4), pl.ds(64 * h, 64))
        return self.links.copy(piece, piece, "x", step, self.first + 2 * h)


class SumRing:
    def __init__(self, links, part, got):
        self.links, self.part, self.got = links, part, got
        self.first = links.take(6)

    def block(self, step):
        return lax.rem(self.links.x + step, 4)

    def far(self, h):
        rows = pl.ds(64 * h, 64)
        return self.links.copy(
            self.part(self.block(2), rows), self.got.at[1, rows], "x", 2 * h + 1, self.first + h
        )

    def near(self, step, early):
        h = 1 if (step == 1) == early else 0
        rows = pl.ds(64 * h, 64)
        return self.links.copy(
            self.part(self.block(step), rows),
            self.got.at[step - 1, rows],
            "x",
            step,
            self.first + 2 + (step - 1) + (0 if early else 1),
        )

    def start_far(self):
        self.far(0).start()
        self.far(1).start()

    def pass_on(self):
        for h, step in ((0, 1), (1, 3)):
            self.far(h).wait_recv()
            rows = pl.ds(64 * h, 64)
            target = self.part(self.block(step), rows)
            target[...] = (
                target[...].astype(F32) + self.got[1, rows].astype(F32)
            ).astype(BF16)
            self.near(step, False).start()

    def total(self, own):
        for step in (1, 3):
            for early in (True, False):
                self.near(step, early).wait()
        self.far(0).wait_send()
        self.far(1).wait_send()
        return own + self.got[0].astype(F32) + self.got[2].astype(F32)


class PlaneSum:
    def __init__(self, links, part, got, last):
        self.links, self.part, self.got, self.last = links, part, got, last
        self.first = links.take(24)

    def last_copy(self, half, step):
        here = self.links.z if half else self.links.y
        return self.links.copy(
            self.got[half].at[0, lax.rem(here + step, 4)],
            self.last[half].at[step - 1],
            "z" if half else "y",
            step,
            self.first + 17 + 3 * half + step,
        )

    def z_copy(self, step, q, far):
        at = lax.rem(self.links.z + (2 if far else step), 4) * 4 + 2 * q
        return self.links.copy(
            self.part(pl.ds(at, 2), 0),
            self.got[0].at[1 if far else step - 1, pl.ds(2 * q, 2)],
            "z",
            step,
            self.first + 2 * (0 if far else (step + 1) // 2) + q,
        )

    def y_copy(self, step, z, far):
        at = z * 4 + lax.rem(self.links.y + (2 if far else step), 4)
        return self.links.copy(
            self.part(at, 1),
            self.got[1].at[1 if far else step - 1, z],
            "y",
            step,
            self.first + 6 + 4 * (0 if far else (step + 1) // 2) + z,
        )

    def start_far(self, low):
        for z in (low, low + 2):
            self.y_copy(1 if z < 2 else 3, z, True).start()

        @pl.when(lax.rem(self.links.z, 2) == low)
        def _():
            self.z_copy(1, 0, True).start()
            self.z_copy(3, 1, True).start()

    def start_near(self):
        self.z_copy(1, 1, False).start()
        self.z_copy(3, 0, False).start()
        for z in range(4):
            self.y_copy(3 if z < 2 else 1, z, False).start()

    def start(self):
        self.z_copy(1, 0, True).start()
        self.z_copy(3, 1, True).start()
        for z in range(4):
            self.y_copy(1 if z < 2 else 3, z, True).start()
        self.start_near()

    def start_direct(self):
        for step in FAR_FIRST:
            for q in range(2):
                self.z_copy(step, q, step == 2).start()
            for z in range(4):
                self.y_copy(step, z, step == 2).start()

    def pass_on(self):
        for q, step in ((0, 1), (1, 3)):
            self.z_copy(step, q, True).wait_recv()
            at = lax.rem(self.links.z + step, 4) * 4 + 2 * q
            for k in range(2):
                self.add(self.part(at + k, 0), self.got[0].at[1, 2 * q + k])
            self.z_copy(step, q, False).start()
        for z in range(4):
            step = 1 if z < 2 else 3
            self.y_copy(step, z, True).wait_recv()
            at = z * 4 + lax.rem(self.links.y + step, 4)
            self.add(self.part(at, 1), self.got[1].at[1, z])
            self.y_copy(step, z, False).start()

    def add(self, target, what):
        target[...] = (target[...].astype(F32) + what[...].astype(F32)).astype(BF16)

    def second(self, direct=False):
        links, steps = self.links, FAR_FIRST if direct else (1, 3)
        for half in range(2):
            for step in steps:
                if half:
                    for z in range(4):
                        self.y_copy(step, z, step == 2).wait_recv()
                else:
                    for q in range(2):
                        self.z_copy(step, q, step == 2).wait_recv()
            for k in range(4):
                slot = k * 4 + links.y if half else links.z * 4 + k
                total = self.part(slot, half)[...].astype(F32)
                for step in steps:
                    total = total + self.got[half][step - 1, k].astype(F32)
                self.got[half][0, k] = total.astype(BF16)

            for step in FAR_FIRST:
                self.last_copy(half, step).start()

    def total(self, half):
        here = self.links.z if half else self.links.y
        received([self.last_copy(half, step) for step in FAR_FIRST])
        total = self.got[half][0, here].astype(F32)
        for step in range(3):
            total = total + self.last[half][step].astype(F32)
        return total

    def sent(self):
        for far in (True, False):
            for q, step in ((0, 1), (1, 3)):
                self.z_copy(step, q, far).wait_send()
                if not far:
                    self.z_copy(4 - step, q, far).wait_send()
            for z in range(4):
                step = 1 if z < 2 else 3
                self.y_copy(step, z, far).wait_send()
                if not far:
                    self.y_copy(4 - step, z, far).wait_send()
        sent([self.last_copy(half, step) for half in range(2) for step in FAR_FIRST])


INS = (
    "tokens",
    "ids",
    "gain_one",
    "w_qkv",
    "w_out",
    "w_router",
    "gain_two",
    "w_sin",
    "w_sout",
    "e_in",
    "e_out",
    "out_grad",
)
FETCHED = ("tokens", "e_in", "e_out", "out_grad")
OUTS = {
    "block_out": ((SEQ, D), BF16),
    "tokens_grad": ((SEQ, D), F32),
    "g_gain_one": ((1, ROWS), F32),
    "g_qkv": ((ROWS, 2560), F32),
    "g_out": ((ROWS, D), F32),
    "g_gain_two": ((1, ROWS), F32),
    "g_router": ((EXPERTS, ROWS), F32),
    "g_sin": ((ROWS, 2 * SH), F32),
    "g_sout": ((ROWS, SH), F32),
    "g_ein": ((96, 1024), F32),
    "g_eout": ((96, 512), F32),
}
SCRATCH = {
    "small": ((128, 128), F32),
    "pack": ((4, 16, W_ALL), BF16),
    "arrived": ((4, 16, W_ALL), BF16),
    "dense": ((16, 2, 48, W_ATT), BF16),
    "shared": ((16, 2, 48, W_SHARED), BF16),
    "got": ((16, 96, D), BF16),
    "full": ((8, 2, 96, D), BF16),
    "nat": ((D, D), BF16),
    "normed": ((4, SEQ, D), BF16),
    "qkv": ((4, SEQ, 640), BF16),
    "mix": ((4, SEQ, 384), BF16),
    "send_y": ((4, 2, SEQ, D), BF16),
    "send_x": ((4, 2, SEQ, WIDE), BF16),
    "pair_y": ((4, SEQ, D), BF16),
    "pair_x": ((4, SEQ, WIDE), BF16),
    "got_y": ((3, SEQ, D), BF16),
    "got_x": ((3, SEQ, WIDE), BF16),
    "hidden": ((SEQ, D), F32),
    "probs": ((SEQ, 128), F32),
    "chosen": ((SEQ, 128), F32),
    "rows": ((4, 2, SEQ, WIDE), BF16),
    "cot": ((4, 2, SEQ, D), BF16),
    "gated": ((4, 2, SEQ, 640), BF16),
    "joint": ((4, 2, SEQ, 1280), BF16),
    "low": ((4, SEQ, D), BF16),
    "dsh": ((16, 2, 48, 384), BF16),
    "back": ((48, W_ALL), BF16),
    "e_got0": ((3, 4, 48, D), BF16),
    "e_got1": ((3, 4, 48, D), BF16),
    "e_last0": ((3, 48, D), BF16),
    "e_last1": ((3, 48, D), BF16),
    "d_got0": ((3, 4, 48, 640), BF16),
    "d_got1": ((3, 4, 48, 512), BF16),
    "d_last0": ((3, 48, 640), BF16),
    "d_last1": ((3, 48, 512), BF16),
    "s_got0": ((3, 4, 48, 384), BF16),
    "s_got1": ((3, 4, 48, 384), BF16),
    "s_last0": ((3, 48, 384), BF16),
    "s_last1": ((3, 48, 384), BF16),
}
SENDS, RECEIVES = 164, 254
PAIRS = (((0, 0), (0, 1)), ((1, 0), (3, 0)), ((2, 0), (2, 1)), ((1, 1), (3, 1)))


class Bag:
    pass


def causal_probs(q, k):
    scores = dot_nt(q, k) * HD**-0.5
    row = lax.broadcasted_iota(jnp.int32, (SEQ, SEQ), 0)
    col = lax.broadcasted_iota(jnp.int32, (SEQ, SEQ), 1)
    scores = jnp.where(col <= row, scores, -1e30)
    exponent = jnp.exp(scores - jnp.max(scores, axis=1, keepdims=True))
    return exponent * (1.0 / jnp.sum(exponent, axis=1, keepdims=True))


def kernel(*refs):
    b = Bag()
    names = [
        *(name + "_given" if name in FETCHED else name for name in INS),
        *(name + "_result" for name in OUTS),
        *OUTS,
        "tokens",
        *SCRATCH,
    ]
    for name, ref in zip(names, refs):
        setattr(b, name, ref)
    links = Links(*refs[len(names) :])
    x, y, z, c = links.x, links.y, links.z, links.c
    other = 1 - c
    results = []
    kept = links.take(links.kept)

    def deliver(*ready):
        for name in ready:
            results.append(links.local(getattr(b, name), getattr(b, name + "_result")))

    here = z * 4 + y
    mine = 2 * x + c
    every = pl.ds(0, 48)
    e_cut = ((pl.ds(0, 48),), (pl.ds(48, 48),))
    d_cut = ((every, pl.ds(0, 640)), (every, pl.ds(640, 512)))
    s_cut = ((every, pl.ds(0, 384)), (every, pl.ds(384, 384)))
    d_part = lambda slots, half: b.dense.at[(slots, c, *half)]
    s_part = lambda slots, half: b.shared.at[(slots, c, *half)]
    e_part = lambda slots, half: b.got.at[(slots, *half)]

    greeted = links.greet("xyzc")
    loads = [
        links.local(b.tokens_given, b.tokens),
        links.local(b.e_in_given, b.got.at[here, :, pl.ds(0, 1024)]),
        links.local(b.e_out_given, b.got.at[here, :, pl.ds(1024, 512)]),
        links.local(b.out_grad_given, b.cot.at[x, c]),
    ]
    b.pack[...] = jnp.zeros_like(b.pack)
    b.small[...] = jnp.zeros_like(b.small)
    b.small[0:EXPERTS, 0:ROWS] = b.w_router[...].astype(F32)
    b.small[8:9, 0:ROWS] = b.gain_two[...].astype(F32)
    b.small[9:10, 0:ROWS] = b.gain_one[...].astype(F32)
    small = b.small[...].T
    lane = lax.broadcasted_iota(jnp.int32, (SEQ, 128), 1)
    row = lax.broadcasted_iota(jnp.int32, (SEQ, 128), 0)
    named = jnp.zeros((SEQ, 128), F32)
    for k in range(TOP):
        named = named + (b.ids[k : k + 1, :] == row).astype(F32)
    b.chosen[...] = named.T
    gain_one = small[0:ROWS, 9:10]
    for k in range(4):
        for start, width, at in ((k * 384, 384, 0), (D + k * 128, 128, 384), (2048 + k * 128, 128, 512)):
            b.pack[k, 0:ROWS, at : at + width] = (
                b.w_qkv[:, start : start + width].astype(F32) * gain_one
            ).astype(BF16)
        b.pack[k, 0:ROWS, 640:1024] = b.w_out[:, k * 384 : k * 384 + 384]
        b.pack[k, 0:ROWS, 1024:1152] = small[0:ROWS].astype(BF16)
        for core in range(2):
            at, unit = W_ATT + 384 * core, (2 * k + core) * 128
            b.pack[k, 0:ROWS, at : at + 128] = b.w_sin[:, unit : unit + 128]
            b.pack[k, 0:ROWS, at + 128 : at + 256] = b.w_sin[:, SH + unit : SH + unit + 128]
            b.pack[k, 0:ROWS, at + 256 : at + 384] = b.w_sout[:, unit : unit + 128]
    finish(loads)
    links.locals = 0
    greeted()

    def exchange(cols):
        return [
            links.send(
                b.pack.at[lax.rem(x + step, 4), :, cols], b.arrived.at[x, :, cols], "x", step
            )
            for step in FAR_FIRST
        ]

    exchanged = exchange(pl.ds(0, W_ATT))
    e_cols = lambda cols: tuple((rows, cols) for (rows,) in e_cut)
    e_first = gather_first(links, b.got.at[here], e_part, here, e_cols(pl.ds(0, 1024)))
    inputs = b.tokens[...].astype(F32)
    inverse_one = lax.rsqrt(jnp.mean(inputs * inputs, axis=1, keepdims=True) + epsilon)
    b.normed[x] = (inputs * inverse_one).astype(BF16)
    cot_pair = links.send(b.cot.at[x, c], b.cot.at[x, c], "c", 1)
    b.arrived[x] = b.pack[x]
    finish(exchanged)
    exchanged = exchange(pl.ds(W_ATT, W_SHARED))
    normed_ring = RowRing(links, lambda s, rows: b.normed.at[s, rows])
    cot_ring = RowRing(links, lambda s, rows: b.cot.at[s, c, rows])
    normed_ring.start()
    pick = pick_matrix((48, 64), lambda row: row // ROWS * 16 + row % ROWS)
    for col in range(0, W_ATT, 384):
        block = moved(pick, b.arrived[:, :, col : col + 384].reshape(64, 384))
        b.dense[here, c, :, col : col + 384] = block

    d_first = gather_first(links, b.dense.at[here, c], d_part, here, d_cut)
    sent(d_first)
    e_first += gather_first(links, b.got.at[here], e_part, here, e_cols(pl.ds(1024, 512)))
    d_ring = PlaneRing(links, d_first, d_part, d_cut)
    normed_ring.pass_on()
    cot_ring.start()
    d_ring.pass_on()
    d_ring.leave()
    finish(exchanged)
    for col in range(W_ATT, W_ALL, 384):
        block = moved(pick, b.arrived[:, :, col : col + 384].reshape(64, 384))
        b.shared[here, c, :, col - W_ATT : col - W_ATT + 384] = block
    s_first = gather_first(links, b.shared.at[here, c], s_part, here, s_cut)
    d_ring.arrive_near()
    d_ring.arrive()
    d_pair = links.take(8)

    def d_forward(j):
        piece = b.dense.at[pl.ds(2 * j, 2), c]
        return links.copy(piece, piece, "c", 1, d_pair + j)

    for j in range(8):
        d_forward(j).start()
    e_ring = PlaneRing(links, e_first, e_part, e_cut)
    normed_ring.arrive()

    order = pick_matrix(
        (192, 192), lambda row: row % 48 // ROWS * 48 + row // 48 * ROWS + row % ROWS
    )

    def to_rows(j, source, start, at, width):
        piece = source[pl.ds(2 * j, 2), :, :, start].reshape(192, width)
        piece = moved(order, piece)
        for k in range(4):
            row = pl.multiple_of(k * 384 + j * 48, 16)
            b.nat[pl.ds(row, 48), at : at + width] = piece[k * 48 : k * 48 + 48]

    def to_blocks(j, target, at, width):
        pieces = [
            b.nat[pl.ds(pl.multiple_of(k * 384 + j * 48, 16), 48), at : at + width]
            for k in range(4)
        ]
        piece = moved(order, jnp.concatenate(pieces, axis=0))
        target[pl.ds(2 * j, 2)] = piece.reshape(2, 2, 48, width)

    @pl.loop(0, 8)
    def _(j):
        d_forward(j).wait()
        to_rows(j, b.dense, pl.ds(0, W_ATT), 0, W_ATT)

    s_ring = PlaneRing(links, s_first, s_part, s_cut)

    mix_ring = SumRing(links, lambda s, rows: b.send_y.at[s, 0, rows], b.got_y)

    def attend(sequences):
        for s in sequences:
            b.qkv[s] = dot(b.normed[s], b.nat[:, 0:640]).astype(BF16)
        for h in range(3):
            head = slice(h * HD, (h + 1) * HD)
            for s in sequences:
                probs = causal_probs(b.qkv[s, :, head], b.qkv[s, :, 384:512])
                b.mix[s, :, head] = dot(probs.astype(BF16), b.qkv[s, :, 512:640]).astype(BF16)
        for s in sequences:
            for n in range(2):
                rows = slice(n * 768, (n + 1) * 768)
                b.send_y[s, 0, :, rows] = dot_nt(b.mix[s], b.nat[rows, 640:1024]).astype(BF16)

    right, left, far = (lax.rem(x + step, 4) for step in (1, 3, 2))
    attend([far])
    mix_ring.start_far()
    attend([right, left])
    mix_ring.near(1, True).start()
    mix_ring.near(3, True).start()
    mix_ring.pass_on()
    attend([x])

    e_ring.pass_on()
    cot_ring.pass_on()
    e_hands = []
    lower, upper = pl.ds(0, 48), pl.ds(48, 48)
    for k in range(2):
        for half, to_other in ((other, True), (c, False)):
            at = 2 * half + k
            pieces = [
                (at == lax.rem(z + 2, 4), b.got.at[pl.ds(at * 4, 4), lower], pl.ds(4 * k, 4), lower)
            ]
            for to in range(4):
                pieces.append(
                    (to == lax.rem(y + 2, 4), b.got.at[at * 4 + to, upper], 4 * k + to, upper)
                )
            for is_far, source, slots, rows in pieces:
                target = b.full.at[slots, c, rows]
                if to_other:
                    copy = links.copy(source, target, "c", 1, links.take(1))
                else:
                    copy = links.local_copy(source, target)
                e_hands.append((is_far, copy))

    def e_hand(far_ones):
        for is_far, copy in e_hands:

            @pl.when(is_far == far_ones)
            def _():
                copy.start()

    e_ring.arrive_near()
    e_hand(False)

    hidden = mix_ring.total(b.tokens[...].astype(F32) + b.send_y[x, 0].astype(F32))
    b.hidden[...] = hidden
    inverse_two = lax.rsqrt(jnp.mean(hidden * hidden, axis=1, keepdims=True) + epsilon)
    lane8 = lax.broadcasted_iota(jnp.int32, (8, 128), 1)
    gain_two = dot_nt((lane8 == 8).astype(BF16), b.nat[:, 1024:1152])[0:1]
    moe_in = (hidden * inverse_two * gain_two).astype(BF16)
    b.rows[x, c, :, 0:D] = moe_in
    logits = jnp.where(lane < EXPERTS, dot(moe_in, b.nat[:, 1024:1152]), -1e30)
    exponent = jnp.exp(logits - jnp.max(logits, axis=1, keepdims=True))
    router_probs = exponent / jnp.sum(exponent, axis=1, keepdims=True)
    b.probs[...] = router_probs
    gates = b.chosen[...] * router_probs
    high = gates.astype(BF16).astype(F32)
    b.rows[x, c, :, D:WIDE] = (high + pltpu.roll(gates - high, 8, 1)).astype(BF16)
    rows_ring = RowRing(links, lambda s, rows: b.rows.at[s, c, rows], kept)
    rows_ring.start()
    pair_rows, pair_cot = kept + 4, kept + 8
    forward_rows = lambda s, d: links.copy(
        b.rows.at[s, c], b.rows.at[s, c], "c", 1, pair_rows + d
    )
    forward_cot = lambda s, d: links.copy(b.cot.at[s, c], b.cot.at[s, c], "c", 1, pair_cot + d)
    forward_rows(x, 0).start()
    s_ring.pass_on()
    e_ring.arrive()
    e_hand(True)
    sent(e_first + s_first)
    s_ring.arrive_near()
    s_ring.arrive()
    half = pl.ds(pl.multiple_of(other * 384, 128), 384)
    s_pair = links.send(b.shared.at[:, c, :, half], b.shared.at[:, c, :, half], "c", 1)

    for _, copy in e_hands:
        copy.wait()

    def shared_rows():
        s_pair.wait()

        @pl.loop(0, 8)
        def _(j):
            to_rows(j, b.shared, pl.ds(pl.multiple_of(c * 384, 128), 384), W_ATT, 384)

    links.left()
    back_pair = links.take(8)
    sum_pair = links.take(4)
    parts = (pl.ds(0, 768), pl.ds(768, WIDE - 768))
    back_forward = lambda s, d, n: links.copy(
        b.send_x.at[s, other, :, parts[n]], b.pair_x.at[s, :, parts[n]], "c", 1, back_pair + 2 * d + n
    )
    sum_forward = lambda s, d: links.copy(
        b.send_y.at[s, other], b.pair_y.at[s], "c", 1, sum_pair + d
    )
    back_ring = SumRing(links, lambda s, rows: b.send_x.at[s, c, rows], b.got_x)
    sum_ring = SumRing(links, lambda s, rows: b.send_y.at[s, c, rows], b.got_y)
    cot_pair.wait()

    normed_ring.sent()
    cot_ring.sent()
    cot_ring.arrive()
    for d in range(1, 4):
        forward_cot(lax.rem(x + d, 4), d).start()
    forward_rows(x, 0).wait_recv()

    def which(i, core):
        sides = ((i == 1) & (core == 0)) | ((i == 3) & (core == 1))
        return ((0, i == 0), (1, sides), (3, sides), (2, i == 2))

    def give_pair(i, n):
        for d, now in which(i, other):

            @pl.when(now)
            def _():
                back_forward(lax.rem(x + d, 4), d, n).start()

    def add_pair(i, n):
        for d, now in which(i, c):
            s = lax.rem(x + d, 4)

            @pl.when(now)
            def _():
                back_forward(s, d, n).wait_recv()
                b.send_x[s, c, :, parts[n]] = (
                    b.send_x[s, c, :, parts[n]].astype(F32) + b.pair_x[s, :, parts[n]].astype(F32)
                ).astype(BF16)
                if n and d == 2:
                    back_ring.start_far()
                elif n and d:
                    back_ring.near(d, True).start()

    def pair_of(i):
        def chosen(k, what):
            values = [PAIRS[step][k][what] for step in range(4)]
            result = values[3]
            for step in range(3):
                result = jnp.where(i == step, values[step], result)
            return result

        return [(lax.rem(x + chosen(k, 0), 4), chosen(k, 1)) for k in range(2)]

    def both(i, ref, cols):
        return jnp.concatenate([ref[s, core, :, cols] for s, core in pair_of(i)], axis=0)

    def keep(i, ref, cols, value):
        for k, (s, core) in enumerate(pair_of(i)):
            ref[s, core, :, cols] = value[k * SEQ : (k + 1) * SEQ]

    def row_grads(i):
        slopes = both(i, b.joint, slice(0, 1280))
        for n in range(2):
            rows = slice(n * 768, (n + 1) * 768)
            result = dot_nt(
                slopes[:, 0:1024], b.full[4 * n : 4 * n + 4, :, :, 0:1024].reshape(768, 1024)
            ) + dot_nt(slopes[:, 1024:1280], b.nat[rows, 1152:1408])
            keep(i, b.send_x, rows, result.astype(BF16))
            give_pair(i, n)
            if n == 0:

                @pl.when(i == 1)
                def _():
                    rows_ring.arrive()
                    forward_rows(lax.rem(x + 2, 4), 2).start()

    @pl.loop(0, 4)
    def _(i):
        for k, far_ones in ((1, (1, 3)), (2, (2,))):

            @pl.when(i == k)
            def _():
                for d in far_ones:
                    forward_cot(lax.rem(x + d, 4), d).wait_recv()
                    forward_rows(lax.rem(x + d, 4), d).wait_recv()

        @pl.when(i > 0)
        def _():
            add_pair(i - 1, 0)

        tokens = both(i, b.rows, slice(0, D))
        grads = both(i, b.cot, slice(0, D))
        lanes = lax.broadcasted_iota(jnp.int32, (256, 128), 1)
        gate = both(i, b.rows, slice(D, WIDE)).astype(F32)
        gate = jnp.where((lanes == mine) | (lanes == mine + 8), gate, 0.0)
        gate = jnp.sum(gate, axis=1, keepdims=True)
        gate_grad = jnp.zeros((256, 1), F32)
        for part in range(3):
            if part < 2:
                at, width = part * 256, 256
                g = dot(tokens, b.full[:, :, :, at : at + 256].reshape(D, 256))
                u = dot(tokens, b.full[:, :, :, at + 512 : at + 768].reshape(D, 256))
                a = dot(grads, b.full[:, :, :, at + 1024 : at + 1280].reshape(D, 256))
                first, second, scale = at, at + 512, gate
            else:

                @pl.when(i == 0)
                def _():
                    shared_rows()

                at, width = 512, 128
                gu = dot(tokens, b.nat[:, 1152:1408])
                g, u = gu[:, 0:128], gu[:, 128:256]
                a = dot(grads, b.nat[:, 1408:1536])
                first, second, scale = 1024, 1152, None
            g = g.astype(BF16).astype(F32)
            u = u.astype(BF16).astype(F32)
            sg = jax.nn.sigmoid(g)
            act = (g * sg * u).astype(BF16)
            if scale is not None:
                gate_grad = gate_grad + jnp.sum(act.astype(F32) * a, axis=1, keepdims=True)
                act = (act.astype(F32) * scale).astype(BF16)
                a = a * scale
            keep(i, b.gated, slice(at, at + width), act)
            keep(
                i,
                b.joint,
                slice(first, first + width),
                (a * u * (sg * (1.0 + g * (1.0 - sg)))).astype(BF16),
            )
            keep(i, b.joint, slice(second, second + width), (a * g * sg).astype(BF16))
        gate_high = gate_grad.astype(BF16).astype(F32)
        spread = jnp.where(lanes == mine, gate_high, 0.0)
        spread = spread + jnp.where(lanes == mine + 8, gate_grad - gate_high, 0.0)
        keep(i, b.send_x, slice(D, WIDE), spread.astype(BF16))

        @pl.when(i > 0)
        def _():
            add_pair(i - 1, 1)

        @pl.when(i == 0)
        def _():
            rows_ring.pass_on()
            for d in (1, 3):
                forward_rows(lax.rem(x + d, 4), d).start()

        row_grads(i)

    add_pair(3, 0)
    add_pair(3, 1)


    e_sum = PlaneSum(
        links,
        lambda slots, half: b.got.at[slots, pl.ds(48 * half, 48)],
        (b.e_got0, b.e_got1),
        (b.e_last0, b.e_last1),
    )
    e_moves = []

    def e_start(low):
        finish(e_moves[low])
        e_sum.start_far(low)

    for low in range(2):
        for n in (2 * low, 2 * low + 1):
            if n == 3:
                e_start(0)
            cols = slice(n * 384, (n + 1) * 384)
            tokens = b.rows[:, :, :, cols].reshape(1024, 384)
            for at in (0, 512):
                result = dot_tn(tokens, b.joint[:, :, :, at : at + 512].reshape(1024, 512))
                b.full[2 * n : 2 * n + 2, :, :, at : at + 512] = result.astype(BF16).reshape(
                    2, 2, 96, 512
                )
            grads = b.cot[:, :, :, cols].reshape(1024, 384)
            result = dot_tn(grads, b.gated[:, :, :, 0:512].reshape(1024, 512))
            result = result.astype(BF16).reshape(2, 2, 2, 48, 512)
            for h in range(2):
                b.dense[8 * h + 2 * n : 8 * h + 2 * n + 2, :, :, 0:512] = result[:, :, h]
        four = pl.ds(4 * low, 4)
        target = pl.ds(8 * c + 4 * low, 4)
        wide, slim = pl.ds(0, 1024), pl.ds(1024, 512)
        moves = [
            links.send(b.full.at[four, other, :, wide], b.got.at[target, :, wide], "c", 1),
            links.local(b.full.at[four, c, :, wide], b.got.at[target, :, wide]),
        ]
        for h in range(2):
            rows, slots = pl.ds(48 * h, 48), pl.ds(8 * h + 4 * low, 4)
            moves += [
                links.send(
                    b.dense.at[slots, other, :, pl.ds(0, 512)], b.got.at[target, rows, slim], "c", 1
                ),
                links.local(b.dense.at[slots, c, :, pl.ds(0, 512)], b.got.at[target, rows, slim]),
            ]
        e_moves.append(moves)
        if not low:
            back_ring.pass_on()

    e_start(1)

    moe_back = back_ring.total(b.send_x[x, c].astype(F32))
    raw = moe_back[:, D:WIDE]
    router_probs = b.probs[...]
    prob_grad = b.chosen[...] * (raw + pltpu.roll(raw, 120, 1))
    logit_grad = router_probs * (
        prob_grad - jnp.sum(router_probs * prob_grad, axis=1, keepdims=True)
    )
    logit_grad = logit_grad.astype(BF16)
    gain_two = dot_nt((lane8 == 8).astype(BF16), b.nat[:, 1024:1152])[0:1]
    moe_in_grad = moe_back[:, 0:D] + dot_nt(logit_grad, b.nat[:, 1024:1152])
    hidden = b.hidden[...]
    inverse_two = lax.rsqrt(jnp.mean(hidden * hidden, axis=1, keepdims=True) + epsilon)
    scaled = gain_two * moe_in_grad
    hidden_grad = (
        b.cot[x, c].astype(F32)
        + inverse_two * scaled
        - hidden
        * (inverse_two * inverse_two * inverse_two)
        * jnp.mean(scaled * hidden, axis=1, keepdims=True)
    )
    b.tokens_grad[...] = hidden_grad
    b.low[x] = hidden_grad.astype(BF16)
    low_ring = RowRing(links, lambda s, rows: b.low.at[s, rows])
    low_ring.start()
    e_sum.start_near()
    misc_grad = dot_tn(b.rows[x, c, :, 0:D], logit_grad) + dot_tn(
        (moe_in_grad * hidden * inverse_two).astype(BF16), (lane == 8).astype(BF16)
    )
    b.nat[:, 1024:1152] = misc_grad.astype(BF16)

    @pl.loop(0, 4)
    def _(d):
        s = lax.rem(x + d, 4)
        for n in range(2):
            rows = slice(n * 768, (n + 1) * 768)
            result = dot_nt(
                b.gated[s, :, :, 0:512].reshape(256, 512), b.full[4 * n : 4 * n + 4, :, :, 1024:1536].reshape(768, 512)
            ) + dot_nt(b.gated[s, :, :, 512:640].reshape(256, 128), b.nat[rows, 1408:1536])
            b.send_y[s, :, :, rows] = result.astype(BF16).reshape(2, SEQ, 768)
        sum_forward(s, d).start()

    for n in range(4):
        cols = slice(n * 384, (n + 1) * 384)
        tokens = b.rows[:, :, :, cols].reshape(1024, 384)
        result = dot_tn(tokens, b.joint[:, :, :, 1024:1280].reshape(1024, 256))
        b.nat[cols, 1152:1408] = result.astype(BF16)
        grads = b.cot[:, :, :, cols].reshape(1024, 384)
        result = dot_tn(grads, b.gated[:, :, :, 512:640].reshape(1024, 128))
        b.nat[cols, 1408:1536] = result.astype(BF16)

    @pl.loop(0, 8)
    def _(j):
        to_blocks(j, b.dsh, W_ATT, 384)

    half = pl.ds(pl.multiple_of(c * 384, 128), 384)
    for d in range(1, 4):
        forward_cot(lax.rem(x + d, 4), d).wait_send()
    s_give = links.send(b.dsh.at[:, other], b.shared.at[:, 0, :, half], "c", 1)
    s_keep = links.local(b.dsh.at[:, c], b.shared.at[:, 0, :, half])
    s_sum = PlaneSum(
        links,
        lambda slots, half: b.shared.at[slots, 0, :, pl.ds(384 * half, 384)],
        (b.s_got0, b.s_got1),
        (b.s_last0, b.s_last1),
    )

    e_sum.pass_on()
    norm_ring = SumRing(
        links,
        lambda s, rows: b.send_x.at[s, 0, rows, pl.ds(0, D)],
        b.got_x.at[:, :, pl.ds(0, D)],
    )
    for d in range(4):
        for n in range(2):
            back_forward(lax.rem(x + d, 4), d, n).wait_send()

    def attend_back(sequences):
        mix_grads, parts_of = [], []
        for s in sequences:
            mix_grads.append(dot(b.low[s], b.nat[:, 640:1024]).astype(BF16))
            parts_of.append((jnp.zeros((SEQ, HD), F32), jnp.zeros((SEQ, HD), F32)))
        for h in range(3):
            head = slice(h * HD, (h + 1) * HD)
            for k, s in enumerate(sequences):
                key_grad, value_grad = parts_of[k]
                key, value = b.qkv[s, :, 384:512], b.qkv[s, :, 512:640]
                query = b.qkv[s, :, head]
                mixed = mix_grads[k][:, head]
                probs = causal_probs(query, key)
                dprob = dot_nt(mixed, value)
                value_grad = value_grad + dot_tn(probs.astype(BF16), mixed)
                delta = jnp.sum(probs * dprob, axis=1, keepdims=True)
                score_grad = (probs * (dprob - delta)).astype(BF16)
                b.qkv[s, :, head] = (dot(score_grad, key) * HD**-0.5).astype(BF16)
                parts_of[k] = (key_grad + dot_tn(score_grad, query), value_grad)
        for k, s in enumerate(sequences):
            key_grad, value_grad = parts_of[k]
            b.qkv[s, :, 384:512] = (key_grad * HD**-0.5).astype(BF16)
            b.qkv[s, :, 512:640] = value_grad.astype(BF16)

    def normed_back(sequences):
        for s in sequences:
            for n in range(2):
                rows = slice(n * 768, (n + 1) * 768)
                b.send_x[s, 0, :, rows] = dot_nt(b.qkv[s], b.nat[rows, 0:640]).astype(BF16)

    attend_back([x])
    low_ring.pass_on()
    normed_back([x])
    attend_back([right, left])
    normed_back([right, left])
    norm_ring.near(1, True).start()
    norm_ring.near(3, True).start()
    s_give.wait()
    s_keep.wait()
    s_sum.start()
    low_ring.arrive()
    attend_back([far])
    normed_back([far])
    norm_ring.start_far()

    for d in (2, 1, 3, 0):
        s = lax.rem(x + d, 4)
        sum_forward(s, d).wait()
        b.send_y[s, c] = (b.send_y[s, c].astype(F32) + b.pair_y[s].astype(F32)).astype(BF16)
        if d == 2:
            sum_ring.start_far()
        elif d:
            sum_ring.near(d, True).start()
    e_sum.second()
    d_base = links.take(8)

    def d_landing(j):
        rows = pl.ds(pl.multiple_of(lax.div(j, 4) * 48, 16), 48)
        return b.cot.at[lax.rem(j, 4), :, rows, pl.ds(0, W_ATT)]

    d_give = lambda j: links.copy(
        b.dense.at[pl.ds(2 * j, 2), other], d_landing(j), "c", 1, d_base + j
    )

    for n in range(4):
        cols = slice(n * 384, (n + 1) * 384)
        result = dot_tn(b.normed[:, :, cols].reshape(512, 384), b.qkv[...].reshape(512, 640))
        b.nat[cols, 0:640] = result.astype(BF16)
        result = dot_tn(b.low[:, :, cols].reshape(512, 384), b.mix[...].reshape(512, 384))
        b.nat[cols, 640:1024] = result.astype(BF16)

    @pl.loop(0, 8)
    def _(j):
        to_blocks(j, b.dense, 0, W_ATT)
        d_give(j).start()

    s_sum.pass_on()

    @pl.loop(0, 8)
    def _(j):
        d_give(j).wait()
        total = b.dense[pl.ds(2 * j, 2), c].astype(F32) + d_landing(j)[...].astype(F32)
        b.dense[pl.ds(2 * j, 2), c] = total.astype(BF16)

    d_sum = PlaneSum(
        links,
        lambda slots, half: d_part(slots, d_cut[half]),
        (b.d_got0, b.d_got1),
        (b.d_last0, b.d_last1),
    )
    d_sum.start_direct()

    s_sum.second()
    norm_ring.pass_on()

    scaled = norm_ring.total(b.send_x[x, 0, :, 0:D].astype(F32))
    inputs = b.tokens[...].astype(F32)
    inverse_one = lax.rsqrt(jnp.mean(inputs * inputs, axis=1, keepdims=True) + epsilon)
    b.tokens_grad[...] = (
        b.tokens_grad[...]
        + inverse_one * scaled
        - inputs
        * (inverse_one * inverse_one * inverse_one)
        * jnp.mean(scaled * inputs, axis=1, keepdims=True)
    )
    deliver("tokens_grad")


    d_sum.second(direct=True)
    sum_ring.pass_on()
    for part in range(2):
        at = W_ATT + 384 * part
        b.back[:, at : at + 384] = s_sum.total(part).astype(BF16)
    for part, cols in ((0, slice(0, 640)), (1, slice(640, 1152))):
        b.back[:, cols] = d_sum.total(part).astype(BF16)
    pick = pick_matrix((64, 48), lambda row: jnp.where(row % 16 < ROWS, row // 16 * ROWS + row % 16, -1))
    for col in range(0, W_ALL, 384):
        b.pack[:, :, col : col + 384] = moved(pick, b.back[:, col : col + 384]).reshape(4, 16, 384)
    exchanged = exchange(pl.ds(0, W_ALL))
    b.arrived[x] = b.pack[x]
    for part in range(2):
        rows = slice(48 * part, 48 * part + 48)
        total = e_sum.total(part)
        b.g_ein[rows] = total[:, 0:1024]
        b.g_eout[rows] = total[:, 1024:1536]
    deliver("g_ein", "g_eout")
    result = sum_ring.total(b.hidden[...] + b.send_y[x, c].astype(F32))
    b.block_out[...] = result.astype(BF16)
    deliver("block_out")

    for ring in (rows_ring, low_ring):
        ring.sent()
    for d in range(4):
        forward_rows(lax.rem(x + d, 4), d).wait_send()
    for plane_sum in (e_sum, s_sum, d_sum):
        plane_sum.sent()
    received(exchanged)
    gain_grad = jnp.zeros((ROWS, 1), F32)
    misc = jnp.zeros((ROWS, 128), F32)
    for k in range(4):
        piece = b.arrived[k].astype(F32)[0:ROWS]
        for start, width, at in ((k * 384, 384, 0), (D + k * 128, 128, 384), (2048 + k * 128, 128, 512)):
            raw = piece[:, at : at + width]
            gain_grad = gain_grad + jnp.sum(
                raw * b.w_qkv[:, start : start + width].astype(F32), axis=1, keepdims=True
            )
            b.g_qkv[:, start : start + width] = raw * gain_one
        b.g_out[:, k * 384 : k * 384 + 384] = piece[:, 640:1024]
        misc = misc + piece[:, 1024:1152]
        for core in range(2):
            at, unit = W_ATT + 384 * core, (2 * k + core) * 128
            b.g_sin[:, unit : unit + 128] = piece[:, at : at + 128]
            b.g_sin[:, SH + unit : SH + unit + 128] = piece[:, at + 128 : at + 256]
            b.g_sout[:, unit : unit + 128] = piece[:, at + 256 : at + 384]
    b.small[0:ROWS] = jnp.where(lane[0:ROWS] == 9, gain_grad, misc)
    small = b.small[...].T
    b.g_router[...] = small[0:EXPERTS, 0:ROWS]
    b.g_gain_two[...] = small[8:9, 0:ROWS]
    b.g_gain_one[...] = small[9:10, 0:ROWS]
    sent(exchanged)
    deliver("g_gain_one", "g_qkv", "g_out", "g_gain_two", "g_router", "g_sin", "g_sout")
    finish(results)


def hand_over(*refs):
    n = len(OUTS)
    sources, targets, held, sems = refs[:n], refs[n : 2 * n], refs[2 * n : 3 * n], refs[3 * n]
    reads = [pltpu.make_async_copy(sources[i], held[i], sems.at[0, i]) for i in range(n)]
    writes = [pltpu.make_async_copy(held[i], targets[i], sems.at[1, i]) for i in range(n)]
    for read in reads:
        read.start()
    for read, write in zip(reads, writes):
        read.wait()
        write.start()
    finish(writes)


def local(
    tokens,
    expert_ids,
    attn_gain,
    w_qkv,
    w_out,
    moe_gain,
    w_router,
    w_shared_in,
    w_shared_out,
    w_expert_in,
    w_expert_out,
    out_grad,
):
    results = pl.pallas_call(
        kernel,
        out_shape=[jax.ShapeDtypeStruct(shape, dtype) for shape, dtype in OUTS.values()],
        in_specs=[
            pl.BlockSpec(memory_space=pl.ANY if name in FETCHED else pltpu.VMEM) for name in INS
        ],
        out_specs=[pl.BlockSpec(memory_space=pl.ANY)] * len(OUTS),
        scratch_shapes=[
            *[
                pltpu.VMEM(shape, dtype)
                for shape, dtype in (*OUTS.values(), ((SEQ, D), BF16), *SCRATCH.values())
            ],
            pltpu.SemaphoreType.DMA((SENDS,)),
            pltpu.SemaphoreType.DMA((RECEIVES,)),
        ],
        compiler_params=pltpu.CompilerParams(
            collective_id=1, has_side_effects=True, vmem_limit_bytes=(64 << 20) - (1 << 16)
        ),
        cost_estimate=pl.CostEstimate(
            flops=23_000_000_000, bytes_accessed=10_000_000, transcendentals=2_000_000
        ),
        name="block",
    )(
        tokens,
        expert_ids.T,
        attn_gain[None],
        w_qkv,
        w_out,
        w_router.T,
        moe_gain[None],
        w_shared_in,
        w_shared_out,
        w_expert_in,
        w_expert_out,
        out_grad,
    )
    results = pl.pallas_call(
        hand_over,
        out_shape=[jax.ShapeDtypeStruct(shape, dtype) for shape, dtype in OUTS.values()],
        in_specs=[pl.BlockSpec(memory_space=pl.ANY)] * len(OUTS),
        out_specs=[pl.BlockSpec(memory_space=pl.ANY)] * len(OUTS),
        scratch_shapes=[
            *[pltpu.VMEM(shape, dtype) for shape, dtype in OUTS.values()],
            pltpu.SemaphoreType.DMA((2, len(OUTS))),
        ],
        name="hand_over",
    )(*results)
    block_out, tokens_grad, gain_one, qkv, out, gain_two, router, sin, sout, ein, eout = results
    return (
        block_out,
        tokens_grad,
        gain_one[0],
        qkv,
        out,
        gain_two[0],
        router.T,
        sin,
        sout,
        ein,
        eout,
    )


def solution(mesh):
    wide, flat = P("fsdp", None), P("fsdp")
    return jax.shard_map(
        local,
        mesh=mesh,
        in_specs=(wide, wide, flat, wide, wide, flat, wide, wide, wide, wide, wide, wide),
        out_specs=(wide, wide, flat, wide, wide, flat, wide, wide, wide, wide, wide),
        check_vma=False,
    )
```
